32 devices in a mesh: seq: 8 (over z, x), dp: 4 (over y, core).
Axes of the slice: x: 2, y: 2, z: 4, core: 2. Of those that a mesh axis runs over, the one named last changes fastest.
Arguments:
- tokens: bfloat16 [4, 1024, 4096], P('dp', 'seq'), may hold values from -6 to 6
- frozen_projections: bfloat16 [3, 4, 1024, 2048], P(None, 'dp', 'seq'), may hold values from -8 to 8
- output_gradient: bfloat16 [4, 1024, 2048], P('dp', 'seq'), may hold values from -2 to 2
- down_weight: bfloat16 [3, 8, 4096], replicated, may hold values from -0.09375 to 0.09375
- up_weight: bfloat16 [3, 8, 2048], replicated, may hold values from -1 to 1
Outputs:
- down_gradient: float32 [3, 8, 4096], replicated
- up_gradient: float32 [3, 8, 2048], replicated
The draws below stay inside these ranges and needn't reach their ends.
All inputs are finite; a program needn't handle non-finite values.
Results may differ from the reference program's by a relative error of at most 0.004.
The reference program's roundings to bfloat16 on the way count: a program that leaves them out, or rounds other values in their place, can miss the bound.
Values may be sent and summed in bfloat16 or wider, within the bound.
No kernel may reach another device: no remote copies, remote signals or barrier semaphores. Data moves between devices by JAX's collectives and lax.ppermute only.
A program may use at most 64 MiB of HBM per device.

```python
import jax
import jax.numpy as jnp
from jax import lax

MODEL_WIDTH = 4096
HEADS = 16
HEAD_DIM = 128
ADAPTER_RANK = 8
GROUP = 128
HALF = 64
HEAD_FEATURES = 2048
TOKENS = 1024
SEQS = 4


def draw_frozen_projections(key, part):
    key = jax.random.fold_in(key, 11)
    key_base = jax.random.fold_in(key, 0)
    base_rows = jnp.clip(jax.random.normal(key_base, (3, SEQS, TOKENS, HEAD_FEATURES), jnp.float32), -8.0, 8.0)
    return base_rows.astype(jnp.bfloat16)


def block_scale(rng, extent, pieces, least, top_value):
    factor_of, own = 1.0, jax.random.fold_in(rng, 6)
    for dim, blocks in pieces:
        steps = jnp.exp(jax.random.uniform(jax.random.fold_in(own, dim), (blocks,), jnp.float32, least / len(pieces), top_value / len(pieces)))
        factor_of = factor_of * jnp.repeat(steps, extent[dim] // blocks).reshape([-1 if axis == dim else 1 for axis in range(len(extent))])
    return factor_of


def centred(key, extent, deviation, most, shards=(), dtype=jnp.bfloat16):
    array = deviation * jax.random.normal(key, extent, jnp.float32)
    if shards:
        array = array * block_scale(key, extent, shards, -0.22, 0.18)
    return jnp.clip(array, -most, most).astype(dtype)


def setup_inputs(seed: int = 0) -> dict:
    key_of = jax.random.split(jax.random.key(seed), 6)
    tokens = centred(key_of[0], (SEQS, TOKENS, MODEL_WIDTH), 1.0, 6.0, ((0, 4), (1, 8)))
    frozen_projections = draw_frozen_projections(jax.random.fold_in(key_of[5], 71), 0)
    output_gradient = centred(key_of[2], (SEQS, TOKENS, HEAD_FEATURES), ((SEQS * TOKENS) ** -0.5 * 8), 2.0, ((0, 4), (1, 8)))
    down_weight = centred(key_of[3], (3, ADAPTER_RANK, MODEL_WIDTH), MODEL_WIDTH ** -0.5, 0.09375)
    up_weight = centred(key_of[4], (3, ADAPTER_RANK, HEAD_FEATURES), 32 ** -0.5, 1.0)
    return {"tokens": tokens, "frozen_projections": frozen_projections, "output_gradient": output_gradient, "down_weight": down_weight, "up_weight": up_weight}


adapter_scale = 2.0


def attend(query_rows, key_rows, value_rows, out_grad):
    score_scale = HEAD_DIM ** -0.5
    highest_precision = lax.Precision.HIGHEST
    query_f = query_rows.astype(jnp.float32)
    key_f = key_rows.astype(jnp.float32)
    value_f = value_rows.astype(jnp.float32)
    grad_f = out_grad.astype(jnp.float32)
    count = query_rows.shape[0]
    scores = jnp.einsum("qhd,khd->hqk", query_f, key_f, precision=highest_precision) * score_scale
    causal = jnp.arange(count)[:, None] >= jnp.arange(count)[None, :]
    scores = jnp.where(causal[None], scores, -jnp.inf)
    row_max = jnp.max(scores, axis=-1, keepdims=True)
    weights_exp = jnp.exp(scores - row_max)
    attn_prob = weights_exp / jnp.sum(weights_exp, axis=-1, keepdims=True)
    prob_b = attn_prob.astype(jnp.bfloat16).astype(jnp.float32)
    output = jnp.einsum("hqk,khd->qhd", prob_b, value_f, precision=highest_precision)
    row_dot = jnp.sum(grad_f * output, axis=-1)
    dprob = jnp.einsum("qhd,khd->hqk", grad_f, value_f, precision=highest_precision)
    dscore = (attn_prob * (dprob - jnp.transpose(row_dot)[:, :, None]) * score_scale).astype(jnp.bfloat16).astype(jnp.float32)
    grad_query = jnp.einsum("hqk,khd->qhd", dscore, key_f, precision=highest_precision)
    grad_key = jnp.einsum("hqk,qhd->khd", dscore, query_f, precision=highest_precision)
    grad_value = jnp.einsum("hqk,qhd->khd", prob_b, grad_f, precision=highest_precision)
    return jnp.stack([grad_query, grad_key, grad_value])


def reference(tokens, frozen_projections, output_gradient, down_weight, up_weight):
    highest_precision = lax.Precision.HIGHEST
    token_floats = tokens.astype(jnp.float32)
    rank_product = jnp.einsum("pfz,nxz->npfx", token_floats, down_weight.astype(jnp.float32), precision=highest_precision).astype(jnp.bfloat16)
    projected_rows = (frozen_projections.astype(jnp.float32) + adapter_scale * jnp.einsum("beyn,bnx->beyx", rank_product.astype(jnp.float32), up_weight.astype(jnp.float32), precision=highest_precision)).astype(jnp.bfloat16)
    stacked = jnp.concatenate([projected_rows, output_gradient[None]], axis=0)
    half_width = HEAD_FEATURES // 2
    moved_rows = jnp.roll(stacked[..., half_width:], -HALF, axis=2)
    arranged = jnp.concatenate([stacked[..., :half_width], moved_rows], axis=-1)
    num_groups = TOKENS // GROUP
    arranged = arranged.reshape(4, SEQS * num_groups, GROUP, HEADS, HEAD_DIM)
    arranged = jnp.moveaxis(arranged, 1, 0)

    def one_group(block):
        return attend(block[0], block[1], block[2], block[3])

    grads = lax.map(one_group, arranged)
    grads = jnp.moveaxis(grads, 0, 1).reshape(3, SEQS, TOKENS, HEAD_FEATURES)
    projection_grad = jnp.concatenate([grads[..., :half_width], jnp.roll(grads[..., half_width:], HALF, axis=2)], axis=-1)
    rank_gradient = jnp.einsum("fonu,fau->fona", projection_grad, up_weight.astype(jnp.float32), precision=highest_precision)
    up_gradient = adapter_scale * jnp.einsum("yuve,yuvc->yec", rank_product.astype(jnp.float32), projection_grad, precision=highest_precision)
    down_gradient = adapter_scale * jnp.einsum("xvup,vub->xpb", rank_gradient, token_floats, precision=highest_precision)
    return down_gradient, up_gradient
```

```python
import jax
import jax.numpy as jnp
from jax import lax
from jax.experimental import pallas as pl
from jax.experimental.pallas import tpu as pltpu
from jax.sharding import PartitionSpec as P

HEAD_DIM = 128
RANK = 8
SCALE = HEAD_DIM ** -0.5
ADAPTER_SCALE = 2.0
BF = jnp.bfloat16
F32 = jnp.float32
AXES = ("seq", "dp")
VMEM = pl.BlockSpec(memory_space=pltpu.VMEM)
LIMIT = 48 * 1024 * 1024


def nt(a, b):
    return lax.dot_general(a, b, (((1,), (1,)), ((), ())), preferred_element_type=F32)


def nn(a, b):
    return lax.dot_general(a, b, (((1,), (0,)), ((), ())), preferred_element_type=F32)


def tn(a, b):
    return lax.dot_general(a, b, (((0,), (0,)), ((), ())), preferred_element_type=F32)


def hi_lo(x):
    high = x.astype(BF).astype(F32)
    return [high, x - high]


def rows(parts):
    return jnp.concatenate(parts, axis=0).astype(BF)


def project(frozen, low_t, up):
    return (frozen.astype(F32) + ADAPTER_SCALE * tn(low_t, up)).astype(BF)


def head(q, k, v, g, ups, low_q, low_k, low_v, mask):
    st = jnp.where(mask, nt(k, q) * SCALE, -jnp.inf)
    e = jnp.exp(st - jnp.max(st, axis=0, keepdims=True))
    p = e * (1.0 / jnp.sum(e, axis=0, keepdims=True))
    pb = p.astype(BF)
    dp = nt(v, g)
    row_dot = jnp.sum(pb.astype(F32) * dp, axis=0, keepdims=True)
    ds = (p * (dp - row_dot) * SCALE).astype(BF)
    bq, bk, bv = nt(ups[0], k), nt(ups[1], q), nt(ups[2], g)
    by_q = nn(rows([low_k] + hi_lo(bq)), ds)
    by_k = nt(rows([low_q] + hi_lo(bk)), ds)
    av = nn(low_v.astype(BF), pb)
    rv = nt(rows(hi_lo(bv)), pb)
    uq = nn(rows(hi_lo(by_k[:8])), k)
    uk = nn(rows(hi_lo(by_q[:8])), q)
    uv = nn(rows(hi_lo(av)), g)
    grads = [u[:8] + u[8:] for u in (uq, uk, uv)]
    ranks = [by_q[8:16] + by_q[16:24], by_k[8:16] + by_k[16:24], rv[:8] + rv[8:]]
    return grads, ranks


def causal(keys, queries, offset):
    return lax.broadcasted_iota(jnp.int32, (keys, queries), 0) <= offset + lax.broadcasted_iota(
        jnp.int32, (keys, queries), 1
    )


def local_kernel(frozen, grad, low_t, up, far_out, up_out, rank_out):
    count, width = grad.shape[1:]
    half, half_width = count // 2, width // 2
    low = [low_t[j] for j in range(3)]
    low_f = [x.astype(F32) for x in low]
    near_f = [x[:, half:] for x in low_f]
    ranks = [jnp.zeros((RANK, count), F32)] * 3
    full_mask = causal(count, count, 0)
    half_mask = causal(half, half, 0)
    for h in range(half_width // HEAD_DIM):
        cols = slice(h * HEAD_DIM, (h + 1) * HEAD_DIM)
        ups = [up[j, :, cols] for j in range(3)]
        q, k, v = [project(frozen[j, 0, :, cols], low[j], ups[j]) for j in range(3)]
        grads, parts = head(q, k, v, grad[0, :, cols], ups, *low_f, full_mask)
        for j in range(3):
            up_out[8 * j : 8 * j + 8, cols] = grads[j]
        ranks = [a + b for a, b in zip(ranks, parts)]
    near_ranks = [jnp.zeros((RANK, half), F32)] * 3
    for h in range(half_width // HEAD_DIM):
        cols = slice(half_width + h * HEAD_DIM, half_width + (h + 1) * HEAD_DIM)
        ups = [up[j, :, cols] for j in range(3)]
        whole = [project(frozen[j, 0, :, cols], low[j], ups[j]) for j in range(3)]
        for j in range(3):
            far_out[j, :, h * HEAD_DIM : (h + 1) * HEAD_DIM] = whole[j][:half]
        q, k, v = [x[half:] for x in whole]
        grads, parts = head(q, k, v, grad[0, half:, cols], ups, *near_f, half_mask)
        for j in range(3):
            up_out[8 * j : 8 * j + 8, cols] = grads[j]
        near_ranks = [a + b for a, b in zip(near_ranks, parts)]
    for j in range(3):
        rank_out[8 * j : 8 * j + 8, :] = ranks[j] + jnp.concatenate(
            [jnp.zeros((RANK, half), F32), near_ranks[j]], axis=1
        )


def far_kernel(own, frozen_kv, low_kv, grad, low_t, up, up_in, rank_in, up_out, rank_out, cross_out):
    half = own.shape[1]
    width = up.shape[2]
    half_width = width // 2
    far_f = [low_t[j].astype(F32)[:, :half] for j in range(3)]
    near = [low_kv[0], low_kv[1]]
    low_k = jnp.concatenate([near[0].astype(F32), far_f[1]], axis=1)
    low_v = jnp.concatenate([near[1].astype(F32), far_f[2]], axis=1)
    mask = causal(2 * half, half, half)
    rank_q = jnp.zeros((RANK, half), F32)
    rank_k = jnp.zeros((RANK, 2 * half), F32)
    rank_v = jnp.zeros((RANK, 2 * half), F32)
    up_out[:, :half_width] = up_in[:, :half_width]
    for h in range(half_width // HEAD_DIM):
        here = slice(h * HEAD_DIM, (h + 1) * HEAD_DIM)
        cols = slice(half_width + h * HEAD_DIM, half_width + (h + 1) * HEAD_DIM)
        ups = [up[j, :, cols] for j in range(3)]
        near_k, near_v = [project(frozen_kv[j, :, here], near[j], ups[j + 1]) for j in range(2)]
        k = jnp.concatenate([near_k, own[1, :, here]], axis=0)
        v = jnp.concatenate([near_v, own[2, :, here]], axis=0)
        grads, parts = head(
            own[0, :, here], k, v, grad[0, :half, cols], ups, far_f[0], low_k, low_v, mask
        )
        for j in range(3):
            up_out[8 * j : 8 * j + 8, cols] = up_in[8 * j : 8 * j + 8, cols] + grads[j]
        rank_q, rank_k, rank_v = rank_q + parts[0], rank_k + parts[1], rank_v + parts[2]
    none = jnp.zeros((RANK, half), F32)
    for j, part in enumerate([rank_q, rank_k[:, half:], rank_v[:, half:]]):
        rank_out[8 * j : 8 * j + 8, :] = rank_in[8 * j : 8 * j + 8, :] + jnp.concatenate(
            [part, none], axis=1
        )
    for j, part in enumerate([rank_k[:, :half], rank_v[:, :half]]):
        cross_out[8 * j : 8 * j + 8, :] = jnp.concatenate([none, part], axis=1)


def position():
    dp = lax.axis_index("dp")
    return dp & 1, (dp & 2) | (lax.axis_index("seq") & 1)


def down_kernel(tokens, rank_in, cross, up_in, keep, send):
    core, place = position()
    ranks = rank_in[...] + jnp.concatenate([jnp.zeros((RANK, rank_in.shape[1]), F32), cross[...]], axis=0)
    both = rows(hi_lo(ranks))
    n = ranks.shape[0]
    up_step, down_step = up_in.shape[1] // 8, tokens.shape[2] // 8
    for c in range(8):
        d = nn(both, tokens[0, :, c * down_step : (c + 1) * down_step])
        d = ADAPTER_SCALE * (d[:n] + d[n:])
        u = ADAPTER_SCALE * up_in[:, c * up_step : (c + 1) * up_step]
        slot = place ^ (c >> 1)

        def put(ref):
            ref[slot, :, :up_step] = u
            ref[slot, :, up_step:] = d

        pl.when(core == (c & 1))(lambda: put(keep))
        pl.when(core != (c & 1))(lambda: put(send))


def spread_kernel(mine, other, down_out, up_out):
    core, place = position()
    up_step, down_step = up_out.shape[2] // 8, down_out.shape[2] // 8
    for c in range(8):
        slot = place ^ (c >> 1)

        def put(ref):
            x = ref[slot].astype(F32)
            for j in range(3):
                up_out[j, :, c * up_step : (c + 1) * up_step] = x[8 * j : 8 * j + 8, :up_step]
                down_out[j, :, c * down_step : (c + 1) * down_step] = x[8 * j : 8 * j + 8, up_step:]

        pl.when(core == (c & 1))(lambda: put(mine))
        pl.when(core != (c & 1))(lambda: put(other))


def call(kernel, outs, *args):
    return pl.pallas_call(
        kernel,
        out_shape=outs,
        in_specs=[VMEM] * len(args),
        out_specs=jax.tree.map(lambda _: VMEM, outs),
        compiler_params=pltpu.CompilerParams(vmem_limit_bytes=LIMIT),
        cost_estimate=pl.CostEstimate(flops=10**9, bytes_accessed=10**6, transcendentals=0),
    )(*args)


def swap(x, bits, total):
    return lax.ppermute(x, AXES, [(i, i ^ bits) for i in range(total)])


def total_sum(keep, send, seqs, dps):
    total = seqs * dps
    keep = keep + swap(send, 1, total)
    own = keep[0]
    got = [swap(keep[s].astype(BF), (s & 2) | (dps if s & 1 else 0), total) for s in (1, 2, 3)]
    own = own + got[0].astype(F32) + got[1].astype(F32) + got[2].astype(F32)
    bit = 2
    while bit < seqs:
        piece = own.astype(BF)
        own = piece.astype(F32) + swap(piece, bit * dps, total).astype(F32)
        bit *= 2
    piece = own.astype(BF)
    mine = jnp.stack([piece] + [swap(piece, (s & 2) | (dps if s & 1 else 0), total) for s in (1, 2, 3)])
    return mine, swap(mine, 1, total)


def on_device(tokens, frozen, grad, down_weight, up_weight):
    seqs, dps = lax.axis_size("seq"), lax.axis_size("dp")
    count, width = grad.shape[1:]
    half, half_width = count // 2, width // 2
    forward = [(i, (i + 1) % seqs) for i in range(seqs)]
    backward = [(i, (i - 1) % seqs) for i in range(seqs)]
    frozen_kv = lax.ppermute(frozen[1:, 0, half:, half_width:], "seq", forward)
    low_t = jnp.einsum("psw,gw->psg", down_weight, tokens[0], preferred_element_type=F32).astype(BF)
    low_kv = lax.ppermute(low_t[1:, :, half:], "seq", forward)
    sds = jax.ShapeDtypeStruct
    own, up_part, rank_part = call(
        local_kernel,
        [sds((3, half, half_width), BF), sds((24, width), F32), sds((24, count), F32)],
        frozen, grad, low_t, up_weight,
    )
    up_part, rank_part, cross = call(
        far_kernel,
        [sds((24, width), F32), sds((24, count), F32), sds((16, count), F32)],
        own, frozen_kv, low_kv, grad, low_t, up_weight, up_part, rank_part,
    )
    cross = lax.ppermute(cross, "seq", backward)
    columns = (width + tokens.shape[2]) // 8
    piece = sds((4, 24, columns), F32)
    keep, send = call(down_kernel, [piece, piece], tokens, rank_part, cross, up_part)
    mine, other = total_sum(keep, send, seqs, dps)
    return tuple(
        call(spread_kernel, [sds((3, RANK, tokens.shape[2]), F32), sds((3, RANK, width), F32)], mine, other)
    )


def solution(mesh):
    return jax.shard_map(
        on_device,
        mesh=mesh,
        in_specs=(P("dp", "seq", None), P(None, "dp", "seq", None), P("dp", "seq", None), P(), P()),
        out_specs=(P(), P()),
        check_vma=False,
    )
```

```python
import jax
import jax.numpy as jnp
from jax import lax
from jax.experimental import pallas as pl
from jax.experimental.pallas import tpu as pltpu
from jax.sharding import PartitionSpec as P

HEAD_DIM = 128
RANK = 8
SCALE = HEAD_DIM ** -0.5
ADAPTER_SCALE = 2.0
BF = jnp.bfloat16
F32 = jnp.float32
AXES = ("seq", "dp")
VMEM = pl.BlockSpec(memory_space=pltpu.VMEM)
TOGETHER = 8
LIMIT = 48 * 1024 * 1024


def nt(a, b):
    return lax.dot_general(a, b, (((1,), (1,)), ((), ())), preferred_element_type=F32)


def nn(a, b):
    return lax.dot_general(a, b, (((1,), (0,)), ((), ())), preferred_element_type=F32)


def tn(a, b):
    return lax.dot_general(a, b, (((0,), (0,)), ((), ())), preferred_element_type=F32)


def hi_lo(x):
    high = x.astype(BF).astype(F32)
    return [high, x - high]


def rows(parts):
    return jnp.concatenate(parts, axis=0).astype(BF)


def project(frozen, low_t, up):
    return (frozen.astype(F32) + ADAPTER_SCALE * tn(low_t, up)).astype(BF)


def heads(items, mask):
    sts = [nt(k, q) for q, k, v, g, ups, lows in items]
    dps = [nt(v, g) for q, k, v, g, ups, lows in items]
    bs = [(nt(ups[0], k), nt(ups[1], q), nt(ups[2], g)) for q, k, v, g, ups, lows in items]
    pbs, dss = [], []
    for st, dp in zip(sts, dps):
        st = jnp.where(mask, st * SCALE, -jnp.inf)
        e = jnp.exp(st - jnp.max(st, axis=0, keepdims=True))
        p = e * (1.0 / jnp.sum(e, axis=0, keepdims=True))
        pb = p.astype(BF)
        row_dot = jnp.sum(pb.astype(F32) * dp, axis=0, keepdims=True)
        pbs.append(pb)
        dss.append((p * (dp - row_dot) * SCALE).astype(BF))
    by_q = [nn(rows([it[5][1]] + hi_lo(b[0])), ds) for it, b, ds in zip(items, bs, dss)]
    by_k = [nt(rows([it[5][0]] + hi_lo(b[1])), ds) for it, b, ds in zip(items, bs, dss)]
    av = [nn(it[5][2].astype(BF), pb) for it, pb in zip(items, pbs)]
    rv = [nt(rows(hi_lo(b[2])), pb) for b, pb in zip(bs, pbs)]
    out = []
    for it, bq, bk, a, r in zip(items, by_q, by_k, av, rv):
        q, k, v, g = it[:4]
        us = [nn(rows(hi_lo(bk[:8])), k), nn(rows(hi_lo(bq[:8])), q), nn(rows(hi_lo(a)), g)]
        grads = [u[:8] + u[8:] for u in us]
        ranks = [bq[8:16] + bq[16:24], bk[8:16] + bk[16:24], r[:8] + r[8:]]
        out.append((grads, ranks))
    return out


def causal(keys, queries, offset):
    return lax.broadcasted_iota(jnp.int32, (keys, queries), 0) <= offset + lax.broadcasted_iota(
        jnp.int32, (keys, queries), 1
    )


def local_kernel(frozen, grad, low_t, up, far_out, up_out, rank_out):
    count, width = grad.shape[1:]
    half, half_width = count // 2, width // 2
    low = [low_t[j] for j in range(3)]
    low_f = [x.astype(F32) for x in low]
    near_f = [x[:, half:] for x in low_f]
    ranks = [jnp.zeros((RANK, count), F32)] * 3
    full_mask = causal(count, count, 0)
    half_mask = causal(half, half, 0)
    for first in range(0, half_width, TOGETHER * HEAD_DIM):
        items, places = [], []
        for start in range(first, first + TOGETHER * HEAD_DIM, HEAD_DIM):
            cols = slice(start, start + HEAD_DIM)
            ups = [up[j, :, cols] for j in range(3)]
            q, k, v = [project(frozen[j, 0, :, cols], low[j], ups[j]) for j in range(3)]
            items.append((q, k, v, grad[0, :, cols], ups, low_f))
            places.append(cols)
        for cols, (grads, parts) in zip(places, heads(items, full_mask)):
            for j in range(3):
                up_out[8 * j : 8 * j + 8, cols] = grads[j]
            ranks = [a + b for a, b in zip(ranks, parts)]
    near_ranks = [jnp.zeros((RANK, half), F32)] * 3
    for first in range(half_width, width, TOGETHER * HEAD_DIM):
        items, places = [], []
        for start in range(first, first + TOGETHER * HEAD_DIM, HEAD_DIM):
            cols = slice(start, start + HEAD_DIM)
            ups = [up[j, :, cols] for j in range(3)]
            whole = [project(frozen[j, 0, :, cols], low[j], ups[j]) for j in range(3)]
            for j in range(3):
                far_out[j, :, start - half_width : start - half_width + HEAD_DIM] = whole[j][:half]
            q, k, v = [x[half:] for x in whole]
            items.append((q, k, v, grad[0, half:, cols], ups, near_f))
            places.append(cols)
        for cols, (grads, parts) in zip(places, heads(items, half_mask)):
            for j in range(3):
                up_out[8 * j : 8 * j + 8, cols] = grads[j]
            near_ranks = [a + b for a, b in zip(near_ranks, parts)]
    for j in range(3):
        rank_out[8 * j : 8 * j + 8, :] = ranks[j] + jnp.concatenate(
            [jnp.zeros((RANK, half), F32), near_ranks[j]], axis=1
        )


def far_kernel(own, frozen_kv, low_kv, grad, low_t, up, up_in, rank_in, up_out, rank_out, cross_out):
    half = own.shape[1]
    width = up.shape[2]
    half_width = width // 2
    far_f = [low_t[j].astype(F32)[:, :half] for j in range(3)]
    near = [low_kv[0], low_kv[1]]
    low_k = jnp.concatenate([near[0].astype(F32), far_f[1]], axis=1)
    low_v = jnp.concatenate([near[1].astype(F32), far_f[2]], axis=1)
    mask = causal(2 * half, half, half)
    rank_q = jnp.zeros((RANK, half), F32)
    rank_k = jnp.zeros((RANK, 2 * half), F32)
    rank_v = jnp.zeros((RANK, 2 * half), F32)
    up_out[:, :half_width] = up_in[:, :half_width]
    for first in range(half_width, width, TOGETHER * HEAD_DIM):
        items, places = [], []
        for start in range(first, first + TOGETHER * HEAD_DIM, HEAD_DIM):
            here = slice(start - half_width, start - half_width + HEAD_DIM)
            cols = slice(start, start + HEAD_DIM)
            ups = [up[j, :, cols] for j in range(3)]
            near_k, near_v = [project(frozen_kv[j, :, here], near[j], ups[j + 1]) for j in range(2)]
            k = jnp.concatenate([near_k, own[1, :, here]], axis=0)
            v = jnp.concatenate([near_v, own[2, :, here]], axis=0)
            items.append((own[0, :, here], k, v, grad[0, :half, cols], ups, (far_f[0], low_k, low_v)))
            places.append(cols)
        for cols, (grads, parts) in zip(places, heads(items, mask)):
            for j in range(3):
                up_out[8 * j : 8 * j + 8, cols] = up_in[8 * j : 8 * j + 8, cols] + grads[j]
            rank_q, rank_k, rank_v = rank_q + parts[0], rank_k + parts[1], rank_v + parts[2]
    none = jnp.zeros((RANK, half), F32)
    for j, part in enumerate([rank_q, rank_k[:, half:], rank_v[:, half:]]):
        rank_out[8 * j : 8 * j + 8, :] = rank_in[8 * j : 8 * j + 8, :] + jnp.concatenate(
            [part, none], axis=1
        )
    for j, part in enumerate([rank_k[:, :half], rank_v[:, :half]]):
        cross_out[8 * j : 8 * j + 8, :] = jnp.concatenate([none, part], axis=1)


def position():
    dp = lax.axis_index("dp")
    return dp & 1, (dp & 2) | (lax.axis_index("seq") & 1)


def down_kernel(tokens, rank_in, cross, up_in, keep, send):
    core, place = position()
    ranks = rank_in[...] + jnp.concatenate([jnp.zeros((RANK, rank_in.shape[1]), F32), cross[...]], axis=0)
    both = rows(hi_lo(ranks))
    n = ranks.shape[0]
    up_step, down_step = up_in.shape[1] // 8, tokens.shape[2] // 8
    for c in range(8):
        d = nn(both, tokens[0, :, c * down_step : (c + 1) * down_step])
        d = ADAPTER_SCALE * (d[:n] + d[n:])
        u = ADAPTER_SCALE * up_in[:, c * up_step : (c + 1) * up_step]
        slot = place ^ (c >> 1)

        def put(ref):
            ref[slot, :, :up_step] = u
            ref[slot, :, up_step:] = d

        pl.when(core == (c & 1))(lambda: put(keep))
        pl.when(core != (c & 1))(lambda: put(send))


def spread_kernel(mine, other, down_out, up_out):
    core, place = position()
    up_step, down_step = up_out.shape[2] // 8, down_out.shape[2] // 8
    for c in range(8):
        slot = place ^ (c >> 1)

        def put(ref):
            x = ref[slot].astype(F32)
            for j in range(3):
                up_out[j, :, c * up_step : (c + 1) * up_step] = x[8 * j : 8 * j + 8, :up_step]
                down_out[j, :, c * down_step : (c + 1) * down_step] = x[8 * j : 8 * j + 8, up_step:]

        pl.when(core == (c & 1))(lambda: put(mine))
        pl.when(core != (c & 1))(lambda: put(other))


def call(kernel, outs, *args):
    return pl.pallas_call(
        kernel,
        out_shape=outs,
        in_specs=[VMEM] * len(args),
        out_specs=jax.tree.map(lambda _: VMEM, outs),
        compiler_params=pltpu.CompilerParams(vmem_limit_bytes=LIMIT),
        cost_estimate=pl.CostEstimate(flops=10**9, bytes_accessed=10**6, transcendentals=0),
    )(*args)


def swap(x, bits, total):
    return lax.ppermute(x, AXES, [(i, i ^ bits) for i in range(total)])


def total_sum(keep, send, seqs, dps):
    total = seqs * dps
    keep = keep + swap(send, 1, total)
    own = keep[0]
    got = [swap(keep[s].astype(BF), (s & 2) | (dps if s & 1 else 0), total) for s in (1, 2, 3)]
    own = own + got[0].astype(F32) + got[1].astype(F32) + got[2].astype(F32)
    bit = 2
    while bit < seqs:
        own = own + swap(own, bit * dps, total)
        bit *= 2
    piece = own.astype(BF)
    mine = jnp.stack([piece] + [swap(piece, (s & 2) | (dps if s & 1 else 0), total) for s in (1, 2, 3)])
    return mine, swap(mine, 1, total)


def on_device(tokens, frozen, grad, down_weight, up_weight):
    seqs, dps = lax.axis_size("seq"), lax.axis_size("dp")
    count, width = grad.shape[1:]
    half, half_width = count // 2, width // 2
    forward = [(i, (i + 1) % seqs) for i in range(seqs)]
    backward = [(i, (i - 1) % seqs) for i in range(seqs)]
    frozen_kv = lax.ppermute(frozen[1:, 0, half:, half_width:], "seq", forward)
    low_t = jnp.einsum("psw,gw->psg", down_weight, tokens[0], preferred_element_type=F32).astype(BF)
    low_kv = lax.ppermute(low_t[1:, :, half:], "seq", forward)
    sds = jax.ShapeDtypeStruct
    own, up_part, rank_part = call(
        local_kernel,
        [sds((3, half, half_width), BF), sds((24, width), F32), sds((24, count), F32)],
        frozen, grad, low_t, up_weight,
    )
    up_part, rank_part, cross = call(
        far_kernel,
        [sds((24, width), F32), sds((24, count), F32), sds((16, count), F32)],
        own, frozen_kv, low_kv, grad, low_t, up_weight, up_part, rank_part,
    )
    cross = lax.ppermute(cross, "seq", backward)
    columns = (width + tokens.shape[2]) // 8
    piece = sds((4, 24, columns), F32)
    keep, send = call(down_kernel, [piece, piece], tokens, rank_part, cross, up_part)
    mine, other = total_sum(keep, send, seqs, dps)
    return tuple(
        call(spread_kernel, [sds((3, RANK, tokens.shape[2]), F32), sds((3, RANK, width), F32)], mine, other)
    )


def solution(mesh):
    return jax.shard_map(
        on_device,
        mesh=mesh,
        in_specs=(P("dp", "seq", None), P(None, "dp", "seq", None), P("dp", "seq", None), P(), P()),
        out_specs=(P(), P()),
        check_vma=False,
    )
```

```python
import jax
import jax.numpy as jnp
from jax import lax
from jax.experimental import pallas as pl
from jax.experimental.pallas import tpu as pltpu
from jax.sharding import PartitionSpec as P

HEAD_DIM = 128
RANK = 8
SCALE = HEAD_DIM ** -0.5
ADAPTER_SCALE = 2.0
BF = jnp.bfloat16
F32 = jnp.float32
AXES = ("seq", "dp")
VMEM = pl.BlockSpec(memory_space=pltpu.VMEM)
TOGETHER = 8
LIMIT = 48 * 1024 * 1024


def nt(a, b):
    return lax.dot_general(a, b, (((1,), (1,)), ((), ())), preferred_element_type=F32)


def nn(a, b):
    return lax.dot_general(a, b, (((1,), (0,)), ((), ())), preferred_element_type=F32)


def tn(a, b):
    return lax.dot_general(a, b, (((0,), (0,)), ((), ())), preferred_element_type=F32)


def hi_lo(x):
    high = x.astype(BF).astype(F32)
    return [high, x - high]


def rows(parts):
    return jnp.concatenate(parts, axis=0).astype(BF)


def project(frozen, low_t, up):
    return (frozen.astype(F32) + ADAPTER_SCALE * tn(low_t, up)).astype(BF)


def heads(items, mask):
    sts = [nt(k, q) for q, k, v, g, ups, lows in items]
    dps = [nt(v, g) for q, k, v, g, ups, lows in items]
    bs = [(nt(ups[0], k), nt(ups[1], q), nt(ups[2], g)) for q, k, v, g, ups, lows in items]
    pbs, dss = [], []
    for st, dp in zip(sts, dps):
        st = jnp.where(mask, st * SCALE, -jnp.inf)
        e = jnp.exp(st - jnp.max(st, axis=0, keepdims=True))
        p = e * (1.0 / jnp.sum(e, axis=0, keepdims=True))
        pb = p.astype(BF)
        row_dot = jnp.sum(pb.astype(F32) * dp, axis=0, keepdims=True)
        pbs.append(pb)
        dss.append((p * (dp - row_dot) * SCALE).astype(BF))
    by_q = [nn(rows([it[5][1]] + hi_lo(b[0])), ds) for it, b, ds in zip(items, bs, dss)]
    by_k = [nt(rows([it[5][0]] + hi_lo(b[1])), ds) for it, b, ds in zip(items, bs, dss)]
    av = [nn(it[5][2].astype(BF), pb) for it, pb in zip(items, pbs)]
    rv = [nt(rows(hi_lo(b[2])), pb) for b, pb in zip(bs, pbs)]
    out = []
    for it, bq, bk, a, r in zip(items, by_q, by_k, av, rv):
        q, k, v, g = it[:4]
        us = [nn(rows(hi_lo(bk[:8])), k), nn(rows(hi_lo(bq[:8])), q), nn(rows(hi_lo(a)), g)]
        grads = [u[:8] + u[8:] for u in us]
        ranks = [bq[8:16] + bq[16:24], bk[8:16] + bk[16:24], r[:8] + r[8:]]
        out.append((grads, ranks))
    return out


def causal(keys, queries, offset):
    return lax.broadcasted_iota(jnp.int32, (keys, queries), 0) <= offset + lax.broadcasted_iota(
        jnp.int32, (keys, queries), 1
    )


def local_kernel(frozen, grad, low_t, up, far_out, up_out, rank_out):
    count, width = grad.shape[1:]
    half, half_width = count // 2, width // 2
    low = [low_t[j] for j in range(3)]
    low_f = [x.astype(F32) for x in low]
    near_f = [x[:, half:] for x in low_f]
    ranks = [jnp.zeros((RANK, count), F32)] * 3
    full_mask = causal(count, count, 0)
    half_mask = causal(half, half, 0)
    for first in range(0, half_width, TOGETHER * HEAD_DIM):
        items, places = [], []
        for start in range(first, first + TOGETHER * HEAD_DIM, HEAD_DIM):
            cols = slice(start, start + HEAD_DIM)
            ups = [up[j, :, cols] for j in range(3)]
            q, k, v = [project(frozen[j, 0, :, cols], low[j], ups[j]) for j in range(3)]
            items.append((q, k, v, grad[0, :, cols], ups, low_f))
            places.append(cols)
        for cols, (grads, parts) in zip(places, heads(items, full_mask)):
            for j in range(3):
                up_out[8 * j : 8 * j + 8, cols] = grads[j]
            ranks = [a + b for a, b in zip(ranks, parts)]
    near_ranks = [jnp.zeros((RANK, half), F32)] * 3
    for first in range(half_width, width, TOGETHER * HEAD_DIM):
        items, places = [], []
        for start in range(first, first + TOGETHER * HEAD_DIM, HEAD_DIM):
            cols = slice(start, start + HEAD_DIM)
            ups = [up[j, :, cols] for j in range(3)]
            whole = [project(frozen[j, 0, :, cols], low[j], ups[j]) for j in range(3)]
            for j in range(3):
                far_out[j, :, start - half_width : start - half_width + HEAD_DIM] = whole[j][:half]
            q, k, v = [x[half:] for x in whole]
            items.append((q, k, v, grad[0, half:, cols], ups, near_f))
            places.append(cols)
        for cols, (grads, parts) in zip(places, heads(items, half_mask)):
            for j in range(3):
                up_out[8 * j : 8 * j + 8, cols] = grads[j]
            near_ranks = [a + b for a, b in zip(near_ranks, parts)]
    for j in range(3):
        rank_out[8 * j : 8 * j + 8, :] = ranks[j] + jnp.concatenate(
            [jnp.zeros((RANK, half), F32), near_ranks[j]], axis=1
        )


def far_kernel(own, frozen_kv, low_kv, grad, low_t, up, up_in, rank_in, up_out, rank_out, cross_out):
    half = own.shape[1]
    width = up.shape[2]
    half_width = width // 2
    far_f = [low_t[j].astype(F32)[:, :half] for j in range(3)]
    near = [low_kv[0], low_kv[1]]
    low_k = jnp.concatenate([near[0].astype(F32), far_f[1]], axis=1)
    low_v = jnp.concatenate([near[1].astype(F32), far_f[2]], axis=1)
    mask = causal(2 * half, half, half)
    rank_q = jnp.zeros((RANK, half), F32)
    rank_k = jnp.zeros((RANK, 2 * half), F32)
    rank_v = jnp.zeros((RANK, 2 * half), F32)
    up_out[:, :half_width] = up_in[:, :half_width]
    for first in range(half_width, width, TOGETHER * HEAD_DIM):
        items, places = [], []
        for start in range(first, first + TOGETHER * HEAD_DIM, HEAD_DIM):
            here = slice(start - half_width, start - half_width + HEAD_DIM)
            cols = slice(start, start + HEAD_DIM)
            ups = [up[j, :, cols] for j in range(3)]
            near_k, near_v = [project(frozen_kv[j, :, here], near[j], ups[j + 1]) for j in range(2)]
            k = jnp.concatenate([near_k, own[1, :, here]], axis=0)
            v = jnp.concatenate([near_v, own[2, :, here]], axis=0)
            items.append((own[0, :, here], k, v, grad[0, :half, cols], ups, (far_f[0], low_k, low_v)))
            places.append(cols)
        for cols, (grads, parts) in zip(places, heads(items, mask)):
            for j in range(3):
                up_out[8 * j : 8 * j + 8, cols] = up_in[8 * j : 8 * j + 8, cols] + grads[j]
            rank_q, rank_k, rank_v = rank_q + parts[0], rank_k + parts[1], rank_v + parts[2]
    none = jnp.zeros((RANK, half), F32)
    for j, part in enumerate([rank_q, rank_k[:, half:], rank_v[:, half:]]):
        rank_out[8 * j : 8 * j + 8, :] = rank_in[8 * j : 8 * j + 8, :] + jnp.concatenate(
            [part, none], axis=1
        )
    for j, part in enumerate([rank_k[:, :half], rank_v[:, :half]]):
        cross_out[8 * j : 8 * j + 8, :] = jnp.concatenate([none, part], axis=1)


def place():
    return (lax.axis_index("dp") & 2) | (lax.axis_index("seq") & 1)


def down_kernel(tokens, rank_in, cross, up_in, out):
    here = place()
    ranks = rank_in[...] + jnp.concatenate([jnp.zeros((RANK, rank_in.shape[1]), F32), cross[...]], axis=0)
    both = rows(hi_lo(ranks))
    n = ranks.shape[0]
    up_step, down_step = up_in.shape[1] // 4, tokens.shape[2] // 4
    for c in range(4):
        d = nn(both, tokens[0, :, c * down_step : (c + 1) * down_step])
        slot = here ^ c
        out[slot, :, :up_step] = ADAPTER_SCALE * up_in[:, c * up_step : (c + 1) * up_step]
        out[slot, :, up_step:] = ADAPTER_SCALE * (d[:n] + d[n:])


def spread_kernel(mine, other, down_out, up_out):
    here = place()
    odd = (lax.axis_index("dp") & 1) == 1
    up_step, down_step = up_out.shape[2] // 4, down_out.shape[2] // 4
    for c in range(4):
        slot = here ^ c

        def put(ref):
            x = ref[slot].astype(F32)
            for j in range(3):
                up_out[j, :, c * up_step : (c + 1) * up_step] = x[8 * j : 8 * j + 8, :up_step]
                down_out[j, :, c * down_step : (c + 1) * down_step] = x[8 * j : 8 * j + 8, up_step:]

        pl.when(odd)(lambda: put(mine))
        pl.when(jnp.logical_not(odd))(lambda: put(other))


def call(kernel, outs, *args):
    return pl.pallas_call(
        kernel,
        out_shape=outs,
        in_specs=[VMEM] * len(args),
        out_specs=jax.tree.map(lambda _: VMEM, outs),
        compiler_params=pltpu.CompilerParams(vmem_limit_bytes=LIMIT),
        cost_estimate=pl.CostEstimate(flops=10**9, bytes_accessed=10**6, transcendentals=0),
    )(*args)


def odd_swap(x, bits, total):
    return lax.ppermute(x, AXES, [(i, i ^ bits) for i in range(1, total, 2)])


def along(x, pairs, seqs, dps):
    moves = [
        (i, i + (b - a) * 2 * dps)
        for i in range(1, seqs * dps, 2)
        for a, b in pairs
        if (i // (2 * dps)) % 4 == a
    ]
    return lax.ppermute(x, AXES, moves)


def total_sum(part, seqs, dps):
    total = seqs * dps
    bits = [(s & 2) | (dps if s & 1 else 0) for s in range(4)]
    part = part + lax.ppermute(part, AXES, [(i, i + 1) for i in range(0, total, 2)])
    got = [odd_swap(part[s].astype(BF), bits[s], total).astype(F32) for s in (1, 2, 3)]
    own = part[0] + got[0] + got[1] + got[2]
    bit = 8
    while bit < seqs:
        own = own + odd_swap(own, bit * dps, total)
        bit *= 2
    own = own + along(own, [(0, 1), (3, 2)], seqs, dps)
    own = own + along(own, [(1, 2), (2, 1)], seqs, dps)
    piece = own.astype(BF)
    line = (lax.axis_index("seq") // 2) % 4
    piece = jnp.where((line == 0) | (line == 3), along(piece, [(1, 0), (2, 3)], seqs, dps), piece)
    mine = jnp.stack([piece] + [odd_swap(piece, bits[s], total) for s in (1, 2, 3)])
    return mine, lax.ppermute(mine, AXES, [(i, i - 1) for i in range(1, total, 2)])


def on_device(tokens, frozen, grad, down_weight, up_weight):
    seqs, dps = lax.axis_size("seq"), lax.axis_size("dp")
    count, width = grad.shape[1:]
    half, half_width = count // 2, width // 2
    forward = [(i, (i + 1) % seqs) for i in range(seqs)]
    backward = [(i, (i - 1) % seqs) for i in range(seqs)]
    frozen_kv = lax.ppermute(frozen[1:, 0, half:, half_width:], "seq", forward)
    low_t = jnp.einsum("psw,gw->psg", down_weight, tokens[0], preferred_element_type=F32).astype(BF)
    low_kv = lax.ppermute(low_t[1:, :, half:], "seq", forward)
    sds = jax.ShapeDtypeStruct
    own, up_part, rank_part = call(
        local_kernel,
        [sds((3, half, half_width), BF), sds((24, width), F32), sds((24, count), F32)],
        frozen, grad, low_t, up_weight,
    )
    up_part, rank_part, cross = call(
        far_kernel,
        [sds((24, width), F32), sds((24, count), F32), sds((16, count), F32)],
        own, frozen_kv, low_kv, grad, low_t, up_weight, up_part, rank_part,
    )
    cross = lax.ppermute(cross, "seq", backward)
    columns = (width + tokens.shape[2]) // 4
    part = call(down_kernel, sds((4, 24, columns), F32), tokens, rank_part, cross, up_part)
    mine, other = total_sum(part, seqs, dps)
    return tuple(
        call(spread_kernel, [sds((3, RANK, tokens.shape[2]), F32), sds((3, RANK, width), F32)], mine, other)
    )


def solution(mesh):
    return jax.shard_map(
        on_device,
        mesh=mesh,
        in_specs=(P("dp", "seq", None), P(None, "dp", "seq", None), P("dp", "seq", None), P(), P()),
        out_specs=(P(), P()),
        check_vma=False,
    )
```

```python
import jax
import jax.numpy as jnp
from jax import lax
from jax.experimental import pallas as pl
from jax.experimental.pallas import tpu as pltpu
from jax.sharding import PartitionSpec as P

HEAD_DIM = 128
RANK = 8
SCALE = HEAD_DIM ** -0.5
ADAPTER_SCALE = 2.0
BF = jnp.bfloat16
F32 = jnp.float32
AXES = ("seq", "dp")
VMEM = pl.BlockSpec(memory_space=pltpu.VMEM)
TOGETHER = 8
LIMIT = 48 * 1024 * 1024


def nt(a, b):
    return lax.dot_general(a, b, (((1,), (1,)), ((), ())), preferred_element_type=F32)


def nn(a, b):
    return lax.dot_general(a, b, (((1,), (0,)), ((), ())), preferred_element_type=F32)


def tn(a, b):
    return lax.dot_general(a, b, (((0,), (0,)), ((), ())), preferred_element_type=F32)


def hi_lo(x):
    high = x.astype(BF).astype(F32)
    return [high, x - high]


def rows(parts):
    return jnp.concatenate(parts, axis=0).astype(BF)


def project(frozen, low_t, up):
    return (frozen.astype(F32) + ADAPTER_SCALE * tn(low_t, up)).astype(BF)


def heads(items, mask):
    sts = [nt(k, q) for q, k, v, g, ups, lows in items]
    dps = [nt(v, g) for q, k, v, g, ups, lows in items]
    bs = [(nt(ups[0], k), nt(ups[1], q), nt(ups[2], g)) for q, k, v, g, ups, lows in items]
    pbs, dss = [], []
    for st, dp in zip(sts, dps):
        st = jnp.where(mask, st * SCALE, -jnp.inf)
        e = jnp.exp(st - jnp.max(st, axis=0, keepdims=True))
        p = e * (1.0 / jnp.sum(e, axis=0, keepdims=True))
        pb = p.astype(BF)
        row_dot = jnp.sum(pb.astype(F32) * dp, axis=0, keepdims=True)
        pbs.append(pb)
        dss.append((p * (dp - row_dot) * SCALE).astype(BF))
    by_q = [nn(rows([it[5][1]] + hi_lo(b[0])), ds) for it, b, ds in zip(items, bs, dss)]
    by_k = [nt(rows([it[5][0]] + hi_lo(b[1])), ds) for it, b, ds in zip(items, bs, dss)]
    av = [nn(it[5][2].astype(BF), pb) for it, pb in zip(items, pbs)]
    rv = [nt(rows(hi_lo(b[2])), pb) for b, pb in zip(bs, pbs)]
    out = []
    for it, bq, bk, a, r in zip(items, by_q, by_k, av, rv):
        q, k, v, g = it[:4]
        us = [nn(rows(hi_lo(bk[:8])), k), nn(rows(hi_lo(bq[:8])), q), nn(rows(hi_lo(a)), g)]
        grads = [u[:8] + u[8:] for u in us]
        ranks = [bq[8:16] + bq[16:24], bk[8:16] + bk[16:24], r[:8] + r[8:]]
        out.append((grads, ranks))
    return out


def causal(keys, queries, offset):
    return lax.broadcasted_iota(jnp.int32, (keys, queries), 0) <= offset + lax.broadcasted_iota(
        jnp.int32, (keys, queries), 1
    )


def local_kernel(frozen, grad, low_t, up, far_out, up_out, rank_out):
    count, width = grad.shape[1:]
    half, half_width = count // 2, width // 2
    low = [low_t[j] for j in range(3)]
    low_f = [x.astype(F32) for x in low]
    near_f = [x[:, half:] for x in low_f]
    ranks = [jnp.zeros((RANK, count), F32)] * 3
    full_mask = causal(count, count, 0)
    half_mask = causal(half, half, 0)
    for first in range(0, half_width, TOGETHER * HEAD_DIM):
        items, places = [], []
        for start in range(first, first + TOGETHER * HEAD_DIM, HEAD_DIM):
            cols = slice(start, start + HEAD_DIM)
            ups = [up[j, :, cols] for j in range(3)]
            q, k, v = [project(frozen[j, 0, :, cols], low[j], ups[j]) for j in range(3)]
            items.append((q, k, v, grad[0, :, cols], ups, low_f))
            places.append(cols)
        for cols, (grads, parts) in zip(places, heads(items, full_mask)):
            for j in range(3):
                up_out[8 * j : 8 * j + 8, cols] = grads[j]
            ranks = [a + b for a, b in zip(ranks, parts)]
    near_ranks = [jnp.zeros((RANK, half), F32)] * 3
    for first in range(half_width, width, TOGETHER * HEAD_DIM):
        items, places = [], []
        for start in range(first, first + TOGETHER * HEAD_DIM, HEAD_DIM):
            cols = slice(start, start + HEAD_DIM)
            ups = [up[j, :, cols] for j in range(3)]
            whole = [project(frozen[j, 0, :, cols], low[j], ups[j]) for j in range(3)]
            for j in range(3):
                far_out[j, :, start - half_width : start - half_width + HEAD_DIM] = whole[j][:half]
            q, k, v = [x[half:] for x in whole]
            items.append((q, k, v, grad[0, half:, cols], ups, near_f))
            places.append(cols)
        for cols, (grads, parts) in zip(places, heads(items, half_mask)):
            for j in range(3):
                up_out[8 * j : 8 * j + 8, cols] = grads[j]
            near_ranks = [a + b for a, b in zip(near_ranks, parts)]
    for j in range(3):
        rank_out[8 * j : 8 * j + 8, :] = ranks[j] + jnp.concatenate(
            [jnp.zeros((RANK, half), F32), near_ranks[j]], axis=1
        )


def far_kernel(own, frozen_kv, low_kv, grad, low_t, up, up_in, rank_in, up_out, rank_out, cross_out):
    half = own.shape[1]
    width = up.shape[2]
    half_width = width // 2
    far_f = [low_t[j].astype(F32)[:, :half] for j in range(3)]
    near = [low_kv[0], low_kv[1]]
    low_k = jnp.concatenate([near[0].astype(F32), far_f[1]], axis=1)
    low_v = jnp.concatenate([near[1].astype(F32), far_f[2]], axis=1)
    mask = causal(2 * half, half, half)
    rank_q = jnp.zeros((RANK, half), F32)
    rank_k = jnp.zeros((RANK, 2 * half), F32)
    rank_v = jnp.zeros((RANK, 2 * half), F32)
    up_out[:, :half_width] = up_in[:, :half_width]
    for first in range(half_width, width, TOGETHER * HEAD_DIM):
        items, places = [], []
        for start in range(first, first + TOGETHER * HEAD_DIM, HEAD_DIM):
            here = slice(start - half_width, start - half_width + HEAD_DIM)
            cols = slice(start, start + HEAD_DIM)
            ups = [up[j, :, cols] for j in range(3)]
            near_k, near_v = [project(frozen_kv[j, :, here], near[j], ups[j + 1]) for j in range(2)]
            k = jnp.concatenate([near_k, own[1, :, here]], axis=0)
            v = jnp.concatenate([near_v, own[2, :, here]], axis=0)
            items.append((own[0, :, here], k, v, grad[0, :half, cols], ups, (far_f[0], low_k, low_v)))
            places.append(cols)
        for cols, (grads, parts) in zip(places, heads(items, mask)):
            for j in range(3):
                up_out[8 * j : 8 * j + 8, cols] = up_in[8 * j : 8 * j + 8, cols] + grads[j]
            rank_q, rank_k, rank_v = rank_q + parts[0], rank_k + parts[1], rank_v + parts[2]
    none = jnp.zeros((RANK, half), F32)
    for j, part in enumerate([rank_q, rank_k[:, half:], rank_v[:, half:]]):
        rank_out[8 * j : 8 * j + 8, :] = rank_in[8 * j : 8 * j + 8, :] + jnp.concatenate(
            [part, none], axis=1
        )
    for j, part in enumerate([rank_k[:, :half], rank_v[:, :half]]):
        cross_out[8 * j : 8 * j + 8, :] = jnp.concatenate([none, part], axis=1)


def position():
    seq, dp = lax.axis_index("seq"), lax.axis_index("dp")
    bits = seq ^ dp
    for shift in (4, 2, 1):
        bits = bits ^ (bits >> shift)
    return bits & 1, (dp & 2) | (seq & 1)


def down_kernel(tokens, rank_in, cross, up_in, keep, send):
    half, quarter = position()
    first = half == 0
    ranks = rank_in[...] + jnp.concatenate([jnp.zeros((RANK, rank_in.shape[1]), F32), cross[...]], axis=0)
    both = rows(hi_lo(ranks))
    n = ranks.shape[0]
    up_step, down_step = up_in.shape[1] // 8, tokens.shape[2] // 8
    for c in range(4):
        d = nn(both, tokens[0, :, 2 * c * down_step : 2 * (c + 1) * down_step])
        d = ADAPTER_SCALE * (d[:n] + d[n:])
        u = ADAPTER_SCALE * up_in[:, 2 * c * up_step : 2 * (c + 1) * up_step]
        slot = quarter ^ c
        keep[slot, :, :up_step] = jnp.where(first, u[:, :up_step], u[:, up_step:])
        send[slot, :, :up_step] = jnp.where(first, u[:, up_step:], u[:, :up_step])
        keep[slot, :, up_step:] = jnp.where(first, d[:, :down_step], d[:, down_step:])
        send[slot, :, up_step:] = jnp.where(first, d[:, down_step:], d[:, :down_step])


def spread_kernel(mine, other, down_out, up_out):
    half, quarter = position()
    up_step, down_step = up_out.shape[2] // 8, down_out.shape[2] // 8
    for c in range(4):
        slot = quarter ^ c
        a, b = mine[slot].astype(F32), other[slot].astype(F32)
        for h in range(2):
            x = jnp.where(half == h, a, b)
            at = 2 * c + h
            for j in range(3):
                part = x[8 * j : 8 * j + 8]
                up_out[j, :, at * up_step : (at + 1) * up_step] = part[:, :up_step]
                down_out[j, :, at * down_step : (at + 1) * down_step] = part[:, up_step:]


def cut_kernel(frozen, out, sems):
    half, half_width = out.shape[1:]
    copies = [
        pltpu.make_async_copy(frozen.at[j + 1, 0, pl.ds(half, half), pl.ds(half_width, half_width)], out.at[j], sems.at[j])
        for j in range(2)
    ]
    for copy in copies:
        copy.start()
    for copy in copies:
        copy.wait()


def cut(frozen):
    half, half_width = frozen.shape[2] // 2, frozen.shape[3] // 2
    return pl.pallas_call(
        cut_kernel,
        out_shape=jax.ShapeDtypeStruct((2, half, half_width), BF),
        in_specs=[pl.BlockSpec(memory_space=pl.ANY)],
        out_specs=VMEM,
        scratch_shapes=[pltpu.SemaphoreType.DMA((2,))],
    )(frozen)


def call(kernel, outs, *args):
    return pl.pallas_call(
        kernel,
        out_shape=outs,
        in_specs=[VMEM] * len(args),
        out_specs=jax.tree.map(lambda _: VMEM, outs),
        compiler_params=pltpu.CompilerParams(vmem_limit_bytes=LIMIT),
        cost_estimate=pl.CostEstimate(flops=10**9, bytes_accessed=10**6, transcendentals=0),
    )(*args)


def swap(x, bits, total):
    return lax.ppermute(x, AXES, [(i, i ^ bits) for i in range(total)])


def total_sum(keep, send, seqs, dps):
    total = seqs * dps
    partner = {1: dps | 1, 2: 3, 3: dps | 2}
    keep = keep + swap(send, 1, total)
    got = [swap(keep[s].astype(BF), partner[s], total).astype(F32) for s in (1, 2, 3)]
    own = keep[0] + got[0] + got[1] + got[2]
    bit = 2
    while bit < seqs:
        own = own + swap(own, bit * dps | 1, total)
        bit *= 2
    piece = own.astype(BF)
    mine = jnp.stack([piece] + [swap(piece, partner[s], total) for s in (1, 2, 3)])
    return mine, swap(mine, 1, total)


def on_device(tokens, frozen, grad, down_weight, up_weight):
    seqs, dps = lax.axis_size("seq"), lax.axis_size("dp")
    count, width = grad.shape[1:]
    half, half_width = count // 2, width // 2
    forward = [(i, (i + 1) % seqs) for i in range(seqs)]
    backward = [(i, (i - 1) % seqs) for i in range(seqs)]
    frozen_kv = lax.ppermute(cut(frozen), "seq", forward)
    low_t = jnp.einsum("psw,gw->psg", down_weight, tokens[0], preferred_element_type=F32).astype(BF)
    low_kv = lax.ppermute(low_t[1:, :, half:], "seq", forward)
    sds = jax.ShapeDtypeStruct
    own, up_part, rank_part = call(
        local_kernel,
        [sds((3, half, half_width), BF), sds((24, width), F32), sds((24, count), F32)],
        frozen, grad, low_t, up_weight,
    )
    up_part, rank_part, cross = call(
        far_kernel,
        [sds((24, width), F32), sds((24, count), F32), sds((16, count), F32)],
        own, frozen_kv, low_kv, grad, low_t, up_weight, up_part, rank_part,
    )
    cross = lax.ppermute(cross, "seq", backward)
    columns = (width + tokens.shape[2]) // 8
    piece = sds((4, 24, columns), F32)
    keep, send = call(down_kernel, [piece, piece], tokens, rank_part, cross, up_part)
    mine, other = total_sum(keep, send, seqs, dps)
    return tuple(
        call(spread_kernel, [sds((3, RANK, tokens.shape[2]), F32), sds((3, RANK, width), F32)], mine, other)
    )


def solution(mesh):
    return jax.shard_map(
        on_device,
        mesh=mesh,
        in_specs=(P("dp", "seq", None), P(None, "dp", "seq", None), P("dp", "seq", None), P(), P()),
        out_specs=(P(), P()),
        check_vma=False,
    )
```

```python
import jax
import jax.numpy as jnp
from jax import lax
from jax.experimental import pallas as pl
from jax.experimental.pallas import tpu as pltpu
from jax.sharding import PartitionSpec as P

HEAD_DIM = 128
RANK = 8
SCALE = HEAD_DIM ** -0.5
ADAPTER_SCALE = 2.0
BF = jnp.bfloat16
F32 = jnp.float32
AXES = ("seq", "dp")
VMEM = pl.BlockSpec(memory_space=pltpu.VMEM)
TOGETHER = 8
LIMIT = 48 * 1024 * 1024


def nt(a, b):
    return lax.dot_general(a, b, (((1,), (1,)), ((), ())), preferred_element_type=F32)


def nn(a, b):
    return lax.dot_general(a, b, (((1,), (0,)), ((), ())), preferred_element_type=F32)


def tn(a, b):
    return lax.dot_general(a, b, (((0,), (0,)), ((), ())), preferred_element_type=F32)


def hi_lo(x):
    high = x.astype(BF).astype(F32)
    return [high, x - high]


def rows(parts):
    return jnp.concatenate(parts, axis=0).astype(BF)


def project(frozen, low_t, up):
    return (frozen.astype(F32) + ADAPTER_SCALE * tn(low_t, up)).astype(BF)


def scores(items, mask):
    sts = [nt(k, q) for q, k, v, g, ups, lows in items]
    dps = [nt(v, g) for q, k, v, g, ups, lows in items]
    bs = [(nt(ups[1], q), nt(ups[2], g)) for q, k, v, g, ups, lows in items]
    pbs, dss = [], []
    for st, dp in zip(sts, dps):
        st = jnp.where(mask, st * SCALE, -jnp.inf)
        e = jnp.exp(st - jnp.max(st, axis=0, keepdims=True))
        p = e * (1.0 / jnp.sum(e, axis=0, keepdims=True))
        pb = p.astype(BF)
        row_dot = jnp.sum(pb.astype(F32) * dp, axis=0, keepdims=True)
        pbs.append(pb)
        dss.append((p * (dp - row_dot) * SCALE).astype(BF))
    by_k = [nt(rows([it[5][0]] + hi_lo(b[0])), ds) for it, b, ds in zip(items, bs, dss)]
    by_v = [nt(rows(hi_lo(b[1])), pb) for b, pb in zip(bs, pbs)]
    return [
        (pb, ds, bk[:8], bk[8:16] + bk[16:24], r[:8] + r[8:])
        for pb, ds, bk, r in zip(pbs, dss, by_k, by_v)
    ]


def rest(items, found):
    bqs = [nt(it[4][0], it[1]) for it in items]
    by_q = [nn(rows([it[5][1]] + hi_lo(b)), f[1]) for it, b, f in zip(items, bqs, found)]
    av = [nn(it[5][2].astype(BF), f[0]) for it, f in zip(items, found)]
    out = []
    for it, f, bq, a in zip(items, found, by_q, av):
        q, k, v, g = it[:4]
        us = [nn(rows(hi_lo(f[2])), k), nn(rows(hi_lo(bq[:8])), q), nn(rows(hi_lo(a)), g)]
        out.append(([u[:8] + u[8:] for u in us], bq[8:16] + bq[16:24]))
    return out


def heads(items, mask):
    found = scores(items, mask)
    return [
        (grads, [rank_q, f[3], f[4]]) for f, (grads, rank_q) in zip(found, rest(items, found))
    ]


def causal(keys, queries, offset):
    return lax.broadcasted_iota(jnp.int32, (keys, queries), 0) <= offset + lax.broadcasted_iota(
        jnp.int32, (keys, queries), 1
    )


def local_kernel(frozen, grad, low_t, up, far_out, up_out, rank_out):
    count, width = grad.shape[1:]
    half, half_width = count // 2, width // 2
    low = [low_t[j] for j in range(3)]
    low_f = [x.astype(F32) for x in low]
    near_f = [x[:, half:] for x in low_f]
    ranks = [jnp.zeros((RANK, count), F32)] * 3
    full_mask = causal(count, count, 0)
    half_mask = causal(half, half, 0)
    for first in range(0, half_width, TOGETHER * HEAD_DIM):
        items, places = [], []
        for start in range(first, first + TOGETHER * HEAD_DIM, HEAD_DIM):
            cols = slice(start, start + HEAD_DIM)
            ups = [up[j, :, cols] for j in range(3)]
            q, k, v = [project(frozen[j, 0, :, cols], low[j], ups[j]) for j in range(3)]
            items.append((q, k, v, grad[0, :, cols], ups, low_f))
            places.append(cols)
        for cols, (grads, parts) in zip(places, heads(items, full_mask)):
            for j in range(3):
                up_out[8 * j : 8 * j + 8, cols] = grads[j]
            ranks = [a + b for a, b in zip(ranks, parts)]
    near_ranks = [jnp.zeros((RANK, half), F32)] * 3
    for first in range(half_width, width, TOGETHER * HEAD_DIM):
        items, places = [], []
        for start in range(first, first + TOGETHER * HEAD_DIM, HEAD_DIM):
            cols = slice(start, start + HEAD_DIM)
            ups = [up[j, :, cols] for j in range(3)]
            whole = [project(frozen[j, 0, :, cols], low[j], ups[j]) for j in range(3)]
            for j in range(3):
                far_out[j, :, start - half_width : start - half_width + HEAD_DIM] = whole[j][:half]
            q, k, v = [x[half:] for x in whole]
            items.append((q, k, v, grad[0, half:, cols], ups, near_f))
            places.append(cols)
        for cols, (grads, parts) in zip(places, heads(items, half_mask)):
            for j in range(3):
                up_out[8 * j : 8 * j + 8, cols] = grads[j]
            near_ranks = [a + b for a, b in zip(near_ranks, parts)]
    for j in range(3):
        rank_out[8 * j : 8 * j + 8, :] = ranks[j] + jnp.concatenate(
            [jnp.zeros((RANK, half), F32), near_ranks[j]], axis=1
        )


def far_items(own, near_kv, low_kv, grad, low_t, up, first):
    half = own.shape[1]
    half_width = up.shape[2] // 2
    far_f = [low_t[j].astype(F32)[:, :half] for j in range(3)]
    lows = [far_f[0]] + [
        jnp.concatenate([low_kv[j].astype(F32), far_f[j + 1]], axis=1) for j in range(2)
    ]
    items = []
    for h, near in enumerate(near_kv):
        here = slice(first + h * HEAD_DIM, first + (h + 1) * HEAD_DIM)
        cols = slice(half_width + here.start, half_width + here.stop)
        ups = [up[j, :, cols] for j in range(3)]
        k, v = [jnp.concatenate([near[j], own[j + 1, :, here]], axis=0) for j in range(2)]
        items.append((own[0, :, here], k, v, grad[0, :half, cols], ups, lows))
    return items


def near_rows(frozen_kv, low_kv, up, first):
    half_width = up.shape[2] // 2
    near = []
    for h in range(frozen_kv.shape[2] // HEAD_DIM):
        here = slice(h * HEAD_DIM, (h + 1) * HEAD_DIM)
        start = half_width + first + h * HEAD_DIM
        near.append(
            [project(frozen_kv[j, :, here], low_kv[j], up[j + 1, :, start : start + HEAD_DIM]) for j in range(2)]
        )
    return near


def left(x):
    return jnp.concatenate([x, jnp.zeros_like(x)], axis=1)


def right(x):
    return jnp.concatenate([jnp.zeros_like(x), x], axis=1)


def far_first(own, frozen_kv, low_kv, grad, low_t, up, rank_in, up_out, rank_out, cross_out):
    half = own.shape[1]
    items = far_items(own, near_rows(frozen_kv, low_kv, up, 0), low_kv, grad, low_t, up, 0)
    parts = heads(items, causal(2 * half, half, half))
    for h, (grads, _) in enumerate(parts):
        for j in range(3):
            up_out[8 * j : 8 * j + 8, h * HEAD_DIM : (h + 1) * HEAD_DIM] = grads[j]
    for j in range(3):
        part = sum(ranks[j] for _, ranks in parts)
        rank_out[8 * j : 8 * j + 8, :] = rank_in[8 * j : 8 * j + 8, :] + left(part[:, -half:])
        if j > 0:
            cross_out[8 * j - 8 : 8 * j, :] = right(part[:, :half])


def far_second(
    own, frozen_kv, low_kv, grad, low_t, up, rank_in, cross_in, rank_out, cross_out, near_out, pb_out, ds_out, aq_out
):
    half = own.shape[1]
    first = own.shape[2] - frozen_kv.shape[2]
    near = near_rows(frozen_kv, low_kv, up, first)
    items = far_items(own, near, low_kv, grad, low_t, up, first)
    found = scores(items, causal(2 * half, half, half))
    rank_out[:8, :] = rank_in[:8, :]
    for j in (1, 2):
        part = sum(f[j + 2] for f in found)
        rank_out[8 * j : 8 * j + 8, :] = rank_in[8 * j : 8 * j + 8, :] + left(part[:, half:])
        cross_out[8 * j - 8 : 8 * j, :] = cross_in[8 * j - 8 : 8 * j, :] + right(part[:, :half])
    for h, f in enumerate(found):
        near_out[h] = near[h][0]
        pb_out[h] = f[0]
        ds_out[h] = f[1]
        aq_out[8 * h : 8 * h + 8, :] = f[2]


def far_rest(own, low_kv, grad, low_t, up, rank_in, near, pb, ds, aq, up_out, rank_out):
    n = near.shape[0]
    first = own.shape[2] - n * HEAD_DIM
    items = far_items(own, [[near[h]] * 2 for h in range(n)], low_kv, grad, low_t, up, first)
    parts = rest(items, [(pb[h], ds[h], aq[8 * h : 8 * h + 8, :]) for h in range(n)])
    for h, (grads, _) in enumerate(parts):
        for j in range(3):
            up_out[8 * j : 8 * j + 8, h * HEAD_DIM : (h + 1) * HEAD_DIM] = grads[j]
    rank_out[:8, :] = rank_in[:8, :] + left(sum(rank for _, rank in parts))
    rank_out[8:, :] = rank_in[8:, :]


def position():
    seq, dp = lax.axis_index("seq"), lax.axis_index("dp")
    bits = seq ^ dp
    for shift in (4, 2, 1):
        bits = bits ^ (bits >> shift)
    return bits & 1, (dp & 2) | (seq & 1)


def down_kernel(tokens, rank_in, cross, up_in, up_a, up_b, keep, send):
    half, quarter = position()
    first = half == 0
    ranks = rank_in[...] + jnp.concatenate([jnp.zeros((RANK, rank_in.shape[1]), F32), cross[...]], axis=0)
    both = rows(hi_lo(ranks))
    n = ranks.shape[0]
    up_step, down_step = up_in.shape[1] // 8, tokens.shape[2] // 8
    for c in range(4):
        d = nn(both, tokens[0, :, 2 * c * down_step : 2 * (c + 1) * down_step])
        d = ADAPTER_SCALE * (d[:n] + d[n:])
        u = up_in[:, 2 * c * up_step : 2 * (c + 1) * up_step]
        u = ADAPTER_SCALE * (u + (up_a[...] if c == 2 else up_b[...]) if c >= 2 else u)
        slot = quarter ^ c
        keep[slot, :, :up_step] = jnp.where(first, u[:, :up_step], u[:, up_step:])
        send[slot, :, :up_step] = jnp.where(first, u[:, up_step:], u[:, :up_step])
        keep[slot, :, up_step:] = jnp.where(first, d[:, :down_step], d[:, down_step:])
        send[slot, :, up_step:] = jnp.where(first, d[:, down_step:], d[:, :down_step])


def spread_kernel(mine, other, down_out, up_out):
    half, quarter = position()
    up_step, down_step = up_out.shape[2] // 8, down_out.shape[2] // 8
    for c in range(4):
        slot = quarter ^ c
        a, b = mine[slot].astype(F32), other[slot].astype(F32)
        for h in range(2):
            x = jnp.where(half == h, a, b)
            at = 2 * c + h
            for j in range(3):
                part = x[8 * j : 8 * j + 8]
                up_out[j, :, at * up_step : (at + 1) * up_step] = part[:, :up_step]
                down_out[j, :, at * down_step : (at + 1) * down_step] = part[:, up_step:]


def call(kernel, outs, *args):
    return pl.pallas_call(
        kernel,
        out_shape=outs,
        in_specs=[VMEM] * len(args),
        out_specs=jax.tree.map(lambda _: VMEM, outs),
        compiler_params=pltpu.CompilerParams(vmem_limit_bytes=LIMIT),
        cost_estimate=pl.CostEstimate(flops=10**9, bytes_accessed=10**6, transcendentals=0),
    )(*args)


def swap(x, bits, total):
    return lax.ppermute(x, AXES, [(i, i ^ bits) for i in range(total)])


def total_sum(keep, send, seqs, dps):
    total = seqs * dps
    partner = {1: dps | 1, 2: 3, 3: dps | 2}
    keep = keep + swap(send, 1, total)
    got = [swap(keep[s].astype(BF), partner[s], total).astype(F32) for s in (1, 2, 3)]
    own = keep[0] + got[0] + got[1] + got[2]
    bit = 2
    while bit < seqs:
        if 2 * bit >= seqs:
            own = own.astype(BF)
        own = own.astype(F32) + swap(own, bit * dps | 1, total).astype(F32)
        bit *= 2
    piece = own.astype(BF)
    mine = jnp.stack([piece] + [swap(piece, partner[s], total) for s in (1, 2, 3)])
    return mine, swap(mine, 1, total)


def on_device(tokens, frozen, grad, down_weight, up_weight):
    seqs, dps = lax.axis_size("seq"), lax.axis_size("dp")
    count, width = grad.shape[1:]
    half, half_width = count // 2, width // 2
    forward = [(i, (i + 1) % seqs) for i in range(seqs)]
    backward = [(i, (i - 1) % seqs) for i in range(seqs)]
    middle = half_width + half_width // 2
    frozen_kv = [
        lax.ppermute(frozen[1:, 0, half:, half_width:middle], "seq", forward),
        lax.ppermute(frozen[1:, 0, half:, middle:], "seq", forward),
    ]
    low_t = jnp.einsum("psw,gw->psg", down_weight, tokens[0], preferred_element_type=F32).astype(BF)
    low_kv = lax.ppermute(low_t[1:, :, half:], "seq", forward)
    sds = jax.ShapeDtypeStruct
    own, up_part, rank = call(
        local_kernel,
        [sds((3, half, half_width), BF), sds((24, width), F32), sds((24, count), F32)],
        frozen, grad, low_t, up_weight,
    )
    up_side, rank_side, cross_side = sds((24, half_width // 2), F32), sds((24, count), F32), sds((16, count), F32)
    up_a, rank, cross = call(
        far_first, [up_side, rank_side, cross_side],
        own, frozen_kv[0], low_kv, grad, low_t, up_weight, rank,
    )
    n = half_width // HEAD_DIM // 2
    by_keys = sds((n, count, half), BF)
    rank, cross, *kept = call(
        far_second,
        [rank_side, cross_side, sds((n, half, HEAD_DIM), BF), by_keys, by_keys, sds((8 * n, count), F32)],
        own, frozen_kv[1], low_kv, grad, low_t, up_weight, rank, cross,
    )
    cross = lax.ppermute(cross, "seq", backward)
    up_b, rank = call(far_rest, [up_side, rank_side], own, low_kv, grad, low_t, up_weight, rank, *kept)
    columns = (width + tokens.shape[2]) // 8
    piece = sds((4, 24, columns), F32)
    keep, send = call(down_kernel, [piece, piece], tokens, rank, cross, up_part, up_a, up_b)
    mine, other = total_sum(keep, send, seqs, dps)
    return tuple(
        call(spread_kernel, [sds((3, RANK, tokens.shape[2]), F32), sds((3, RANK, width), F32)], mine, other)
    )


def solution(mesh):
    return jax.shard_map(
        on_device,
        mesh=mesh,
        in_specs=(P("dp", "seq", None), P(None, "dp", "seq", None), P("dp", "seq", None), P(), P()),
        out_specs=(P(), P()),
        check_vma=False,
    )
```

```python
import jax
import jax.numpy as jnp
from jax import lax
from jax.experimental import pallas as pl
from jax.experimental.pallas import tpu as pltpu
from jax.sharding import PartitionSpec as P

HEAD_DIM = 128
RANK = 8
SCALE = HEAD_DIM ** -0.5
ADAPTER_SCALE = 2.0
BF = jnp.bfloat16
F32 = jnp.float32
AXES = ("seq", "dp")
COST = pl.CostEstimate(flops=10**9, bytes_accessed=10**6, transcendentals=0)
VMEM = pl.BlockSpec(memory_space=pltpu.VMEM)
LIMIT = 48 * 1024 * 1024


def nt(a, b):
    return lax.dot_general(a, b, (((1,), (1,)), ((), ())), preferred_element_type=F32)


def nn(a, b):
    return lax.dot_general(a, b, (((1,), (0,)), ((), ())), preferred_element_type=F32)


def tn(a, b):
    return lax.dot_general(a, b, (((0,), (0,)), ((), ())), preferred_element_type=F32)


def hi_lo(x):
    high = x.astype(BF).astype(F32)
    return [high, x - high]


def rows(parts):
    return jnp.concatenate(parts, axis=0).astype(BF)


def project(frozen, low_t, up):
    return (frozen.astype(F32) + ADAPTER_SCALE * tn(low_t, up)).astype(BF)


def scores(items, mask):
    sts = [nt(k, q) for q, k, v, g, ups, lows in items]
    dps = [nt(v, g) for q, k, v, g, ups, lows in items]
    bs = [(nt(ups[1], q), nt(ups[2], g)) for q, k, v, g, ups, lows in items]
    pbs, dss = [], []
    for st, dp in zip(sts, dps):
        st = jnp.where(mask, st * SCALE, -jnp.inf)
        e = jnp.exp(st - jnp.max(st, axis=0, keepdims=True))
        p = e * (1.0 / jnp.sum(e, axis=0, keepdims=True))
        pb = p.astype(BF)
        row_dot = jnp.sum(pb.astype(F32) * dp, axis=0, keepdims=True)
        pbs.append(pb)
        dss.append((p * (dp - row_dot) * SCALE).astype(BF))
    by_k = [nt(rows([it[5][0]] + hi_lo(b[0])), ds) for it, b, ds in zip(items, bs, dss)]
    by_v = [nt(rows(hi_lo(b[1])), pb) for b, pb in zip(bs, pbs)]
    return [
        (pb, ds, bk[:8], bk[8:16] + bk[16:24], r[:8] + r[8:])
        for pb, ds, bk, r in zip(pbs, dss, by_k, by_v)
    ]


def rest(items, found):
    bqs = [nt(it[4][0], it[1]) for it in items]
    by_q = [nn(rows([it[5][1]] + hi_lo(b)), f[1]) for it, b, f in zip(items, bqs, found)]
    av = [nn(it[5][2].astype(BF), f[0]) for it, f in zip(items, found)]
    out = []
    for it, f, bq, a in zip(items, found, by_q, av):
        q, k, v, g = it[:4]
        us = [nn(rows(hi_lo(f[2])), k), nn(rows(hi_lo(bq[:8])), q), nn(rows(hi_lo(a)), g)]
        out.append(([u[:8] + u[8:] for u in us], bq[8:16] + bq[16:24]))
    return out


def heads(items, mask):
    found = scores(items, mask)
    return [
        (grads, [rank_q, f[3], f[4]]) for f, (grads, rank_q) in zip(found, rest(items, found))
    ]


def causal(keys, queries, offset):
    return lax.broadcasted_iota(jnp.int32, (keys, queries), 0) <= offset + lax.broadcasted_iota(
        jnp.int32, (keys, queries), 1
    )


def low_kernel(tokens, down, low_out, near_out, buffer, sems):
    chunks = buffer.shape[0]
    step = buffer.shape[2]
    copies = [
        pltpu.make_async_copy(tokens.at[0, :, pl.ds(c * step, step)], buffer.at[c], sems.at[c])
        for c in range(chunks)
    ]
    for copy in copies:
        copy.start()
    low = 0.0
    for c, copy in enumerate(copies):
        copy.wait()
        low = low + nt(down[:, c * step : (c + 1) * step], buffer[c])
    half = near_out.shape[2]
    for j in range(3):
        part = low[8 * j : 8 * j + 8].astype(BF)
        low_out[j] = part
        if j > 0:
            near_out[j - 1] = part[:, half:]


def low_rank(tokens, down_weight):
    count, model = tokens.shape[1:]
    chunks = 4
    return pl.pallas_call(
        low_kernel,
        out_shape=[
            jax.ShapeDtypeStruct((3, RANK, count), BF),
            jax.ShapeDtypeStruct((2, RANK, count // 2), BF),
        ],
        in_specs=[pl.BlockSpec(memory_space=pltpu.HBM), VMEM],
        out_specs=[VMEM, VMEM],
        scratch_shapes=[pltpu.VMEM((chunks, count, model // chunks), BF), pltpu.SemaphoreType.DMA((chunks,))],
    )(tokens, down_weight.reshape(3 * RANK, model))


def plain_kernel(frozen, grad, low_t, up, far_out, up_out, rank_out, plain_grad, sem):
    count, width = grad.shape[1:]
    half, half_width = count // 2, width // 2
    copy = pltpu.make_async_copy(grad.at[0, :, pl.ds(0, half_width)], plain_grad, sem)
    copy.start()
    low = [low_t[j] for j in range(3)]
    low_f = [x.astype(F32) for x in low]
    far = [x[:, :half] for x in low]
    starts = range(0, half_width, HEAD_DIM)
    held = []
    for start in starts:
        cols = slice(start, start + HEAD_DIM)
        held.append([project(frozen[j, 0, :, cols], low[j], up[j, :, cols]) for j in range(3)])
    for start in starts:
        cols = slice(half_width + start, half_width + start + HEAD_DIM)
        for j in range(3):
            far_out[j, :, start : start + HEAD_DIM] = project(frozen[j, 0, :half, cols], far[j], up[j, :, cols])
    copy.wait()
    items = []
    for start, (q, k, v) in zip(starts, held):
        cols = slice(start, start + HEAD_DIM)
        items.append((q, k, v, plain_grad[:, cols], [up[j, :, cols] for j in range(3)], low_f))
    parts = heads(items, causal(count, count, 0))
    for start, (grads, _) in zip(starts, parts):
        for j in range(3):
            up_out[8 * j : 8 * j + 8, start : start + HEAD_DIM] = grads[j]
    for j in range(3):
        rank_out[8 * j : 8 * j + 8, :] = sum(ranks[j] for _, ranks in parts)


def near_kernel(frozen, grad, low_t, up, up_out, rank_out):
    count, width = grad.shape[1:]
    half, half_width = count // 2, width // 2
    low = [low_t[j][:, half:] for j in range(3)]
    low_f = [x.astype(F32) for x in low]
    starts = range(half_width, width, HEAD_DIM)
    items = []
    for start in starts:
        cols = slice(start, start + HEAD_DIM)
        ups = [up[j, :, cols] for j in range(3)]
        q, k, v = [project(frozen[j, 0, half:, cols], low[j], ups[j]) for j in range(3)]
        items.append((q, k, v, grad[0, half:, cols], ups, low_f))
    parts = heads(items, causal(half, half, 0))
    for start, (grads, _) in zip(starts, parts):
        for j in range(3):
            up_out[8 * j : 8 * j + 8, start - half_width : start - half_width + HEAD_DIM] = grads[j]
    for j in range(3):
        rank_out[8 * j : 8 * j + 8, :] = right(sum(ranks[j] for _, ranks in parts))


def far_items(own, near_kv, low_kv, grad, low_t, up, first):
    half = own.shape[1]
    half_width = up.shape[2] // 2
    far_f = [low_t[j].astype(F32)[:, :half] for j in range(3)]
    lows = [far_f[0]] + [
        jnp.concatenate([low_kv[j].astype(F32), far_f[j + 1]], axis=1) for j in range(2)
    ]
    items = []
    for h, near in enumerate(near_kv):
        here = slice(first + h * HEAD_DIM, first + (h + 1) * HEAD_DIM)
        cols = slice(half_width + here.start, half_width + here.stop)
        ups = [up[j, :, cols] for j in range(3)]
        k, v = [jnp.concatenate([near[j], own[j + 1, :, here]], axis=0) for j in range(2)]
        items.append((own[0, :, here], k, v, grad[0, :half, cols], ups, lows))
    return items


def near_rows(frozen_kv, low_kv, up, first):
    half_width = up.shape[2] // 2
    near = []
    for h in range(frozen_kv.shape[2] // HEAD_DIM):
        here = slice(h * HEAD_DIM, (h + 1) * HEAD_DIM)
        start = half_width + first + h * HEAD_DIM
        near.append(
            [project(frozen_kv[j, :, here], low_kv[j], up[j + 1, :, start : start + HEAD_DIM]) for j in range(2)]
        )
    return near


def left(x):
    return jnp.concatenate([x, jnp.zeros_like(x)], axis=1)


def right(x):
    return jnp.concatenate([jnp.zeros_like(x), x], axis=1)


def far_first(own, frozen_kv, low_kv, grad, low_t, up, rank_in, up_out, rank_out, cross_out):
    half = own.shape[1]
    items = far_items(own, near_rows(frozen_kv, low_kv, up, 0), low_kv, grad, low_t, up, 0)
    parts = heads(items, causal(2 * half, half, half))
    for h, (grads, _) in enumerate(parts):
        for j in range(3):
            up_out[8 * j : 8 * j + 8, h * HEAD_DIM : (h + 1) * HEAD_DIM] = grads[j]
    for j in range(3):
        part = sum(ranks[j] for _, ranks in parts)
        rank_out[8 * j : 8 * j + 8, :] = rank_in[8 * j : 8 * j + 8, :] + left(part[:, -half:])
        if j > 0:
            cross_out[8 * j - 8 : 8 * j, :] = right(part[:, :half])


def far_second(
    own, frozen_kv, low_kv, grad, low_t, up, rank_in, cross_in, rank_out, cross_out, near_out, pb_out, ds_out, aq_out
):
    half = own.shape[1]
    first = own.shape[2] - frozen_kv.shape[2]
    near = near_rows(frozen_kv, low_kv, up, first)
    items = far_items(own, near, low_kv, grad, low_t, up, first)
    found = scores(items, causal(2 * half, half, half))
    rank_out[:8, :] = rank_in[:8, :]
    for j in (1, 2):
        part = sum(f[j + 2] for f in found)
        rank_out[8 * j : 8 * j + 8, :] = rank_in[8 * j : 8 * j + 8, :] + left(part[:, half:])
        cross_out[8 * j - 8 : 8 * j, :] = cross_in[8 * j - 8 : 8 * j, :] + right(part[:, :half])
    for h, f in enumerate(found):
        near_out[h] = near[h][0]
        pb_out[h] = f[0]
        ds_out[h] = f[1]
        aq_out[8 * h : 8 * h + 8, :] = f[2]


def far_rest(own, low_kv, grad, low_t, up, rank_in, near, pb, ds, aq, up_out, rank_out):
    n = near.shape[0]
    first = own.shape[2] - n * HEAD_DIM
    items = far_items(own, [[near[h]] * 2 for h in range(n)], low_kv, grad, low_t, up, first)
    parts = rest(items, [(pb[h], ds[h], aq[8 * h : 8 * h + 8, :]) for h in range(n)])
    for h, (grads, _) in enumerate(parts):
        for j in range(3):
            up_out[8 * j : 8 * j + 8, h * HEAD_DIM : (h + 1) * HEAD_DIM] = grads[j]
    rank_out[:8, :] = rank_in[:8, :] + left(sum(rank for _, rank in parts))
    rank_out[8:, :] = rank_in[8:, :]


def position():
    seq, dp = lax.axis_index("seq"), lax.axis_index("dp")
    bits = seq ^ dp
    for shift in (4, 2, 1):
        bits = bits ^ (bits >> shift)
    return bits & 1, (dp & 2) | (seq & 1)


def down_kernel(tokens, rank_in, rank_near, cross, up_plain, up_near, up_a, up_b, keep, send):
    half, quarter = position()
    first = half == 0
    ranks = rank_in[...] + rank_near[...] + jnp.concatenate(
        [jnp.zeros((RANK, rank_in.shape[1]), F32), cross[...]], axis=0
    )
    both = rows(hi_lo(ranks))
    n = ranks.shape[0]
    up_step, down_step = up_a.shape[1] // 2, tokens.shape[2] // 8
    for c in range(4):
        d = nn(both, tokens[0, :, 2 * c * down_step : 2 * (c + 1) * down_step])
        d = ADAPTER_SCALE * (d[:n] + d[n:])
        cols = slice((c % 2) * 2 * up_step, (c % 2 + 1) * 2 * up_step)
        if c < 2:
            u = up_plain[:, cols]
        else:
            u = up_near[:, cols] + (up_a if c == 2 else up_b)[...]
        u = ADAPTER_SCALE * u
        slot = quarter ^ c
        keep[slot, :, :up_step] = jnp.where(first, u[:, :up_step], u[:, up_step:])
        send[slot, :, :up_step] = jnp.where(first, u[:, up_step:], u[:, :up_step])
        keep[slot, :, up_step:] = jnp.where(first, d[:, :down_step], d[:, down_step:])
        send[slot, :, up_step:] = jnp.where(first, d[:, down_step:], d[:, :down_step])


def spread_kernel(mine, other, down_out, up_out):
    half, quarter = position()
    up_step, down_step = up_out.shape[2] // 8, down_out.shape[2] // 8
    for c in range(4):
        slot = quarter ^ c
        a, b = mine[slot].astype(F32), other[slot].astype(F32)
        for h in range(2):
            x = jnp.where(half == h, a, b)
            at = 2 * c + h
            for j in range(3):
                part = x[8 * j : 8 * j + 8]
                up_out[j, :, at * up_step : (at + 1) * up_step] = part[:, :up_step]
                down_out[j, :, at * down_step : (at + 1) * down_step] = part[:, up_step:]


def call(kernel, outs, *args):
    return pl.pallas_call(
        kernel,
        out_shape=outs,
        in_specs=[VMEM] * len(args),
        out_specs=jax.tree.map(lambda _: VMEM, outs),
        compiler_params=pltpu.CompilerParams(vmem_limit_bytes=LIMIT),
        cost_estimate=COST,
    )(*args)


def swap(x, bits, total):
    return lax.ppermute(x, AXES, [(i, i ^ bits) for i in range(total)])


def total_sum(keep, send, seqs, dps):
    total = seqs * dps
    partner = {1: dps | 1, 2: 3, 3: dps | 2}
    keep = keep + swap(send, 1, total)
    got = [swap(keep[s].astype(BF), partner[s], total).astype(F32) for s in (1, 2, 3)]
    own = keep[0] + got[0] + got[1] + got[2]
    bit = 2
    while bit < seqs:
        if 2 * bit >= seqs:
            own = own.astype(BF)
        own = own.astype(F32) + swap(own, bit * dps | 1, total).astype(F32)
        bit *= 2
    piece = own.astype(BF)
    mine = jnp.stack([piece] + [swap(piece, partner[s], total) for s in (1, 2, 3)])
    return mine, swap(mine, 1, total)


def on_device(tokens, frozen, grad, down_weight, up_weight):
    seqs, dps = lax.axis_size("seq"), lax.axis_size("dp")
    count, width = grad.shape[1:]
    half, half_width = count // 2, width // 2
    forward = [(i, (i + 1) % seqs) for i in range(seqs)]
    backward = [(i, (i - 1) % seqs) for i in range(seqs)]
    middle = half_width + half_width // 2
    frozen_kv = [
        lax.ppermute(frozen[1:, 0, half:, half_width:middle], "seq", forward),
        lax.ppermute(frozen[1:, 0, half:, middle:], "seq", forward),
    ]
    low_t, low_near = low_rank(tokens, down_weight)
    low_kv = lax.ppermute(low_near, "seq", forward)
    sds = jax.ShapeDtypeStruct
    up_half, up_side = sds((24, half_width), F32), sds((24, half_width // 2), F32)
    rank_side, cross_side = sds((24, count), F32), sds((16, count), F32)
    own, up_plain, rank = pl.pallas_call(
        plain_kernel,
        out_shape=[sds((3, half, half_width), BF), up_half, rank_side],
        in_specs=[VMEM, pl.BlockSpec(memory_space=pltpu.HBM), VMEM, VMEM],
        out_specs=[VMEM] * 3,
        scratch_shapes=[pltpu.VMEM((count, half_width), BF), pltpu.SemaphoreType.DMA],
        compiler_params=pltpu.CompilerParams(vmem_limit_bytes=LIMIT),
        cost_estimate=COST,
    )(frozen, grad, low_t, up_weight)
    up_a, rank, cross = call(
        far_first, [up_side, rank_side, cross_side],
        own, frozen_kv[0], low_kv, grad, low_t, up_weight, rank,
    )
    n = half_width // HEAD_DIM // 2
    by_keys = sds((n, count, half), BF)
    rank, cross, *kept = call(
        far_second,
        [rank_side, cross_side, sds((n, half, HEAD_DIM), BF), by_keys, by_keys, sds((8 * n, count), F32)],
        own, frozen_kv[1], low_kv, grad, low_t, up_weight, rank, cross,
    )
    rank, *held = lax.optimization_barrier((rank, grad, low_t, up_weight))
    cross = lax.ppermute(cross, "seq", backward)
    up_near, rank_near = call(near_kernel, [up_half, rank_side], frozen, *held)
    up_b, rank = call(far_rest, [up_side, rank_side], own, low_kv, grad, low_t, up_weight, rank, *kept)
    columns = (width + tokens.shape[2]) // 8
    piece = sds((4, 24, columns), F32)
    keep, send = call(down_kernel, [piece, piece], tokens, rank, rank_near, cross, up_plain, up_near, up_a, up_b)
    mine, other = total_sum(keep, send, seqs, dps)
    return tuple(
        call(spread_kernel, [sds((3, RANK, tokens.shape[2]), F32), sds((3, RANK, width), F32)], mine, other)
    )


def solution(mesh):
    return jax.shard_map(
        on_device,
        mesh=mesh,
        in_specs=(P("dp", "seq", None), P(None, "dp", "seq", None), P("dp", "seq", None), P(), P()),
        out_specs=(P(), P()),
        check_vma=False,
    )
```

```python
import functools

import jax
import jax.numpy as jnp
from jax import lax
from jax.experimental import pallas as pl
from jax.experimental.pallas import tpu as pltpu
from jax.sharding import PartitionSpec as P

HEAD_DIM = 128
RANK = 8
SCALE = HEAD_DIM ** -0.5
ADAPTER_SCALE = 2.0
BF = jnp.bfloat16
F32 = jnp.float32
AXES = ("seq", "dp")
COST = pl.CostEstimate(flops=10**6, bytes_accessed=10**4, transcendentals=0)
VMEM = pl.BlockSpec(memory_space=pltpu.VMEM)
LIMIT = 48 * 1024 * 1024


def nt(a, b):
    return lax.dot_general(a, b, (((1,), (1,)), ((), ())), preferred_element_type=F32)


def nn(a, b):
    return lax.dot_general(a, b, (((1,), (0,)), ((), ())), preferred_element_type=F32)


def tn(a, b):
    return lax.dot_general(a, b, (((0,), (0,)), ((), ())), preferred_element_type=F32)


def hi_lo(x):
    high = x.astype(BF).astype(F32)
    return [high, x - high]


def rows(parts):
    return jnp.concatenate(parts, axis=0).astype(BF)


def project(frozen, low_t, up):
    return (frozen.astype(F32) + ADAPTER_SCALE * tn(low_t, up)).astype(BF)


def scores(items, mask):
    sts = [nt(k, q) for q, k, v, g, ups, lows in items]
    dps = [nt(v, g) for q, k, v, g, ups, lows in items]
    bs = [(nt(ups[1], q), nt(ups[2], g)) for q, k, v, g, ups, lows in items]
    pbs, dss = [], []
    for st, dp in zip(sts, dps):
        st = jnp.where(mask, st * SCALE, -jnp.inf)
        e = jnp.exp(st - jnp.max(st, axis=0, keepdims=True))
        p = e * (1.0 / jnp.sum(e, axis=0, keepdims=True))
        pb = p.astype(BF)
        row_dot = jnp.sum(pb.astype(F32) * dp, axis=0, keepdims=True)
        pbs.append(pb)
        dss.append((p * (dp - row_dot) * SCALE).astype(BF))
    by_k = [nt(rows([it[5][0]] + hi_lo(b[0])), ds) for it, b, ds in zip(items, bs, dss)]
    by_v = [nt(rows(hi_lo(b[1])), pb) for b, pb in zip(bs, pbs)]
    return [
        (pb, ds, bk[:8], bk[8:16] + bk[16:24], r[:8] + r[8:])
        for pb, ds, bk, r in zip(pbs, dss, by_k, by_v)
    ]


def rest(items, found):
    bqs = [nt(it[4][0], it[1]) for it in items]
    by_q = [nn(rows([it[5][1]] + hi_lo(b)), f[1]) for it, b, f in zip(items, bqs, found)]
    av = [nn(it[5][2].astype(BF), f[0]) for it, f in zip(items, found)]
    out = []
    for it, f, bq, a in zip(items, found, by_q, av):
        q, k, v, g = it[:4]
        us = [nn(rows(hi_lo(f[2])), k), nn(rows(hi_lo(bq[:8])), q), nn(rows(hi_lo(a)), g)]
        out.append(([u[:8] + u[8:] for u in us], bq[8:16] + bq[16:24]))
    return out


def heads(items, mask):
    found = scores(items, mask)
    return [
        (grads, [rank_q, f[3], f[4]]) for f, (grads, rank_q) in zip(found, rest(items, found))
    ]


def causal(keys, queries, offset):
    return lax.broadcasted_iota(jnp.int32, (keys, queries), 0) <= offset + lax.broadcasted_iota(
        jnp.int32, (keys, queries), 1
    )


def project_kernel(frozen, low_t, up, out):
    for j in range(3):
        for start in range(0, out.shape[2], 512):
            cols = slice(start, start + 512)
            out[j, :, cols] = project(frozen[j, 0, :, cols], low_t[j], up[j, :, cols])


def group_kernel(first, start, projected, grad, low_t, up, up_out, rank_out):
    count = grad.shape[1]
    low = [low_t[j].astype(F32)[:, first:] for j in range(3)]
    starts = range(0, up_out.shape[1], HEAD_DIM)
    items = []
    for h in starts:
        cols = slice(start + h, start + h + HEAD_DIM)
        q, k, v = [projected[j, first:, cols] for j in range(3)]
        items.append((q, k, v, grad[0, first:, cols], [up[j, :, cols] for j in range(3)], low))
    parts = heads(items, causal(count - first, count - first, 0))
    for h, (grads, _) in zip(starts, parts):
        for j in range(3):
            up_out[8 * j : 8 * j + 8, h : h + HEAD_DIM] = grads[j]
    for j in range(3):
        part = sum(ranks[j] for _, ranks in parts)
        rank_out[8 * j : 8 * j + 8, :] = right(part) if first else part


def far_items(projected, near_kv, low_kv, grad, low_t, up, first):
    half = projected.shape[1] // 2
    half_width = up.shape[2] // 2
    far_f = [low_t[j].astype(F32)[:, :half] for j in range(3)]
    lows = [far_f[0]] + [
        jnp.concatenate([low_kv[j].astype(F32), far_f[j + 1]], axis=1) for j in range(2)
    ]
    items = []
    for h, near in enumerate(near_kv):
        start = half_width + first + h * HEAD_DIM
        cols = slice(start, start + HEAD_DIM)
        ups = [up[j, :, cols] for j in range(3)]
        k, v = [jnp.concatenate([near[j], projected[j + 1, :half, cols]], axis=0) for j in range(2)]
        items.append((projected[0, :half, cols], k, v, grad[0, :half, cols], ups, lows))
    return items


def near_rows(frozen_kv, low_kv, up, first):
    half_width = up.shape[2] // 2
    near = []
    for h in range(frozen_kv.shape[2] // HEAD_DIM):
        here = slice(h * HEAD_DIM, (h + 1) * HEAD_DIM)
        start = half_width + first + h * HEAD_DIM
        near.append(
            [project(frozen_kv[j, :, here], low_kv[j], up[j + 1, :, start : start + HEAD_DIM]) for j in range(2)]
        )
    return near


def left(x):
    return jnp.concatenate([x, jnp.zeros_like(x)], axis=1)


def right(x):
    return jnp.concatenate([jnp.zeros_like(x), x], axis=1)


def far_first(projected, frozen_kv, low_kv, grad, low_t, up, rank_in, up_out, rank_out, cross_out):
    half = projected.shape[1] // 2
    items = far_items(projected, near_rows(frozen_kv, low_kv, up, 0), low_kv, grad, low_t, up, 0)
    parts = heads(items, causal(2 * half, half, half))
    for h, (grads, _) in enumerate(parts):
        for j in range(3):
            up_out[8 * j : 8 * j + 8, h * HEAD_DIM : (h + 1) * HEAD_DIM] = grads[j]
    for j in range(3):
        part = sum(ranks[j] for _, ranks in parts)
        rank_out[8 * j : 8 * j + 8, :] = rank_in[8 * j : 8 * j + 8, :] + left(part[:, -half:])
        if j > 0:
            cross_out[8 * j - 8 : 8 * j, :] = right(part[:, :half])


def far_second(
    projected, frozen_kv, low_kv, grad, low_t, up, rank_in, cross_in, rank_out, cross_out, near_out, pb_out, ds_out, aq_out
):
    half = projected.shape[1] // 2
    first = projected.shape[2] // 2 - frozen_kv.shape[2]
    near = near_rows(frozen_kv, low_kv, up, first)
    items = far_items(projected, near, low_kv, grad, low_t, up, first)
    found = scores(items, causal(2 * half, half, half))
    rank_out[:8, :] = rank_in[:8, :]
    for j in (1, 2):
        part = sum(f[j + 2] for f in found)
        rank_out[8 * j : 8 * j + 8, :] = rank_in[8 * j : 8 * j + 8, :] + left(part[:, half:])
        cross_out[8 * j - 8 : 8 * j, :] = cross_in[8 * j - 8 : 8 * j, :] + right(part[:, :half])
    for h, f in enumerate(found):
        near_out[h] = near[h][0]
        pb_out[h] = f[0]
        ds_out[h] = f[1]
        aq_out[8 * h : 8 * h + 8, :] = f[2]


def far_rest(projected, low_kv, grad, low_t, up, rank_in, near, pb, ds, aq, up_out, rank_out):
    n = near.shape[0]
    first = projected.shape[2] // 2 - n * HEAD_DIM
    items = far_items(projected, [[near[h]] * 2 for h in range(n)], low_kv, grad, low_t, up, first)
    parts = rest(items, [(pb[h], ds[h], aq[8 * h : 8 * h + 8, :]) for h in range(n)])
    for h, (grads, _) in enumerate(parts):
        for j in range(3):
            up_out[8 * j : 8 * j + 8, h * HEAD_DIM : (h + 1) * HEAD_DIM] = grads[j]
    rank_out[:8, :] = rank_in[:8, :] + left(sum(rank for _, rank in parts))
    rank_out[8:, :] = rank_in[8:, :]


def position():
    seq, dp = lax.axis_index("seq"), lax.axis_index("dp")
    bits = seq ^ dp
    for shift in (4, 2, 1):
        bits = bits ^ (bits >> shift)
    return bits & 1, (dp & 2) | (seq & 1)


def down_kernel(tokens, rank_in, rank_near, cross, up_plain, up_near, up_a, up_b, keep, send):
    half, quarter = position()
    first = half == 0
    ranks = rank_in[...] + rank_near[...] + jnp.concatenate(
        [jnp.zeros((RANK, rank_in.shape[1]), F32), cross[...]], axis=0
    )
    both = rows(hi_lo(ranks))
    n = ranks.shape[0]
    up_step, down_step = up_a.shape[1] // 2, tokens.shape[2] // 8
    for c in range(4):
        d = nn(both, tokens[0, :, 2 * c * down_step : 2 * (c + 1) * down_step])
        d = ADAPTER_SCALE * (d[:n] + d[n:])
        cols = slice((c % 2) * 2 * up_step, (c % 2 + 1) * 2 * up_step)
        if c < 2:
            u = up_plain[:, cols]
        else:
            u = up_near[:, cols] + (up_a if c == 2 else up_b)[...]
        u = ADAPTER_SCALE * u
        slot = quarter ^ c
        keep[slot, :, :up_step] = jnp.where(first, u[:, :up_step], u[:, up_step:])
        send[slot, :, :up_step] = jnp.where(first, u[:, up_step:], u[:, :up_step])
        keep[slot, :, up_step:] = jnp.where(first, d[:, :down_step], d[:, down_step:])
        send[slot, :, up_step:] = jnp.where(first, d[:, down_step:], d[:, :down_step])


def spread_kernel(mine, other, down_out, up_out):
    half, quarter = position()
    up_step, down_step = up_out.shape[2] // 8, down_out.shape[2] // 8
    for c in range(4):
        slot = quarter ^ c
        a, b = mine[slot].astype(F32), other[slot].astype(F32)
        for h in range(2):
            x = jnp.where(half == h, a, b)
            at = 2 * c + h
            for j in range(3):
                part = x[8 * j : 8 * j + 8]
                up_out[j, :, at * up_step : (at + 1) * up_step] = part[:, :up_step]
                down_out[j, :, at * down_step : (at + 1) * down_step] = part[:, up_step:]


def call(kernel, outs, *args):
    return pl.pallas_call(
        kernel,
        out_shape=outs,
        in_specs=[VMEM] * len(args),
        out_specs=jax.tree.map(lambda _: VMEM, outs),
        compiler_params=pltpu.CompilerParams(vmem_limit_bytes=LIMIT),
        cost_estimate=COST,
    )(*args)


def swap(x, bits, total):
    return lax.ppermute(x, AXES, [(i, i ^ bits) for i in range(total)])


def total_sum(keep, send, seqs, dps):
    total = seqs * dps
    partner = {1: dps | 1, 2: 3, 3: dps | 2}
    keep = keep + swap(send, 1, total)
    got = [swap(keep[s].astype(BF), partner[s], total).astype(F32) for s in (1, 2, 3)]
    own = keep[0] + got[0] + got[1] + got[2]
    bit = 2
    while bit < seqs:
        if 2 * bit >= seqs:
            own = own.astype(BF)
        own = own.astype(F32) + swap(own, bit * dps | 1, total).astype(F32)
        bit *= 2
    piece = own.astype(BF)
    mine = jnp.stack([piece] + [swap(piece, partner[s], total) for s in (1, 2, 3)])
    return mine, swap(mine, 1, total)


def on_device(tokens, frozen, grad, down_weight, up_weight):
    seqs, dps = lax.axis_size("seq"), lax.axis_size("dp")
    count, width = grad.shape[1:]
    half, half_width = count // 2, width // 2
    forward = [(i, (i + 1) % seqs) for i in range(seqs)]
    backward = [(i, (i - 1) % seqs) for i in range(seqs)]
    middle = half_width + half_width // 2
    frozen_kv = [
        lax.ppermute(frozen[1:, 0, half:, half_width:middle], "seq", forward),
        lax.ppermute(frozen[1:, 0, half:, middle:], "seq", forward),
    ]
    low_t = jnp.einsum("psw,gw->psg", down_weight, tokens[0], preferred_element_type=F32).astype(BF)
    low_kv = lax.ppermute(low_t[1:, :, half:], "seq", forward)
    sds = jax.ShapeDtypeStruct
    up_half, up_side = sds((24, half_width), F32), sds((24, half_width // 2), F32)
    rank_side, cross_side = sds((24, count), F32), sds((16, count), F32)
    projected = call(project_kernel, sds((3, count, width), BF), frozen, low_t, up_weight)
    up_plain, rank = call(
        functools.partial(group_kernel, 0, 0), [up_half, rank_side], projected, grad, low_t, up_weight
    )
    up_a, rank, cross = call(
        far_first, [up_side, rank_side, cross_side],
        projected, frozen_kv[0], low_kv, grad, low_t, up_weight, rank,
    )
    n = half_width // HEAD_DIM // 2
    by_keys = sds((n, count, half), BF)
    rank, cross, *kept = call(
        far_second,
        [rank_side, cross_side, sds((n, half, HEAD_DIM), BF), by_keys, by_keys, sds((8 * n, count), F32)],
        projected, frozen_kv[1], low_kv, grad, low_t, up_weight, rank, cross,
    )
    rank, *held = lax.optimization_barrier((rank, grad, low_t, up_weight))
    cross = lax.ppermute(cross, "seq", backward)
    up_near, rank_near = call(
        functools.partial(group_kernel, half, half_width), [up_half, rank_side], projected, *held
    )
    up_b, rank = call(far_rest, [up_side, rank_side], projected, low_kv, grad, low_t, up_weight, rank, *kept)
    columns = (width + tokens.shape[2]) // 8
    piece = sds((4, 24, columns), F32)
    keep, send = call(down_kernel, [piece, piece], tokens, rank, rank_near, cross, up_plain, up_near, up_a, up_b)
    mine, other = total_sum(keep, send, seqs, dps)
    return tuple(
        call(spread_kernel, [sds((3, RANK, tokens.shape[2]), F32), sds((3, RANK, width), F32)], mine, other)
    )


def solution(mesh):
    return jax.shard_map(
        on_device,
        mesh=mesh,
        in_specs=(P("dp", "seq", None), P(None, "dp", "seq", None), P("dp", "seq", None), P(), P()),
        out_specs=(P(), P()),
        check_vma=False,
    )
```

```python
import functools

import jax
import jax.numpy as jnp
from jax import lax
from jax.experimental import pallas as pl
from jax.experimental.pallas import tpu as pltpu
from jax.sharding import PartitionSpec as P

HEAD_DIM = 128
RANK = 8
SCALE = HEAD_DIM ** -0.5
ADAPTER_SCALE = 2.0
BF = jnp.bfloat16
F32 = jnp.float32
AXES = ("seq", "dp")
COST = pl.CostEstimate(flops=10**6, bytes_accessed=10**4, transcendentals=0)
VMEM = pl.BlockSpec(memory_space=pltpu.VMEM)
LIMIT = 48 * 1024 * 1024


def nt(a, b):
    return lax.dot_general(a, b, (((1,), (1,)), ((), ())), preferred_element_type=F32)


def nn(a, b):
    return lax.dot_general(a, b, (((1,), (0,)), ((), ())), preferred_element_type=F32)


def tn(a, b):
    return lax.dot_general(a, b, (((0,), (0,)), ((), ())), preferred_element_type=F32)


def hi_lo(x):
    high = x.astype(BF).astype(F32)
    return [high, x - high]


def rows(parts):
    return jnp.concatenate(parts, axis=0).astype(BF)


def project(frozen, low_t, up):
    return (frozen.astype(F32) + ADAPTER_SCALE * tn(low_t, up)).astype(BF)


def scores(items, mask):
    sts = [nt(k, q) for q, k, v, g, ups, lows in items]
    dps = [nt(v, g) for q, k, v, g, ups, lows in items]
    bs = [(nt(ups[1], q), nt(ups[2], g)) for q, k, v, g, ups, lows in items]
    pbs, dss = [], []
    for st, dp in zip(sts, dps):
        st = jnp.where(mask, st * SCALE, -jnp.inf)
        e = jnp.exp(st - jnp.max(st, axis=0, keepdims=True))
        p = e * (1.0 / jnp.sum(e, axis=0, keepdims=True))
        pb = p.astype(BF)
        row_dot = jnp.sum(pb.astype(F32) * dp, axis=0, keepdims=True)
        pbs.append(pb)
        dss.append((p * (dp - row_dot) * SCALE).astype(BF))
    by_k = [nt(rows([it[5][0]] + hi_lo(b[0])), ds) for it, b, ds in zip(items, bs, dss)]
    by_v = [nt(rows(hi_lo(b[1])), pb) for b, pb in zip(bs, pbs)]
    return [
        (pb, ds, bk[:8], bk[8:16] + bk[16:24], r[:8] + r[8:])
        for pb, ds, bk, r in zip(pbs, dss, by_k, by_v)
    ]


def rest(items, found):
    bqs = [nt(it[4][0], it[1]) for it in items]
    by_q = [nn(rows([it[5][1]] + hi_lo(b)), f[1]) for it, b, f in zip(items, bqs, found)]
    av = [nn(it[5][2].astype(BF), f[0]) for it, f in zip(items, found)]
    out = []
    for it, f, bq, a in zip(items, found, by_q, av):
        q, k, v, g = it[:4]
        us = [nn(rows(hi_lo(f[2])), k), nn(rows(hi_lo(bq[:8])), q), nn(rows(hi_lo(a)), g)]
        out.append(([u[:8] + u[8:] for u in us], bq[8:16] + bq[16:24]))
    return out


def heads(items, mask):
    found = scores(items, mask)
    return [
        (grads, [rank_q, f[3], f[4]]) for f, (grads, rank_q) in zip(found, rest(items, found))
    ]


def causal(keys, queries, offset):
    return lax.broadcasted_iota(jnp.int32, (keys, queries), 0) <= offset + lax.broadcasted_iota(
        jnp.int32, (keys, queries), 1
    )


def project_kernel(frozen, low_t, up, out):
    for j in range(3):
        for start in range(0, out.shape[2], 512):
            cols = slice(start, start + 512)
            out[j, :, cols] = project(frozen[j, 0, :, cols], low_t[j], up[j, :, cols])


def group_kernel(first, start, projected, grad, low_t, up, up_out, rank_out):
    count = grad.shape[1]
    low = [low_t[j].astype(F32)[:, first:] for j in range(3)]
    starts = range(0, up_out.shape[1], HEAD_DIM)
    items = []
    for h in starts:
        cols = slice(start + h, start + h + HEAD_DIM)
        q, k, v = [projected[j, first:, cols] for j in range(3)]
        items.append((q, k, v, grad[0, first:, cols], [up[j, :, cols] for j in range(3)], low))
    parts = heads(items, causal(count - first, count - first, 0))
    for h, (grads, _) in zip(starts, parts):
        for j in range(3):
            up_out[8 * j : 8 * j + 8, h : h + HEAD_DIM] = grads[j]
    for j in range(3):
        part = sum(ranks[j] for _, ranks in parts)
        rank_out[8 * j : 8 * j + 8, :] = right(part) if first else part


def far_items(projected, near_kv, low_kv, grad, low_t, up):
    half = projected.shape[1] // 2
    half_width = up.shape[2] // 2
    far_f = [low_t[j].astype(F32)[:, :half] for j in range(3)]
    lows = [far_f[0]] + [
        jnp.concatenate([low_kv[j].astype(F32), far_f[j + 1]], axis=1) for j in range(2)
    ]
    items = []
    for h, near in enumerate(near_kv):
        start = half_width + h * HEAD_DIM
        cols = slice(start, start + HEAD_DIM)
        ups = [up[j, :, cols] for j in range(3)]
        k, v = [jnp.concatenate([near[j], projected[j + 1, :half, cols]], axis=0) for j in range(2)]
        items.append((projected[0, :half, cols], k, v, grad[0, :half, cols], ups, lows))
    return items


def near_rows(frozen_kv, low_kv, up):
    half_width = up.shape[2] // 2
    near = []
    for h in range(frozen_kv.shape[2] // HEAD_DIM):
        here = slice(h * HEAD_DIM, (h + 1) * HEAD_DIM)
        start = half_width + h * HEAD_DIM
        near.append(
            [project(frozen_kv[j, :, here], low_kv[j], up[j + 1, :, start : start + HEAD_DIM]) for j in range(2)]
        )
    return near


def left(x):
    return jnp.concatenate([x, jnp.zeros_like(x)], axis=1)


def right(x):
    return jnp.concatenate([jnp.zeros_like(x), x], axis=1)


def far_scores(
    projected, frozen_kv, low_kv, grad, low_t, up, rank_in, rank_out, cross_out, near_out, pb_out, ds_out, aq_out
):
    half = projected.shape[1] // 2
    near = near_rows(frozen_kv, low_kv, up)
    items = far_items(projected, near, low_kv, grad, low_t, up)
    found = scores(items, causal(2 * half, half, half))
    for j in (1, 2):
        part = sum(f[j + 2] for f in found)
        cross_out[8 * j - 8 : 8 * j, :] = right(part[:, :half])
        rank_out[8 * j : 8 * j + 8, :] = rank_in[8 * j : 8 * j + 8, :] + left(part[:, half:])
    rank_out[:8, :] = rank_in[:8, :]
    for h, f in enumerate(found):
        near_out[h] = near[h][0]
        pb_out[h] = f[0]
        ds_out[h] = f[1]
        aq_out[8 * h : 8 * h + 8, :] = f[2]


def far_rest(projected, low_kv, grad, low_t, up, rank_in, near, pb, ds, aq, up_out, rank_out):
    n = near.shape[0]
    items = far_items(projected, [[near[h]] * 2 for h in range(n)], low_kv, grad, low_t, up)
    parts = rest(items, [(pb[h], ds[h], aq[8 * h : 8 * h + 8, :]) for h in range(n)])
    for h, (grads, _) in enumerate(parts):
        for j in range(3):
            up_out[8 * j : 8 * j + 8, h * HEAD_DIM : (h + 1) * HEAD_DIM] = grads[j]
    rank_out[:8, :] = rank_in[:8, :] + left(sum(rank for _, rank in parts))
    rank_out[8:, :] = rank_in[8:, :]


def position():
    seq, dp = lax.axis_index("seq"), lax.axis_index("dp")
    bits = seq ^ dp
    for shift in (4, 2, 1):
        bits = bits ^ (bits >> shift)
    return bits & 1, (dp & 2) | (seq & 1)


def down_kernel(tokens, rank_in, rank_near, cross, up_plain, up_near, up_far, keep, send):
    half, quarter = position()
    first = half == 0
    ranks = rank_in[...] + rank_near[...] + jnp.concatenate(
        [jnp.zeros((RANK, rank_in.shape[1]), F32), cross[...]], axis=0
    )
    both = rows(hi_lo(ranks))
    n = ranks.shape[0]
    up_step, down_step = up_plain.shape[1] // 4, tokens.shape[2] // 8
    for c in range(4):
        d = nn(both, tokens[0, :, 2 * c * down_step : 2 * (c + 1) * down_step])
        d = ADAPTER_SCALE * (d[:n] + d[n:])
        cols = slice((c % 2) * 2 * up_step, (c % 2 + 1) * 2 * up_step)
        if c < 2:
            u = up_plain[:, cols]
        else:
            u = up_near[:, cols] + up_far[:, cols]
        u = ADAPTER_SCALE * u
        slot = quarter ^ c
        keep[slot, :, :up_step] = jnp.where(first, u[:, :up_step], u[:, up_step:])
        send[slot, :, :up_step] = jnp.where(first, u[:, up_step:], u[:, :up_step])
        keep[slot, :, up_step:] = jnp.where(first, d[:, :down_step], d[:, down_step:])
        send[slot, :, up_step:] = jnp.where(first, d[:, down_step:], d[:, :down_step])


def spread(pieces, own, down_out, up_out):
    half, quarter = position()
    half = half if own else 1 - half
    up_step, down_step = up_out.shape[2] // 8, down_out.shape[2] // 8
    for c in range(4):
        x = pieces[quarter ^ c].astype(F32)
        at = 2 * c + half
        ups = pl.ds(pl.multiple_of(at * up_step, up_step), up_step)
        downs = pl.ds(pl.multiple_of(at * down_step, down_step), down_step)
        for j in range(3):
            part = x[8 * j : 8 * j + 8]
            up_out[j, :, ups] = part[:, :up_step]
            down_out[j, :, downs] = part[:, up_step:]


def first_spread(pieces, down_out, up_out):
    spread(pieces, True, down_out, up_out)


def last_spread(pieces, down_in, up_in, down_out, up_out):
    down_out[...] = down_in[...]
    up_out[...] = up_in[...]
    spread(pieces, False, down_out, up_out)


def call(kernel, outs, *args):
    return pl.pallas_call(
        kernel,
        out_shape=outs,
        in_specs=[VMEM] * len(args),
        out_specs=jax.tree.map(lambda _: VMEM, outs),
        compiler_params=pltpu.CompilerParams(vmem_limit_bytes=LIMIT),
        cost_estimate=COST,
    )(*args)


def swap(x, bits, total):
    return lax.ppermute(x, AXES, [(i, i ^ bits) for i in range(total)])


def total_sum(keep, send, seqs, dps):
    total = seqs * dps
    partner = {1: dps | 1, 2: 3, 3: dps | 2}
    keep = keep + swap(send, 1, total)
    got = [swap(keep[s].astype(BF), partner[s], total).astype(F32) for s in (1, 2, 3)]
    own = keep[0] + got[0] + got[1] + got[2]
    bit = 2
    while bit < seqs:
        steps = [bit, 2 * bit, 3 * bit] if 2 * bit < seqs else [bit]
        bit *= len(steps) + 1
        if bit >= seqs:
            own = own.astype(BF)
        parts = [swap(own, step * dps | (step & (step - 1) == 0), total) for step in steps]
        own = own.astype(F32)
        if len(parts) == 3:
            own = (own + parts[0].astype(F32)) + (parts[1].astype(F32) + parts[2].astype(F32))
        else:
            own = own + parts[0].astype(F32)
    piece = own.astype(BF)
    mine = jnp.stack([piece] + [swap(piece, partner[s], total) for s in (1, 2, 3)])
    return mine, swap(mine, 1, total)


def on_device(tokens, frozen, grad, down_weight, up_weight):
    seqs, dps = lax.axis_size("seq"), lax.axis_size("dp")
    count, width = grad.shape[1:]
    half, half_width = count // 2, width // 2
    forward = [(i, (i + 1) % seqs) for i in range(seqs)]
    backward = [(i, (i - 1) % seqs) for i in range(seqs)]
    frozen_kv = lax.ppermute(frozen[1:, 0, half:, half_width:], "seq", forward)
    low_t = jnp.einsum("psw,gw->psg", down_weight, tokens[0], preferred_element_type=F32).astype(BF)
    low_kv = lax.ppermute(low_t[1:, :, half:], "seq", forward)
    sds = jax.ShapeDtypeStruct
    up_half, rank_side = sds((24, half_width), F32), sds((24, count), F32)
    projected = call(project_kernel, sds((3, count, width), BF), frozen, low_t, up_weight)
    up_plain, rank = call(
        functools.partial(group_kernel, 0, 0), [up_half, rank_side], projected, grad, low_t, up_weight
    )
    n = half_width // HEAD_DIM
    by_keys = sds((n, count, half), BF)
    rank, cross, *kept = call(
        far_scores,
        [
            rank_side, sds((16, count), F32), sds((n, half, HEAD_DIM), BF), by_keys, by_keys,
            sds((8 * n, count), F32),
        ],
        projected, frozen_kv, low_kv, grad, low_t, up_weight, rank,
    )
    rank, *held = lax.optimization_barrier((rank, grad, low_t, up_weight))
    cross = lax.ppermute(cross, "seq", backward)
    up_near, rank_near = call(
        functools.partial(group_kernel, half, half_width), [up_half, rank_side], projected, *held
    )
    up_far, rank = call(far_rest, [up_half, rank_side], projected, low_kv, grad, low_t, up_weight, rank, *kept)
    columns = (width + tokens.shape[2]) // 8
    piece = sds((4, 24, columns), F32)
    keep, send = call(down_kernel, [piece, piece], tokens, rank, rank_near, cross, up_plain, up_near, up_far)
    mine, other = total_sum(keep, send, seqs, dps)
    outs = [sds((3, RANK, tokens.shape[2]), F32), sds((3, RANK, width), F32)]
    return tuple(call(last_spread, outs, other, *call(first_spread, outs, mine)))


def solution(mesh):
    return jax.shard_map(
        on_device,
        mesh=mesh,
        in_specs=(P("dp", "seq", None), P(None, "dp", "seq", None), P("dp", "seq", None), P(), P()),
        out_specs=(P(), P()),
        check_vma=False,
    )
```

```python
import functools

import jax
import jax.numpy as jnp
from jax import lax
from jax.experimental import pallas as pl
from jax.experimental.pallas import tpu as pltpu
from jax.sharding import PartitionSpec as P

HEAD_DIM = 128
RANK = 8
SCALE = HEAD_DIM ** -0.5
ADAPTER_SCALE = 2.0
BF = jnp.bfloat16
F32 = jnp.float32
AXES = ("seq", "dp")
COST = pl.CostEstimate(flops=10**6, bytes_accessed=10**4, transcendentals=0)
VMEM = pl.BlockSpec(memory_space=pltpu.VMEM)
LIMIT = 48 * 1024 * 1024


def nt(a, b):
    return lax.dot_general(a, b, (((1,), (1,)), ((), ())), preferred_element_type=F32)


def nn(a, b):
    return lax.dot_general(a, b, (((1,), (0,)), ((), ())), preferred_element_type=F32)


def tn(a, b):
    return lax.dot_general(a, b, (((0,), (0,)), ((), ())), preferred_element_type=F32)


def hi_lo(x):
    high = x.astype(BF).astype(F32)
    return [high, x - high]


def rows(parts):
    return jnp.concatenate(parts, axis=0).astype(BF)


def project(frozen, low_t, up):
    return (frozen.astype(F32) + ADAPTER_SCALE * tn(low_t, up)).astype(BF)


def scores(items, mask):
    sts = [nt(k, q) for q, k, v, g, ups, lows in items]
    dps = [nt(v, g) for q, k, v, g, ups, lows in items]
    bs = [(nt(ups[1], q), nt(ups[2], g)) for q, k, v, g, ups, lows in items]
    pbs, dss = [], []
    for st, dp in zip(sts, dps):
        st = jnp.where(mask, st * SCALE, -jnp.inf)
        e = jnp.exp(st - jnp.max(st, axis=0, keepdims=True))
        p = e * (1.0 / jnp.sum(e, axis=0, keepdims=True))
        pb = p.astype(BF)
        row_dot = jnp.sum(pb.astype(F32) * dp, axis=0, keepdims=True)
        pbs.append(pb)
        dss.append((p * (dp - row_dot) * SCALE).astype(BF))
    by_k = [nt(rows([it[5][0]] + hi_lo(b[0])), ds) for it, b, ds in zip(items, bs, dss)]
    by_v = [nt(rows(hi_lo(b[1])), pb) for b, pb in zip(bs, pbs)]
    return [
        (pb, ds, bk[:8], bk[8:16] + bk[16:24], r[:8] + r[8:])
        for pb, ds, bk, r in zip(pbs, dss, by_k, by_v)
    ]


def rest(items, found):
    bqs = [nt(it[4][0], it[1]) for it in items]
    by_q = [nn(rows([it[5][1]] + hi_lo(b)), f[1]) for it, b, f in zip(items, bqs, found)]
    av = [nn(it[5][2].astype(BF), f[0]) for it, f in zip(items, found)]
    out = []
    for it, f, bq, a in zip(items, found, by_q, av):
        q, k, v, g = it[:4]
        us = [nn(rows(hi_lo(f[2])), k), nn(rows(hi_lo(bq[:8])), q), nn(rows(hi_lo(a)), g)]
        out.append(([u[:8] + u[8:] for u in us], bq[8:16] + bq[16:24]))
    return out


def heads(items, mask):
    found = scores(items, mask)
    return [
        (grads, [rank_q, f[3], f[4]]) for f, (grads, rank_q) in zip(found, rest(items, found))
    ]


def causal(keys, queries, offset):
    return lax.broadcasted_iota(jnp.int32, (keys, queries), 0) <= offset + lax.broadcasted_iota(
        jnp.int32, (keys, queries), 1
    )


def project_kernel(frozen, low_t, up, out):
    for j in range(3):
        for start in range(0, out.shape[2], 512):
            cols = slice(start, start + 512)
            out[j, :, cols] = project(frozen[j, 0, :, cols], low_t[j], up[j, :, cols])


def group_kernel(first, start, projected, grad, low_t, up, up_out, rank_out):
    count = grad.shape[1]
    low = [low_t[j].astype(F32)[:, first:] for j in range(3)]
    starts = range(0, up_out.shape[1], HEAD_DIM)
    items = []
    for h in starts:
        cols = slice(start + h, start + h + HEAD_DIM)
        q, k, v = [projected[j, first:, cols] for j in range(3)]
        items.append((q, k, v, grad[0, first:, cols], [up[j, :, cols] for j in range(3)], low))
    parts = heads(items, causal(count - first, count - first, 0))
    for h, (grads, _) in zip(starts, parts):
        for j in range(3):
            up_out[8 * j : 8 * j + 8, h : h + HEAD_DIM] = grads[j]
    for j in range(3):
        part = sum(ranks[j] for _, ranks in parts)
        rank_out[8 * j : 8 * j + 8, :] = right(part) if first else part


def left(x):
    return jnp.concatenate([x, jnp.zeros_like(x)], axis=1)


def right(x):
    return jnp.concatenate([jnp.zeros_like(x), x], axis=1)


def shifted_columns(up):
    half_width = up.shape[2] // 2
    return [slice(start, start + HEAD_DIM) for start in range(half_width, 2 * half_width, HEAD_DIM)]


def far_ready(projected, grad, up, e_out, dp_out, top_out, sum_out, bk_out, bv_out):
    half = projected.shape[1] // 2
    mask = causal(half, half, 0)
    for h, cols in enumerate(shifted_columns(up)):
        q, k, v = [projected[j, :half, cols] for j in range(3)]
        g = grad[0, :half, cols]
        st = jnp.where(mask, nt(k, q) * SCALE, -jnp.inf)
        top = jnp.max(st, axis=0, keepdims=True)
        e = jnp.exp(st - top)
        e_out[h] = e
        dp_out[h] = nt(v, g)
        top_out[h : h + 1, :] = top
        sum_out[h : h + 1, :] = jnp.sum(e, axis=0, keepdims=True)
        bk_out[h] = rows(hi_lo(nt(up[1, :, cols], q)))
        bv_out[h] = rows(hi_lo(nt(up[2, :, cols], g)))


def far_scores(
    projected, frozen_kv, low_kv, grad, up, e, dp, top, total, bk, bv,
    cross_out, near_out, pb_out, ds_out, factor_out, dot_out,
):
    half = projected.shape[1] // 2
    columns = shifted_columns(up)
    near = []
    for h, cols in enumerate(columns):
        here = slice(h * HEAD_DIM, (h + 1) * HEAD_DIM)
        near.append([project(frozen_kv[j, :, here], low_kv[j], up[j + 1, :, cols]) for j in range(2)])
    sts = [nt(near[h][0], projected[0, :half, cols]) for h, cols in enumerate(columns)]
    dps = [nt(near[h][1], grad[0, :half, cols]) for h, cols in enumerate(columns)]
    found = []
    for h, (st, dpn) in enumerate(zip(sts, dps)):
        st = st * SCALE
        far_top = top[h : h + 1, :]
        highest = jnp.maximum(far_top, jnp.max(st, axis=0, keepdims=True))
        en = jnp.exp(st - highest)
        rescale = jnp.exp(far_top - highest)
        inverse = 1.0 / (total[h : h + 1, :] * rescale + jnp.sum(en, axis=0, keepdims=True))
        factor = rescale * inverse
        p = en * inverse
        pb = p.astype(BF)
        far_pb = (e[h] * factor).astype(BF).astype(F32)
        dot = jnp.sum(pb.astype(F32) * dpn, axis=0, keepdims=True)
        dot = dot + jnp.sum(far_pb * dp[h], axis=0, keepdims=True)
        ds = (p * (dpn - dot) * SCALE).astype(BF)
        factor_out[h : h + 1, :] = factor
        dot_out[h : h + 1, :] = dot
        found.append((pb, ds))
    by_k = sum(nt(bk[h], ds) for h, (_, ds) in enumerate(found))
    by_v = sum(nt(bv[h], pb) for h, (pb, _) in enumerate(found))
    cross_out[:8, :] = right(by_k[:8] + by_k[8:])
    cross_out[8:, :] = right(by_v[:8] + by_v[8:])
    for h, (pb, ds) in enumerate(found):
        near_out[h] = near[h][0]
        pb_out[h] = pb
        ds_out[h] = ds


def far_rest(
    projected, low_kv, grad, low_t, up, e, dp, bk, bv, near, near_pb, near_ds, factor, dot, up_out, rank_out
):
    half = projected.shape[1] // 2
    far_f = [low_t[j].astype(F32)[:, :half] for j in range(3)]
    lows = [far_f[0]] + [
        jnp.concatenate([low_kv[j].astype(F32), far_f[j + 1]], axis=1) for j in range(2)
    ]
    items, found, far_ds, far_pb = [], [], [], []
    for h, cols in enumerate(shifted_columns(up)):
        p = e[h] * factor[h : h + 1, :]
        pb = p.astype(BF)
        ds = (p * (dp[h] - dot[h : h + 1, :]) * SCALE).astype(BF)
        far_pb.append(pb)
        far_ds.append(ds)
        whole_ds = jnp.concatenate([near_ds[h], ds], axis=0)
        k = jnp.concatenate([near[h], projected[1, :half, cols]], axis=0)
        items.append(
            (projected[0, :half, cols], k, None, grad[0, :half, cols], [up[j, :, cols] for j in range(3)], lows)
        )
        found.append((jnp.concatenate([near_pb[h], pb], axis=0), whole_ds, nt(lows[0].astype(BF), whole_ds)))
    by_k = sum(nt(bk[h], ds) for h, ds in enumerate(far_ds))
    by_v = sum(nt(bv[h], pb) for h, pb in enumerate(far_pb))
    parts = rest(items, found)
    for h, (grads, _) in enumerate(parts):
        for j in range(3):
            up_out[8 * j : 8 * j + 8, h * HEAD_DIM : (h + 1) * HEAD_DIM] = grads[j]
    rank_out[:8, :] = left(sum(rank for _, rank in parts))
    rank_out[8:16, :] = left(by_k[:8] + by_k[8:])
    rank_out[16:, :] = left(by_v[:8] + by_v[8:])


def position():
    seq, dp = lax.axis_index("seq"), lax.axis_index("dp")
    bits = seq ^ dp
    for shift in (4, 2, 1):
        bits = bits ^ (bits >> shift)
    return bits & 1, (dp & 2) | (seq & 1)


def down_kernel(tokens, rank_plain, rank_near, rank_far, cross, up_plain, up_near, up_far, keep, send):
    half, quarter = position()
    first = half == 0
    ranks = rank_plain[...] + rank_near[...] + rank_far[...]
    ranks = ranks + jnp.concatenate([jnp.zeros((RANK, ranks.shape[1]), F32), cross[...]], axis=0)
    both = rows(hi_lo(ranks))
    n = ranks.shape[0]
    up_step, down_step = up_plain.shape[1] // 4, tokens.shape[2] // 8
    for c in range(4):
        d = nn(both, tokens[0, :, 2 * c * down_step : 2 * (c + 1) * down_step])
        d = ADAPTER_SCALE * (d[:n] + d[n:])
        cols = slice((c % 2) * 2 * up_step, (c % 2 + 1) * 2 * up_step)
        if c < 2:
            u = up_plain[:, cols]
        else:
            u = up_near[:, cols] + up_far[:, cols]
        u = ADAPTER_SCALE * u
        slot = quarter ^ c
        keep[slot, :, :up_step] = jnp.where(first, u[:, :up_step], u[:, up_step:])
        send[slot, :, :up_step] = jnp.where(first, u[:, up_step:], u[:, :up_step])
        keep[slot, :, up_step:] = jnp.where(first, d[:, :down_step], d[:, down_step:])
        send[slot, :, up_step:] = jnp.where(first, d[:, down_step:], d[:, :down_step])


def spread(pieces, own, down_out, up_out):
    half, quarter = position()
    half = half if own else 1 - half
    up_step, down_step = up_out.shape[2] // 8, down_out.shape[2] // 8
    for c in range(4):
        x = pieces[quarter ^ c].astype(F32)
        at = 2 * c + half
        ups = pl.ds(pl.multiple_of(at * up_step, up_step), up_step)
        downs = pl.ds(pl.multiple_of(at * down_step, down_step), down_step)
        for j in range(3):
            part = x[8 * j : 8 * j + 8]
            up_out[j, :, ups] = part[:, :up_step]
            down_out[j, :, downs] = part[:, up_step:]


def first_spread(pieces, down_out, up_out):
    spread(pieces, True, down_out, up_out)


def last_spread(pieces, down_in, up_in, down_out, up_out):
    down_out[...] = down_in[...]
    up_out[...] = up_in[...]
    spread(pieces, False, down_out, up_out)


def call(kernel, outs, *args):
    return pl.pallas_call(
        kernel,
        out_shape=outs,
        in_specs=[VMEM] * len(args),
        out_specs=jax.tree.map(lambda _: VMEM, outs),
        compiler_params=pltpu.CompilerParams(vmem_limit_bytes=LIMIT),
        cost_estimate=COST,
    )(*args)


def swap(x, bits, total):
    return lax.ppermute(x, AXES, [(i, i ^ bits) for i in range(total)])


def total_sum(keep, send, seqs, dps):
    total = seqs * dps
    partner = {1: dps | 1, 2: 3, 3: dps | 2}
    keep = keep + swap(send, 1, total)
    got = [swap(keep[s].astype(BF), partner[s], total).astype(F32) for s in (1, 2, 3)]
    own = keep[0] + got[0] + got[1] + got[2]
    bit = 2
    while bit < seqs:
        steps = [bit, 2 * bit, 3 * bit] if 2 * bit < seqs else [bit]
        bit *= len(steps) + 1
        if bit >= seqs:
            own = own.astype(BF)
        parts = [swap(own, step * dps | (step & (step - 1) == 0), total) for step in steps]
        own = own.astype(F32)
        if len(parts) == 3:
            own = (own + parts[0].astype(F32)) + (parts[2].astype(F32) + parts[1].astype(F32))
        else:
            own = own + parts[0].astype(F32)
    piece = own.astype(BF)
    mine = jnp.stack([piece] + [swap(piece, partner[s], total) for s in (1, 2, 3)])
    return mine, swap(mine, 1, total)


def on_device(tokens, frozen, grad, down_weight, up_weight):
    seqs, dps = lax.axis_size("seq"), lax.axis_size("dp")
    count, width = grad.shape[1:]
    half, half_width = count // 2, width // 2
    forward = [(i, (i + 1) % seqs) for i in range(seqs)]
    backward = [(i, (i - 1) % seqs) for i in range(seqs)]
    frozen_kv = lax.ppermute(frozen[1:, 0, half:, half_width:], "seq", forward)
    low_t = jnp.einsum("psw,gw->psg", down_weight, tokens[0], preferred_element_type=F32).astype(BF)
    low_kv = lax.ppermute(low_t[1:, :, half:], "seq", forward)
    sds = jax.ShapeDtypeStruct
    up_half, rank_side = sds((24, half_width), F32), sds((24, count), F32)
    projected = call(project_kernel, sds((3, count, width), BF), frozen, low_t, up_weight)
    up_plain, rank_plain = call(
        functools.partial(group_kernel, 0, 0), [up_half, rank_side], projected, grad, low_t, up_weight
    )
    n = half_width // HEAD_DIM
    square, line, pairs = sds((n, half, half), F32), sds((n, half), F32), sds((n, 2 * RANK, half), BF)
    e, dp, top, total, bk, bv = call(
        far_ready, [square, square, line, line, pairs, pairs], projected, grad, up_weight
    )
    bk, rank_plain = lax.optimization_barrier((bk, rank_plain))
    squares = sds((n, half, half), BF)
    cross, near, pb, ds, factor, dot = call(
        far_scores,
        [sds((2 * RANK, count), F32), sds((n, half, HEAD_DIM), BF), squares, squares, line, line],
        projected, frozen_kv, low_kv, grad, up_weight, e, dp, top, total, bk, bv,
    )
    factor, *held = lax.optimization_barrier((factor, grad, low_t, up_weight))
    cross = lax.ppermute(cross, "seq", backward)
    up_near, rank_near = call(
        functools.partial(group_kernel, half, half_width), [up_half, rank_side], projected, *held
    )
    up_far, rank_far = call(
        far_rest, [up_half, rank_side],
        projected, low_kv, grad, low_t, up_weight, e, dp, bk, bv, near, pb, ds, factor, dot,
    )
    columns = (width + tokens.shape[2]) // 8
    piece = sds((4, 24, columns), F32)
    keep, send = call(down_kernel, [piece, piece], tokens, rank_plain, rank_near, rank_far, cross, up_plain, up_near, up_far)
    mine, other = total_sum(keep, send, seqs, dps)
    outs = [sds((3, RANK, tokens.shape[2]), F32), sds((3, RANK, width), F32)]
    return tuple(call(last_spread, outs, other, *call(first_spread, outs, mine)))


def solution(mesh):
    return jax.shard_map(
        on_device,
        mesh=mesh,
        in_specs=(P("dp", "seq", None), P(None, "dp", "seq", None), P("dp", "seq", None), P(), P()),
        out_specs=(P(), P()),
        check_vma=False,
    )
```

```python
import functools

import jax
import jax.numpy as jnp
from jax import lax
from jax.experimental import pallas as pl
from jax.experimental.pallas import tpu as pltpu
from jax.sharding import PartitionSpec as P

HEAD_DIM = 128
RANK = 8
SCALE = HEAD_DIM ** -0.5
ADAPTER_SCALE = 2.0
BF = jnp.bfloat16
F32 = jnp.float32
AXES = ("seq", "dp")
COST = pl.CostEstimate(flops=10**6, bytes_accessed=10**4, transcendentals=0)
VMEM = pl.BlockSpec(memory_space=pltpu.VMEM)
LIMIT = 48 * 1024 * 1024


def nt(a, b):
    return lax.dot_general(a, b, (((1,), (1,)), ((), ())), preferred_element_type=F32)


def nn(a, b):
    return lax.dot_general(a, b, (((1,), (0,)), ((), ())), preferred_element_type=F32)


def tn(a, b):
    return lax.dot_general(a, b, (((0,), (0,)), ((), ())), preferred_element_type=F32)


def hi_lo(x):
    high = x.astype(BF).astype(F32)
    return [high, x - high]


def rows(parts):
    return jnp.concatenate(parts, axis=0).astype(BF)


def project(frozen, low_t, up):
    return (frozen.astype(F32) + ADAPTER_SCALE * tn(low_t, up)).astype(BF)


def scores(items, mask):
    sts = [nt(k, q) for q, k, v, g, ups, lows in items]
    dps = [nt(v, g) for q, k, v, g, ups, lows in items]
    bs = [(nt(ups[1], q), nt(ups[2], g)) for q, k, v, g, ups, lows in items]
    pbs, dss = [], []
    for st, dp in zip(sts, dps):
        st = jnp.where(mask, st * SCALE, -jnp.inf)
        e = jnp.exp(st - jnp.max(st, axis=0, keepdims=True))
        p = e * (1.0 / jnp.sum(e, axis=0, keepdims=True))
        pb = p.astype(BF)
        row_dot = jnp.sum(pb.astype(F32) * dp, axis=0, keepdims=True)
        pbs.append(pb)
        dss.append((p * (dp - row_dot) * SCALE).astype(BF))
    by_k = [nt(rows([it[5][0]] + hi_lo(b[0])), ds) for it, b, ds in zip(items, bs, dss)]
    by_v = [nt(rows(hi_lo(b[1])), pb) for b, pb in zip(bs, pbs)]
    return [
        (pb, ds, bk[:8], bk[8:16] + bk[16:24], r[:8] + r[8:])
        for pb, ds, bk, r in zip(pbs, dss, by_k, by_v)
    ]


def rest(items, found):
    bqs = [nt(it[4][0], it[1]) for it in items]
    by_q = [nn(rows([it[5][1]] + hi_lo(b)), f[1]) for it, b, f in zip(items, bqs, found)]
    av = [nn(it[5][2].astype(BF), f[0]) for it, f in zip(items, found)]
    out = []
    for it, f, bq, a in zip(items, found, by_q, av):
        q, k, v, g = it[:4]
        us = [nn(rows(hi_lo(f[2])), k), nn(rows(hi_lo(bq[:8])), q), nn(rows(hi_lo(a)), g)]
        out.append(([u[:8] + u[8:] for u in us], bq[8:16] + bq[16:24]))
    return out


def heads(items, mask):
    found = scores(items, mask)
    return [
        (grads, [rank_q, f[3], f[4]]) for f, (grads, rank_q) in zip(found, rest(items, found))
    ]


def causal(keys, queries, offset):
    return lax.broadcasted_iota(jnp.int32, (keys, queries), 0) <= offset + lax.broadcasted_iota(
        jnp.int32, (keys, queries), 1
    )


def project_kernel(frozen, low_t, up, out):
    for j in range(3):
        for start in range(0, out.shape[2], 512):
            cols = slice(start, start + 512)
            out[j, :, cols] = project(frozen[j, 0, :, cols], low_t[j], up[j, :, cols])


def group_kernel(first, start, projected, grad, low_t, up, up_out, rank_out):
    count = grad.shape[1]
    low = [low_t[j].astype(F32)[:, first:] for j in range(3)]
    starts = range(0, up_out.shape[1], HEAD_DIM)
    items = []
    for h in starts:
        cols = slice(start + h, start + h + HEAD_DIM)
        q, k, v = [projected[j, first:, cols] for j in range(3)]
        items.append((q, k, v, grad[0, first:, cols], [up[j, :, cols] for j in range(3)], low))
    parts = heads(items, causal(count - first, count - first, 0))
    for h, (grads, _) in zip(starts, parts):
        for j in range(3):
            up_out[8 * j : 8 * j + 8, h : h + HEAD_DIM] = grads[j]
    for j in range(3):
        part = sum(ranks[j] for _, ranks in parts)
        rank_out[8 * j : 8 * j + 8, :] = right(part) if first else part


def left(x):
    return jnp.concatenate([x, jnp.zeros_like(x)], axis=1)


def right(x):
    return jnp.concatenate([jnp.zeros_like(x), x], axis=1)


def shifted_columns(up):
    half_width = up.shape[2] // 2
    return [slice(start, start + HEAD_DIM) for start in range(half_width, 2 * half_width, HEAD_DIM)]


def far_ready(projected, grad, up, e_out, dp_out, top_out, sum_out, bk_out, bv_out):
    half = projected.shape[1] // 2
    mask = causal(half, half, 0)
    for h, cols in enumerate(shifted_columns(up)):
        q, k, v = [projected[j, :half, cols] for j in range(3)]
        g = grad[0, :half, cols]
        st = jnp.where(mask, nt(k, q) * SCALE, -jnp.inf)
        top = jnp.max(st, axis=0, keepdims=True)
        e = jnp.exp(st - top)
        e_out[h] = e
        dp_out[h] = nt(v, g)
        top_out[h : h + 1, :] = top
        sum_out[h : h + 1, :] = jnp.sum(e, axis=0, keepdims=True)
        bk_out[h] = rows(hi_lo(nt(up[1, :, cols], q)))
        bv_out[h] = rows(hi_lo(nt(up[2, :, cols], g)))


def far_scores(
    projected, frozen_kv, low_kv, grad, up, e, dp, top, total, bk, bv,
    cross_out, near_out, pb_out, ds_out, factor_out, dot_out,
):
    half = projected.shape[1] // 2
    columns = shifted_columns(up)
    wide = [project(frozen_kv[j], low_kv[j], up[j + 1, :, columns[0].start :]) for j in range(2)]
    near = [[x[:, h * HEAD_DIM : (h + 1) * HEAD_DIM] for x in wide] for h in range(len(columns))]
    sts = [nt(near[h][0], projected[0, :half, cols]) for h, cols in enumerate(columns)]
    dps = [nt(near[h][1], grad[0, :half, cols]) for h, cols in enumerate(columns)]
    found = []
    for h, (st, dpn) in enumerate(zip(sts, dps)):
        st = st * SCALE
        far_top = top[h : h + 1, :]
        highest = jnp.maximum(far_top, jnp.max(st, axis=0, keepdims=True))
        en = jnp.exp(st - highest)
        rescale = jnp.exp(far_top - highest)
        inverse = 1.0 / (total[h : h + 1, :] * rescale + jnp.sum(en, axis=0, keepdims=True))
        factor = rescale * inverse
        p = en * inverse
        pb = p.astype(BF)
        far_pb = (e[h] * factor).astype(BF).astype(F32)
        dot = jnp.sum(pb.astype(F32) * dpn, axis=0, keepdims=True)
        dot = dot + jnp.sum(far_pb * dp[h], axis=0, keepdims=True)
        ds = (p * (dpn - dot) * SCALE).astype(BF)
        factor_out[h : h + 1, :] = factor
        dot_out[h : h + 1, :] = dot
        found.append((pb, ds))
    by_k = sum(nt(bk[h], ds) for h, (_, ds) in enumerate(found))
    by_v = sum(nt(bv[h], pb) for h, (pb, _) in enumerate(found))
    cross_out[:8, :] = right(by_k[:8] + by_k[8:])
    cross_out[8:, :] = right(by_v[:8] + by_v[8:])
    for h, (pb, ds) in enumerate(found):
        near_out[h] = near[h][0]
        pb_out[h] = pb
        ds_out[h] = ds


def far_rest(
    projected, low_kv, grad, low_t, up, e, dp, bk, bv, near, near_pb, near_ds, factor, dot, up_out, rank_out
):
    half = projected.shape[1] // 2
    far_f = [low_t[j].astype(F32)[:, :half] for j in range(3)]
    lows = [far_f[0]] + [
        jnp.concatenate([low_kv[j].astype(F32), far_f[j + 1]], axis=1) for j in range(2)
    ]
    items, found, far_ds, far_pb = [], [], [], []
    for h, cols in enumerate(shifted_columns(up)):
        p = e[h] * factor[h : h + 1, :]
        pb = p.astype(BF)
        ds = (p * (dp[h] - dot[h : h + 1, :]) * SCALE).astype(BF)
        far_pb.append(pb)
        far_ds.append(ds)
        whole_ds = jnp.concatenate([near_ds[h], ds], axis=0)
        k = jnp.concatenate([near[h], projected[1, :half, cols]], axis=0)
        items.append(
            (projected[0, :half, cols], k, None, grad[0, :half, cols], [up[j, :, cols] for j in range(3)], lows)
        )
        found.append((jnp.concatenate([near_pb[h], pb], axis=0), whole_ds, nt(lows[0].astype(BF), whole_ds)))
    by_k = sum(nt(bk[h], ds) for h, ds in enumerate(far_ds))
    by_v = sum(nt(bv[h], pb) for h, pb in enumerate(far_pb))
    parts = rest(items, found)
    for h, (grads, _) in enumerate(parts):
        for j in range(3):
            up_out[8 * j : 8 * j + 8, h * HEAD_DIM : (h + 1) * HEAD_DIM] = grads[j]
    rank_out[:8, :] = left(sum(rank for _, rank in parts))
    rank_out[8:16, :] = left(by_k[:8] + by_k[8:])
    rank_out[16:, :] = left(by_v[:8] + by_v[8:])


def position():
    seq, dp = lax.axis_index("seq"), lax.axis_index("dp")
    bits = seq ^ dp
    for shift in (4, 2, 1):
        bits = bits ^ (bits >> shift)
    return bits & 1, (dp & 2) | (seq & 1)


def down_kernel(tokens, rank_plain, rank_near, rank_far, cross, up_plain, up_near, up_far, keep, send):
    half, quarter = position()
    first = half == 0
    ranks = rank_plain[...] + rank_near[...] + rank_far[...]
    ranks = ranks + jnp.concatenate([jnp.zeros((RANK, ranks.shape[1]), F32), cross[...]], axis=0)
    both = rows(hi_lo(ranks))
    n = ranks.shape[0]
    up_step, down_step = up_plain.shape[1] // 4, tokens.shape[2] // 8
    for c in range(4):
        d = nn(both, tokens[0, :, 2 * c * down_step : 2 * (c + 1) * down_step])
        d = ADAPTER_SCALE * (d[:n] + d[n:])
        cols = slice((c % 2) * 2 * up_step, (c % 2 + 1) * 2 * up_step)
        if c < 2:
            u = up_plain[:, cols]
        else:
            u = up_near[:, cols] + up_far[:, cols]
        u = ADAPTER_SCALE * u
        slot = quarter ^ c
        keep[slot, :, :up_step] = jnp.where(first, u[:, :up_step], u[:, up_step:])
        send[slot, :, :up_step] = jnp.where(first, u[:, up_step:], u[:, :up_step])
        keep[slot, :, up_step:] = jnp.where(first, d[:, :down_step], d[:, down_step:])
        send[slot, :, up_step:] = jnp.where(first, d[:, down_step:], d[:, :down_step])


def spread(pieces, own, down_out, up_out):
    half, quarter = position()
    half = half if own else 1 - half
    up_step, down_step = up_out.shape[2] // 8, down_out.shape[2] // 8
    for c in range(4):
        x = pieces[quarter ^ c].astype(F32)
        at = 2 * c + half
        ups = pl.ds(pl.multiple_of(at * up_step, up_step), up_step)
        downs = pl.ds(pl.multiple_of(at * down_step, down_step), down_step)
        for j in range(3):
            part = x[8 * j : 8 * j + 8]
            up_out[j, :, ups] = part[:, :up_step]
            down_out[j, :, downs] = part[:, up_step:]


def first_spread(pieces, down_out, up_out):
    spread(pieces, True, down_out, up_out)


def last_spread(pieces, down_in, up_in, down_out, up_out):
    down_out[...] = down_in[...]
    up_out[...] = up_in[...]
    spread(pieces, False, down_out, up_out)


def call(kernel, outs, *args):
    return pl.pallas_call(
        kernel,
        out_shape=outs,
        in_specs=[VMEM] * len(args),
        out_specs=jax.tree.map(lambda _: VMEM, outs),
        compiler_params=pltpu.CompilerParams(vmem_limit_bytes=LIMIT),
        cost_estimate=COST,
    )(*args)


def swap(x, bits, total):
    return lax.ppermute(x, AXES, [(i, i ^ bits) for i in range(total)])


def total_sum(keep, send, seqs, dps):
    total = seqs * dps
    partner = {1: dps | 1, 2: 3, 3: dps | 2}
    keep = keep + swap(send, 1, total)
    got = [swap(keep[s].astype(BF), partner[s], total).astype(F32) for s in (1, 2, 3)]
    own = keep[0] + got[2] + got[0] + got[1]
    bit = 2
    while bit < seqs:
        steps = [bit, 2 * bit, 3 * bit] if 2 * bit < seqs else [bit]
        bit *= len(steps) + 1
        if bit >= seqs:
            own = own.astype(BF)
        parts = [swap(own, step * dps | (step & (step - 1) == 0), total) for step in steps]
        own = own.astype(F32)
        if len(parts) == 3:
            own = (own + parts[0].astype(F32)) + (parts[2].astype(F32) + parts[1].astype(F32))
        else:
            own = own + parts[0].astype(F32)
    piece = own.astype(BF)
    mine = jnp.stack([piece] + [swap(piece, partner[s], total) for s in (1, 2, 3)])
    return mine, swap(mine, 1, total)


def on_device(tokens, frozen, grad, down_weight, up_weight):
    seqs, dps = lax.axis_size("seq"), lax.axis_size("dp")
    count, width = grad.shape[1:]
    half, half_width = count // 2, width // 2
    forward = [(i, (i + 1) % seqs) for i in range(seqs)]
    backward = [(i, (i - 1) % seqs) for i in range(seqs)]
    frozen_kv = lax.ppermute(frozen[1:, 0, half:, half_width:], "seq", forward)
    low_t = jnp.einsum("psw,gw->psg", down_weight, tokens[0], preferred_element_type=F32).astype(BF)
    low_kv = lax.ppermute(low_t[1:, :, half:], "seq", forward)
    sds = jax.ShapeDtypeStruct
    up_half, rank_side = sds((24, half_width), F32), sds((24, count), F32)
    projected = call(project_kernel, sds((3, count, width), BF), frozen, low_t, up_weight)
    up_plain, rank_plain = call(
        functools.partial(group_kernel, 0, 0), [up_half, rank_side], projected, grad, low_t, up_weight
    )
    n = half_width // HEAD_DIM
    square, line, pairs = sds((n, half, half), F32), sds((n, half), F32), sds((n, 2 * RANK, half), BF)
    e, dp, top, total, bk, bv = call(
        far_ready, [square, square, line, line, pairs, pairs], projected, grad, up_weight
    )
    up_near, rank_near = call(
        functools.partial(group_kernel, half, half_width), [up_half, rank_side], projected, grad, low_t, up_weight
    )
    bk, rank_plain, rank_near = lax.optimization_barrier((bk, rank_plain, rank_near))
    squares = sds((n, half, half), BF)
    cross, near, pb, ds, factor, dot = call(
        far_scores,
        [sds((2 * RANK, count), F32), sds((n, half, HEAD_DIM), BF), squares, squares, line, line],
        projected, frozen_kv, low_kv, grad, up_weight, e, dp, top, total, bk, bv,
    )
    cross = lax.ppermute(cross, "seq", backward)
    up_far, rank_far = call(
        far_rest, [up_half, rank_side],
        projected, low_kv, grad, low_t, up_weight, e, dp, bk, bv, near, pb, ds, factor, dot,
    )
    columns = (width + tokens.shape[2]) // 8
    piece = sds((4, 24, columns), F32)
    keep, send = call(down_kernel, [piece, piece], tokens, rank_plain, rank_near, rank_far, cross, up_plain, up_near, up_far)
    mine, other = total_sum(keep, send, seqs, dps)
    outs = [sds((3, RANK, tokens.shape[2]), F32), sds((3, RANK, width), F32)]
    return tuple(call(last_spread, outs, other, *call(first_spread, outs, mine)))


def solution(mesh):
    return jax.shard_map(
        on_device,
        mesh=mesh,
        in_specs=(P("dp", "seq", None), P(None, "dp", "seq", None), P("dp", "seq", None), P(), P()),
        out_specs=(P(), P()),
        check_vma=False,
    )
```

```python
import functools

import jax
import jax.numpy as jnp
from jax import lax
from jax.experimental import pallas as pl
from jax.experimental.pallas import tpu as pltpu
from jax.sharding import PartitionSpec as P

HEAD_DIM = 128
RANK = 8
SCALE = HEAD_DIM ** -0.5
ADAPTER_SCALE = 2.0
BF = jnp.bfloat16
F32 = jnp.float32
AXES = ("seq", "dp")
COST = pl.CostEstimate(flops=10**6, bytes_accessed=10**4, transcendentals=0)
VMEM = pl.BlockSpec(memory_space=pltpu.VMEM)
LIMIT = 48 * 1024 * 1024


def nt(a, b):
    return lax.dot_general(a, b, (((1,), (1,)), ((), ())), preferred_element_type=F32)


def nn(a, b):
    return lax.dot_general(a, b, (((1,), (0,)), ((), ())), preferred_element_type=F32)


def tn(a, b):
    return lax.dot_general(a, b, (((0,), (0,)), ((), ())), preferred_element_type=F32)


def hi_lo(x):
    high = x.astype(BF).astype(F32)
    return [high, x - high]


def rows(parts):
    return jnp.concatenate(parts, axis=0).astype(BF)


def project(frozen, low_t, up):
    return (frozen.astype(F32) + ADAPTER_SCALE * tn(low_t, up)).astype(BF)


def scores(items, mask):
    sts = [nt(k, q) for q, k, v, g, ups, lows in items]
    dps = [nt(v, g) for q, k, v, g, ups, lows in items]
    bs = [(nt(ups[1], q), nt(ups[2], g)) for q, k, v, g, ups, lows in items]
    pbs, dss = [], []
    for st, dp in zip(sts, dps):
        st = jnp.where(mask, st * SCALE, -jnp.inf)
        e = jnp.exp(st - jnp.max(st, axis=0, keepdims=True))
        p = e * (1.0 / jnp.sum(e, axis=0, keepdims=True))
        pb = p.astype(BF)
        row_dot = jnp.sum(pb.astype(F32) * dp, axis=0, keepdims=True)
        pbs.append(pb)
        dss.append((p * (dp - row_dot) * SCALE).astype(BF))
    by_k = [nt(rows([it[5][0]] + hi_lo(b[0])), ds) for it, b, ds in zip(items, bs, dss)]
    by_v = [nt(rows(hi_lo(b[1])), pb) for b, pb in zip(bs, pbs)]
    return [
        (pb, ds, bk[:8], bk[8:16] + bk[16:24], r[:8] + r[8:])
        for pb, ds, bk, r in zip(pbs, dss, by_k, by_v)
    ]


def rest(items, found):
    bqs = [nt(it[4][0], it[1]) for it in items]
    by_q = [nn(rows([it[5][1]] + hi_lo(b)), f[1]) for it, b, f in zip(items, bqs, found)]
    av = [nn(it[5][2].astype(BF), f[0]) for it, f in zip(items, found)]
    out = []
    for it, f, bq, a in zip(items, found, by_q, av):
        q, k, v, g = it[:4]
        us = [nn(rows(hi_lo(f[2])), k), nn(rows(hi_lo(bq[:8])), q), nn(rows(hi_lo(a)), g)]
        out.append(([u[:8] + u[8:] for u in us], bq[8:16] + bq[16:24]))
    return out


def heads(items, mask):
    found = scores(items, mask)
    return [
        (grads, [rank_q, f[3], f[4]]) for f, (grads, rank_q) in zip(found, rest(items, found))
    ]


def causal(keys, queries, offset):
    return lax.broadcasted_iota(jnp.int32, (keys, queries), 0) <= offset + lax.broadcasted_iota(
        jnp.int32, (keys, queries), 1
    )


def project_kernel(frozen, low_t, up, out):
    for j in range(3):
        for start in range(0, out.shape[2], 512):
            cols = slice(start, start + 512)
            out[j, :, cols] = project(frozen[j, 0, :, cols], low_t[j], up[j, :, cols])


def group_kernel(first, start, projected, grad, low_t, up, up_out, rank_out):
    count = grad.shape[1]
    low = [low_t[j].astype(F32)[:, first:] for j in range(3)]
    starts = range(0, up_out.shape[1], HEAD_DIM)
    items = []
    for h in starts:
        cols = slice(start + h, start + h + HEAD_DIM)
        q, k, v = [projected[j, first:, cols] for j in range(3)]
        items.append((q, k, v, grad[0, first:, cols], [up[j, :, cols] for j in range(3)], low))
    parts = heads(items, causal(count - first, count - first, 0))
    for h, (grads, _) in zip(starts, parts):
        for j in range(3):
            up_out[8 * j : 8 * j + 8, h : h + HEAD_DIM] = grads[j]
    for j in range(3):
        part = sum(ranks[j] for _, ranks in parts)
        rank_out[8 * j : 8 * j + 8, :] = right(part) if first else part


def left(x):
    return jnp.concatenate([x, jnp.zeros_like(x)], axis=1)


def right(x):
    return jnp.concatenate([jnp.zeros_like(x), x], axis=1)


def shifted_columns(up):
    half_width = up.shape[2] // 2
    return [slice(start, start + HEAD_DIM) for start in range(half_width, 2 * half_width, HEAD_DIM)]


def far_ready(projected, grad, up, e_out, dp_out, top_out, sum_out, bk_out, bv_out):
    half = projected.shape[1] // 2
    mask = causal(half, half, 0)
    for h, cols in enumerate(shifted_columns(up)):
        q, k, v = [projected[j, :half, cols] for j in range(3)]
        g = grad[0, :half, cols]
        st = jnp.where(mask, nt(k, q) * SCALE, -jnp.inf)
        top = jnp.max(st, axis=0, keepdims=True)
        e = jnp.exp(st - top)
        e_out[h] = e
        dp_out[h] = nt(v, g)
        top_out[h : h + 1, :] = top
        sum_out[h : h + 1, :] = jnp.sum(e, axis=0, keepdims=True)
        bk_out[h] = rows(hi_lo(nt(up[1, :, cols], q)))
        bv_out[h] = rows(hi_lo(nt(up[2, :, cols], g)))


def far_scores(
    projected, frozen_kv, low_kv, grad, up, e, dp, top, total, bk, bv,
    cross_out, near_out, pb_out, ds_out, factor_out, dot_out,
):
    half = projected.shape[1] // 2
    columns = shifted_columns(up)
    wide = [project(frozen_kv[j], low_kv[j], up[j + 1, :, columns[0].start :]) for j in range(2)]
    near = [[x[:, h * HEAD_DIM : (h + 1) * HEAD_DIM] for x in wide] for h in range(len(columns))]
    sts = [nt(near[h][0], projected[0, :half, cols]) for h, cols in enumerate(columns)]
    dps = [nt(near[h][1], grad[0, :half, cols]) for h, cols in enumerate(columns)]
    found = []
    for h, (st, dpn) in enumerate(zip(sts, dps)):
        st = st * SCALE
        far_top = top[h : h + 1, :]
        highest = jnp.maximum(far_top, jnp.max(st, axis=0, keepdims=True))
        en = jnp.exp(st - highest)
        rescale = jnp.exp(far_top - highest)
        inverse = 1.0 / (total[h : h + 1, :] * rescale + jnp.sum(en, axis=0, keepdims=True))
        factor = rescale * inverse
        p = en * inverse
        pb = p.astype(BF)
        far_pb = (e[h] * factor).astype(BF).astype(F32)
        dot = jnp.sum(pb.astype(F32) * dpn, axis=0, keepdims=True)
        dot = dot + jnp.sum(far_pb * dp[h], axis=0, keepdims=True)
        ds = (p * (dpn - dot) * SCALE).astype(BF)
        factor_out[h : h + 1, :] = factor
        dot_out[h : h + 1, :] = dot
        found.append((pb, ds))
    by_k = sum(nt(bk[h], ds) for h, (_, ds) in enumerate(found))
    by_v = sum(nt(bv[h], pb) for h, (pb, _) in enumerate(found))
    cross_out[:8, :] = right(by_k[:8] + by_k[8:])
    cross_out[8:, :] = right(by_v[:8] + by_v[8:])
    for h, (pb, ds) in enumerate(found):
        near_out[h] = near[h][0]
        pb_out[h] = pb
        ds_out[h] = ds


def far_rest(
    projected, low_kv, grad, low_t, up, e, dp, bk, bv, near, near_pb, near_ds, factor, dot, up_out, rank_out
):
    half = projected.shape[1] // 2
    far_f = [low_t[j].astype(F32)[:, :half] for j in range(3)]
    lows = [far_f[0]] + [
        jnp.concatenate([low_kv[j].astype(F32), far_f[j + 1]], axis=1) for j in range(2)
    ]
    items, found, far_ds, far_pb = [], [], [], []
    for h, cols in enumerate(shifted_columns(up)):
        p = e[h] * factor[h : h + 1, :]
        pb = p.astype(BF)
        ds = (p * (dp[h] - dot[h : h + 1, :]) * SCALE).astype(BF)
        far_pb.append(pb)
        far_ds.append(ds)
        whole_ds = jnp.concatenate([near_ds[h], ds], axis=0)
        k = jnp.concatenate([near[h], projected[1, :half, cols]], axis=0)
        items.append(
            (projected[0, :half, cols], k, None, grad[0, :half, cols], [up[j, :, cols] for j in range(3)], lows)
        )
        found.append((jnp.concatenate([near_pb[h], pb], axis=0), whole_ds, nt(lows[0].astype(BF), whole_ds)))
    by_k = sum(nt(bk[h], ds) for h, ds in enumerate(far_ds))
    by_v = sum(nt(bv[h], pb) for h, pb in enumerate(far_pb))
    parts = rest(items, found)
    for h, (grads, _) in enumerate(parts):
        for j in range(3):
            up_out[8 * j : 8 * j + 8, h * HEAD_DIM : (h + 1) * HEAD_DIM] = grads[j]
    rank_out[:8, :] = left(sum(rank for _, rank in parts))
    rank_out[8:16, :] = left(by_k[:8] + by_k[8:])
    rank_out[16:, :] = left(by_v[:8] + by_v[8:])


def position():
    seq, dp = lax.axis_index("seq"), lax.axis_index("dp")
    return (seq ^ dp) & 1, (dp & 2) | (seq & 1)


def down_kernel(tokens, rank_plain, rank_near, rank_far, cross, up_plain, up_near, up_far, keep, send):
    half, quarter = position()
    first = half == 0
    ranks = rank_plain[...] + rank_near[...] + rank_far[...]
    ranks = ranks + jnp.concatenate([jnp.zeros((RANK, ranks.shape[1]), F32), cross[...]], axis=0)
    both = rows(hi_lo(ranks))
    n = ranks.shape[0]
    up_step, down_step = up_plain.shape[1] // 4, tokens.shape[2] // 8
    for c in range(4):
        d = nn(both, tokens[0, :, 2 * c * down_step : 2 * (c + 1) * down_step])
        d = ADAPTER_SCALE * (d[:n] + d[n:])
        cols = slice((c % 2) * 2 * up_step, (c % 2 + 1) * 2 * up_step)
        if c < 2:
            u = up_plain[:, cols]
        else:
            u = up_near[:, cols] + up_far[:, cols]
        u = ADAPTER_SCALE * u
        slot = quarter ^ c
        keep[slot, :, :up_step] = jnp.where(first, u[:, :up_step], u[:, up_step:])
        send[slot, :, :up_step] = jnp.where(first, u[:, up_step:], u[:, :up_step])
        keep[slot, :, up_step:] = jnp.where(first, d[:, :down_step], d[:, down_step:])
        send[slot, :, up_step:] = jnp.where(first, d[:, down_step:], d[:, :down_step])


def spread(pieces, own, down_out, up_out):
    half, quarter = position()
    half = half if own else 1 - half
    up_step, down_step = up_out.shape[2] // 8, down_out.shape[2] // 8
    for c in range(4):
        x = pieces[quarter ^ c].astype(F32)
        at = 2 * c + half
        ups = pl.ds(pl.multiple_of(at * up_step, up_step), up_step)
        downs = pl.ds(pl.multiple_of(at * down_step, down_step), down_step)
        for j in range(3):
            part = x[8 * j : 8 * j + 8]
            up_out[j, :, ups] = part[:, :up_step]
            down_out[j, :, downs] = part[:, up_step:]


def first_spread(pieces, down_out, up_out):
    spread(pieces, True, down_out, up_out)


def last_spread(pieces, down_in, up_in, down_out, up_out):
    down_out[...] = down_in[...]
    up_out[...] = up_in[...]
    spread(pieces, False, down_out, up_out)


def call(kernel, outs, *args):
    return pl.pallas_call(
        kernel,
        out_shape=outs,
        in_specs=[VMEM] * len(args),
        out_specs=jax.tree.map(lambda _: VMEM, outs),
        compiler_params=pltpu.CompilerParams(vmem_limit_bytes=LIMIT),
        cost_estimate=COST,
    )(*args)


def swap(x, bits, total):
    return lax.ppermute(x, AXES, [(i, i ^ bits) for i in range(total)])


def total_sum(keep, send, seqs, dps):
    total = seqs * dps
    partner = {1: dps | 1, 2: 2, 3: dps | 3}
    keep = keep + swap(send, 1, total)
    got = [swap(keep[s].astype(BF), partner[s], total).astype(F32) for s in (1, 2, 3)]
    own = keep[0] + got[2] + got[0] + got[1]
    bit = 2
    while bit < seqs:
        steps = [bit, 2 * bit, 3 * bit] if 2 * bit < seqs else [bit]
        bit *= len(steps) + 1
        if bit >= seqs:
            own = own.astype(BF)
        parts = [swap(own, step * dps, total) for step in steps]
        own = own.astype(F32)
        if len(parts) == 3:
            own = (own + parts[0].astype(F32)) + (parts[2].astype(F32) + parts[1].astype(F32))
        else:
            own = own + parts[0].astype(F32)
    piece = own.astype(BF)
    mine = jnp.stack([piece] + [swap(piece, partner[s], total) for s in (1, 2, 3)])
    return mine, swap(mine, 1, total)


def on_device(tokens, frozen, grad, down_weight, up_weight):
    seqs, dps = lax.axis_size("seq"), lax.axis_size("dp")
    count, width = grad.shape[1:]
    half, half_width = count // 2, width // 2
    forward = [(i, (i + 1) % seqs) for i in range(seqs)]
    backward = [(i, (i - 1) % seqs) for i in range(seqs)]
    frozen_kv = lax.ppermute(frozen[1:, 0, half:, half_width:], "seq", forward)
    low_t = jnp.einsum("psw,gw->psg", down_weight, tokens[0], preferred_element_type=F32).astype(BF)
    low_kv = lax.ppermute(low_t[1:, :, half:], "seq", forward)
    sds = jax.ShapeDtypeStruct
    up_half, rank_side = sds((24, half_width), F32), sds((24, count), F32)
    projected = call(project_kernel, sds((3, count, width), BF), frozen, low_t, up_weight)
    up_plain, rank_plain = call(
        functools.partial(group_kernel, 0, 0), [up_half, rank_side], projected, grad, low_t, up_weight
    )
    n = half_width // HEAD_DIM
    square, line, pairs = sds((n, half, half), F32), sds((n, half), F32), sds((n, 2 * RANK, half), BF)
    e, dp, top, total, bk, bv = call(
        far_ready, [square, square, line, line, pairs, pairs], projected, grad, up_weight
    )
    up_near, rank_near = call(
        functools.partial(group_kernel, half, half_width), [up_half, rank_side], projected, grad, low_t, up_weight
    )
    bk, rank_plain, rank_near = lax.optimization_barrier((bk, rank_plain, rank_near))
    squares = sds((n, half, half), BF)
    cross, near, pb, ds, factor, dot = call(
        far_scores,
        [sds((2 * RANK, count), F32), sds((n, half, HEAD_DIM), BF), squares, squares, line, line],
        projected, frozen_kv, low_kv, grad, up_weight, e, dp, top, total, bk, bv,
    )
    cross = lax.ppermute(cross, "seq", backward)
    up_far, rank_far = call(
        far_rest, [up_half, rank_side],
        projected, low_kv, grad, low_t, up_weight, e, dp, bk, bv, near, pb, ds, factor, dot,
    )
    columns = (width + tokens.shape[2]) // 8
    piece = sds((4, 24, columns), F32)
    keep, send = call(down_kernel, [piece, piece], tokens, rank_plain, rank_near, rank_far, cross, up_plain, up_near, up_far)
    mine, other = total_sum(keep, send, seqs, dps)
    outs = [sds((3, RANK, tokens.shape[2]), F32), sds((3, RANK, width), F32)]
    return tuple(call(last_spread, outs, other, *call(first_spread, outs, mine)))


def solution(mesh):
    return jax.shard_map(
        on_device,
        mesh=mesh,
        in_specs=(P("dp", "seq", None), P(None, "dp", "seq", None), P("dp", "seq", None), P(), P()),
        out_specs=(P(), P()),
        check_vma=False,
    )
```

```python
import functools

import jax
import jax.numpy as jnp
from jax import lax
from jax.experimental import pallas as pl
from jax.experimental.pallas import tpu as pltpu
from jax.sharding import PartitionSpec as P

HEAD_DIM = 128
RANK = 8
SCALE = HEAD_DIM ** -0.5
ADAPTER_SCALE = 2.0
BF = jnp.bfloat16
F32 = jnp.float32
AXES = ("seq", "dp")
COST = pl.CostEstimate(flops=10**6, bytes_accessed=10**4, transcendentals=0)
VMEM = pl.BlockSpec(memory_space=pltpu.VMEM)
LIMIT = 48 * 1024 * 1024


def nt(a, b):
    return lax.dot_general(a, b, (((1,), (1,)), ((), ())), preferred_element_type=F32)


def nn(a, b):
    return lax.dot_general(a, b, (((1,), (0,)), ((), ())), preferred_element_type=F32)


def tn(a, b):
    return lax.dot_general(a, b, (((0,), (0,)), ((), ())), preferred_element_type=F32)


def hi_lo(x):
    high = x.astype(BF).astype(F32)
    return [high, x - high]


def rows(parts):
    return jnp.concatenate(parts, axis=0).astype(BF)


def project(frozen, low_t, up):
    return (frozen.astype(F32) + ADAPTER_SCALE * tn(low_t, up)).astype(BF)


def scores(items, mask):
    sts = [nt(k, q) for q, k, v, g, ups, lows in items]
    dps = [nt(v, g) for q, k, v, g, ups, lows in items]
    bs = [(nt(ups[1], q), nt(ups[2], g)) for q, k, v, g, ups, lows in items]
    pbs, dss = [], []
    for st, dp in zip(sts, dps):
        st = jnp.where(mask, st * SCALE, -jnp.inf)
        e = jnp.exp(st - jnp.max(st, axis=0, keepdims=True))
        p = e * (1.0 / jnp.sum(e, axis=0, keepdims=True))
        pb = p.astype(BF)
        row_dot = jnp.sum(pb.astype(F32) * dp, axis=0, keepdims=True)
        pbs.append(pb)
        dss.append((p * (dp - row_dot) * SCALE).astype(BF))
    by_k = [nt(rows([it[5][0]] + hi_lo(b[0])), ds) for it, b, ds in zip(items, bs, dss)]
    by_v = [nt(rows(hi_lo(b[1])), pb) for b, pb in zip(bs, pbs)]
    return [
        (pb, ds, bk[:8], bk[8:16] + bk[16:24], r[:8] + r[8:])
        for pb, ds, bk, r in zip(pbs, dss, by_k, by_v)
    ]


def rest(items, found):
    bqs = [nt(it[4][0], it[1]) for it in items]
    by_q = [nn(rows([it[5][1]] + hi_lo(b)), f[1]) for it, b, f in zip(items, bqs, found)]
    av = [nn(it[5][2].astype(BF), f[0]) for it, f in zip(items, found)]
    out = []
    for it, f, bq, a in zip(items, found, by_q, av):
        q, k, v, g = it[:4]
        us = [nn(rows(hi_lo(f[2])), k), nn(rows(hi_lo(bq[:8])), q), nn(rows(hi_lo(a)), g)]
        out.append(([u[:8] + u[8:] for u in us], bq[8:16] + bq[16:24]))
    return out


def heads(items, mask):
    found = scores(items, mask)
    return [
        (grads, [rank_q, f[3], f[4]]) for f, (grads, rank_q) in zip(found, rest(items, found))
    ]


def causal(keys, queries, offset):
    return lax.broadcasted_iota(jnp.int32, (keys, queries), 0) <= offset + lax.broadcasted_iota(
        jnp.int32, (keys, queries), 1
    )


def project_kernel(frozen, low_t, up, out):
    for j in range(3):
        for start in range(0, out.shape[2], 512):
            cols = slice(start, start + 512)
            out[j, :, cols] = project(frozen[j, 0, :, cols], low_t[j], up[j, :, cols])


def group_kernel(first, start, projected, grad, low_t, up, up_out, rank_out):
    count = grad.shape[1]
    low = [low_t[j].astype(F32)[:, first:] for j in range(3)]
    starts = range(0, up_out.shape[1], HEAD_DIM)
    items = []
    for h in starts:
        cols = slice(start + h, start + h + HEAD_DIM)
        q, k, v = [projected[j, first:, cols] for j in range(3)]
        items.append((q, k, v, grad[0, first:, cols], [up[j, :, cols] for j in range(3)], low))
    parts = heads(items, causal(count - first, count - first, 0))
    for h, (grads, _) in zip(starts, parts):
        for j in range(3):
            up_out[8 * j : 8 * j + 8, h : h + HEAD_DIM] = grads[j]
    for j in range(3):
        part = sum(ranks[j] for _, ranks in parts)
        rank_out[8 * j : 8 * j + 8, :] = right(part) if first else part


def left(x):
    return jnp.concatenate([x, jnp.zeros_like(x)], axis=1)


def right(x):
    return jnp.concatenate([jnp.zeros_like(x), x], axis=1)


def shifted_pairs(up):
    half_width = up.shape[2] // 2
    return [slice(start, start + 2 * HEAD_DIM) for start in range(half_width, 2 * half_width, 2 * HEAD_DIM)]


def block_diagonal(x):
    none = jnp.zeros_like(x[:, :HEAD_DIM])
    return jnp.concatenate(
        [
            jnp.concatenate([x[:, :HEAD_DIM], none], axis=1),
            jnp.concatenate([none, x[:, HEAD_DIM:]], axis=1),
        ],
        axis=0,
    )


def far_ready(projected, grad, up, q_out, g_out, e_out, dp_out, top_out, sum_out, bk_out, bv_out):
    half = projected.shape[1] // 2
    key = lax.broadcasted_iota(jnp.int32, (half, 2 * half), 0)
    query = lax.broadcasted_iota(jnp.int32, (half, 2 * half), 1)
    mask = key <= jnp.where(query >= half, query - half, query)
    for h, cols in enumerate(shifted_pairs(up)):
        q = block_diagonal(projected[0, :half, cols])
        g = block_diagonal(grad[0, :half, cols])
        st = jnp.where(mask, nt(projected[1, :half, cols], q) * SCALE, -jnp.inf)
        top = jnp.max(st, axis=0, keepdims=True)
        e = jnp.exp(st - top)
        q_out[h] = q
        g_out[h] = g
        e_out[h] = e
        dp_out[h] = nt(projected[2, :half, cols], g)
        top_out[h : h + 1, :] = top
        sum_out[h : h + 1, :] = jnp.sum(e, axis=0, keepdims=True)
        bk_out[h] = rows(hi_lo(nt(up[1, :, cols], q)))
        bv_out[h] = rows(hi_lo(nt(up[2, :, cols], g)))


def far_scores(
    frozen_kv, low_kv, up, q, g, e, dp, top, total, bk, bv,
    cross_out, near_out, pb_out, ds_out, factor_out, dot_out,
):
    pairs = shifted_pairs(up)
    wide = [project(frozen_kv[j], low_kv[j], up[j + 1, :, pairs[0].start :]) for j in range(2)]
    here = [slice(h * 2 * HEAD_DIM, (h + 1) * 2 * HEAD_DIM) for h in range(len(pairs))]
    sts = [nt(wide[0][:, cols], q[h]) for h, cols in enumerate(here)]
    dps = [nt(wide[1][:, cols], g[h]) for h, cols in enumerate(here)]
    found = []
    for h, (st, dpn) in enumerate(zip(sts, dps)):
        st = st * SCALE
        far_top = top[h : h + 1, :]
        highest = jnp.maximum(far_top, jnp.max(st, axis=0, keepdims=True))
        en = jnp.exp(st - highest)
        rescale = jnp.exp(far_top - highest)
        inverse = 1.0 / (total[h : h + 1, :] * rescale + jnp.sum(en, axis=0, keepdims=True))
        factor = rescale * inverse
        p = en * inverse
        pb = p.astype(BF)
        far_pb = (e[h] * factor).astype(BF).astype(F32)
        dot = jnp.sum(pb.astype(F32) * dpn, axis=0, keepdims=True)
        dot = dot + jnp.sum(far_pb * dp[h], axis=0, keepdims=True)
        ds = (p * (dpn - dot) * SCALE).astype(BF)
        factor_out[h : h + 1, :] = factor
        dot_out[h : h + 1, :] = dot
        found.append((pb, ds))
    by_k = sum(nt(bk[h], ds) for h, (_, ds) in enumerate(found))
    by_v = sum(nt(bv[h], pb) for h, (pb, _) in enumerate(found))
    cross_out[:8, :] = right(by_k[:8] + by_k[8:])
    cross_out[8:, :] = right(by_v[:8] + by_v[8:])
    near_out[...] = wide[0]
    for h, (pb, ds) in enumerate(found):
        pb_out[h] = pb
        ds_out[h] = ds


def far_rest(
    projected, low_kv, low_t, up, q, g, e, dp, bk, bv, near, near_pb, near_ds, factor, dot, up_out, rank_out
):
    half = projected.shape[1] // 2
    far_f = [low_t[j].astype(F32)[:, :half] for j in range(3)]
    low_q = rows([left(far_f[0]), right(far_f[0])])
    low_k, low_v = [jnp.concatenate([low_kv[j].astype(F32), far_f[j + 1]], axis=1) for j in range(2)]
    first_head = lax.broadcasted_iota(jnp.int32, (3 * RANK, 2 * half), 1) < half
    pairs = shifted_pairs(up)
    here = [slice(h * 2 * HEAD_DIM, (h + 1) * 2 * HEAD_DIM) for h in range(len(pairs))]
    far_ds, far_pb, whole_ds, whole_pb, keys = [], [], [], [], []
    for h, cols in enumerate(pairs):
        p = e[h] * factor[h : h + 1, :]
        far_pb.append(p.astype(BF))
        far_ds.append((p * (dp[h] - dot[h : h + 1, :]) * SCALE).astype(BF))
        whole_pb.append(jnp.concatenate([near_pb[h], far_pb[h]], axis=0))
        whole_ds.append(jnp.concatenate([near_ds[h], far_ds[h]], axis=0))
        keys.append(jnp.concatenate([near[:, here[h]], projected[1, :half, cols]], axis=0))
    by_k = sum(nt(bk[h], ds) for h, ds in enumerate(far_ds))
    by_v = sum(nt(bv[h], pb) for h, pb in enumerate(far_pb))
    aq = [nt(low_q, ds) for ds in whole_ds]
    av = [nn(low_v.astype(BF), pb) for pb in whole_pb]
    by_q = []
    for h, cols in enumerate(pairs):
        both = []
        for t in range(2):
            head = slice(t * HEAD_DIM, (t + 1) * HEAD_DIM)
            both += [low_k] + hi_lo(nt(up[0, :, cols][:, head], keys[h][:, head]))
        x = nn(rows(both), whole_ds[h])
        by_q.append(jnp.where(first_head, x[: 3 * RANK], x[3 * RANK :]))
    rank_q = 0.0
    for h in range(len(pairs)):
        uk = nn(rows(hi_lo(by_q[h][:8])), q[h])
        uv = nn(rows(hi_lo(av[h])), g[h])
        up_out[8:16, here[h]] = uk[:8] + uk[8:]
        up_out[16:, here[h]] = uv[:8] + uv[8:]
        for t in range(2):
            uq = nn(rows(hi_lo(aq[h][8 * t : 8 * t + 8])), keys[h][:, t * HEAD_DIM : (t + 1) * HEAD_DIM])
            start = here[h].start + t * HEAD_DIM
            up_out[:8, start : start + HEAD_DIM] = uq[:8] + uq[8:]
        rank_q = rank_q + by_q[h][8:16] + by_q[h][16:24]
    rank_out[:8, :] = left(rank_q[:, :half] + rank_q[:, half:])
    rank_out[8:16, :] = left(by_k[:8] + by_k[8:])
    rank_out[16:, :] = left(by_v[:8] + by_v[8:])


def position():
    seq, dp = lax.axis_index("seq"), lax.axis_index("dp")
    return (seq ^ dp) & 1, (dp & 2) | (seq & 1)


def down_kernel(tokens, rank_plain, rank_near, rank_far, cross, up_plain, up_near, up_far, keep, send):
    half, quarter = position()
    first = half == 0
    ranks = rank_plain[...] + rank_near[...] + rank_far[...]
    ranks = ranks + jnp.concatenate([jnp.zeros((RANK, ranks.shape[1]), F32), cross[...]], axis=0)
    both = rows(hi_lo(ranks))
    n = ranks.shape[0]
    up_step, down_step = up_plain.shape[1] // 4, tokens.shape[2] // 8
    for c in range(4):
        d = nn(both, tokens[0, :, 2 * c * down_step : 2 * (c + 1) * down_step])
        d = ADAPTER_SCALE * (d[:n] + d[n:])
        cols = slice((c % 2) * 2 * up_step, (c % 2 + 1) * 2 * up_step)
        if c < 2:
            u = up_plain[:, cols]
        else:
            u = up_near[:, cols] + up_far[:, cols]
        u = ADAPTER_SCALE * u
        slot = quarter ^ c
        keep[slot, :, :up_step] = jnp.where(first, u[:, :up_step], u[:, up_step:])
        send[slot, :, :up_step] = jnp.where(first, u[:, up_step:], u[:, :up_step])
        keep[slot, :, up_step:] = jnp.where(first, d[:, :down_step], d[:, down_step:])
        send[slot, :, up_step:] = jnp.where(first, d[:, down_step:], d[:, :down_step])


def spread(pieces, own, down_out, up_out):
    half, quarter = position()
    half = half if own else 1 - half
    up_step, down_step = up_out.shape[2] // 8, down_out.shape[2] // 8
    for c in range(4):
        x = pieces[quarter ^ c].astype(F32)
        at = 2 * c + half
        ups = pl.ds(pl.multiple_of(at * up_step, up_step), up_step)
        downs = pl.ds(pl.multiple_of(at * down_step, down_step), down_step)
        for j in range(3):
            part = x[8 * j : 8 * j + 8]
            up_out[j, :, ups] = part[:, :up_step]
            down_out[j, :, downs] = part[:, up_step:]


def first_spread(pieces, down_out, up_out):
    spread(pieces, True, down_out, up_out)


def last_spread(pieces, down_in, up_in, down_out, up_out):
    down_out[...] = down_in[...]
    up_out[...] = up_in[...]
    spread(pieces, False, down_out, up_out)


def call(kernel, outs, *args):
    return pl.pallas_call(
        kernel,
        out_shape=outs,
        in_specs=[VMEM] * len(args),
        out_specs=jax.tree.map(lambda _: VMEM, outs),
        compiler_params=pltpu.CompilerParams(vmem_limit_bytes=LIMIT),
        cost_estimate=COST,
    )(*args)


def swap(x, bits, total):
    return lax.ppermute(x, AXES, [(i, i ^ bits) for i in range(total)])


def total_sum(keep, send, seqs, dps):
    total = seqs * dps
    partner = {1: dps | 1, 2: 2, 3: dps | 3}
    keep = keep + swap(send, 1, total)
    got = [swap(keep[s].astype(BF), partner[s], total).astype(F32) for s in (1, 2, 3)]
    own = keep[0] + got[2] + got[0] + got[1]
    bit = 2
    while bit < seqs:
        steps = [bit, 2 * bit, 3 * bit] if 2 * bit < seqs else [bit]
        bit *= len(steps) + 1
        if bit >= seqs:
            own = own.astype(BF)
        parts = [swap(own, step * dps, total) for step in steps]
        own = own.astype(F32)
        if len(parts) == 3:
            own = (own + parts[0].astype(F32)) + (parts[2].astype(F32) + parts[1].astype(F32))
        else:
            own = own + parts[0].astype(F32)
    piece = own.astype(BF)
    mine = [piece] + [swap(piece, partner[s], total) for s in (1, 2, 3)]
    return jnp.stack(mine), jnp.stack([swap(x, 1, total) for x in mine])


def on_device(tokens, frozen, grad, down_weight, up_weight):
    seqs, dps = lax.axis_size("seq"), lax.axis_size("dp")
    count, width = grad.shape[1:]
    half, half_width = count // 2, width // 2
    forward = [(i, (i + 1) % seqs) for i in range(seqs)]
    backward = [(i, (i - 1) % seqs) for i in range(seqs)]
    frozen_kv = lax.ppermute(frozen[1:, 0, half:, half_width:], "seq", forward)
    low_t = jnp.einsum("psw,gw->psg", down_weight, tokens[0], preferred_element_type=F32).astype(BF)
    low_kv = lax.ppermute(low_t[1:, :, half:], "seq", forward)
    sds = jax.ShapeDtypeStruct
    up_half, rank_side = sds((24, half_width), F32), sds((24, count), F32)
    projected = call(project_kernel, sds((3, count, width), BF), frozen, low_t, up_weight)
    up_plain, rank_plain = call(
        functools.partial(group_kernel, 0, 0), [up_half, rank_side], projected, grad, low_t, up_weight
    )
    n = half_width // HEAD_DIM // 2
    diagonal, line, pairs = sds((n, 2 * half, 2 * HEAD_DIM), BF), sds((n, 2 * half), F32), sds((n, 2 * RANK, 2 * half), BF)
    square = sds((n, half, 2 * half), F32)
    q, g, e, dp, top, total, bk, bv = call(
        far_ready, [diagonal, diagonal, square, square, line, line, pairs, pairs], projected, grad, up_weight
    )
    up_near, rank_near = call(
        functools.partial(group_kernel, half, half_width), [up_half, rank_side], projected, grad, low_t, up_weight
    )
    bk, rank_plain, rank_near = lax.optimization_barrier((bk, rank_plain, rank_near))
    squares = sds((n, half, 2 * half), BF)
    cross, near, pb, ds, factor, dot = call(
        far_scores,
        [sds((2 * RANK, count), F32), sds((half, half_width), BF), squares, squares, line, line],
        frozen_kv, low_kv, up_weight, q, g, e, dp, top, total, bk, bv,
    )
    cross = lax.ppermute(cross, "seq", backward)
    up_far, rank_far = call(
        far_rest, [up_half, rank_side],
        projected, low_kv, low_t, up_weight, q, g, e, dp, bk, bv, near, pb, ds, factor, dot,
    )
    columns = (width + tokens.shape[2]) // 8
    piece = sds((4, 24, columns), F32)
    keep, send = call(down_kernel, [piece, piece], tokens, rank_plain, rank_near, rank_far, cross, up_plain, up_near, up_far)
    mine, other = total_sum(keep, send, seqs, dps)
    outs = [sds((3, RANK, tokens.shape[2]), F32), sds((3, RANK, width), F32)]
    return tuple(call(last_spread, outs, other, *call(first_spread, outs, mine)))


def solution(mesh):
    return jax.shard_map(
        on_device,
        mesh=mesh,
        in_specs=(P("dp", "seq", None), P(None, "dp", "seq", None), P("dp", "seq", None), P(), P()),
        out_specs=(P(), P()),
        check_vma=False,
    )
```

```python
import functools

import jax
import jax.numpy as jnp
from jax import lax
from jax.experimental import pallas as pl
from jax.experimental.pallas import tpu as pltpu
from jax.sharding import PartitionSpec as P

HEAD_DIM = 128
RANK = 8
SCALE = HEAD_DIM ** -0.5
ADAPTER_SCALE = 2.0
BF = jnp.bfloat16
F32 = jnp.float32
AXES = ("seq", "dp")
COST = pl.CostEstimate(flops=10**6, bytes_accessed=10**4, transcendentals=0)
VMEM = pl.BlockSpec(memory_space=pltpu.VMEM)
LIMIT = 48 * 1024 * 1024


def nt(a, b):
    return lax.dot_general(a, b, (((1,), (1,)), ((), ())), preferred_element_type=F32)


def nn(a, b):
    return lax.dot_general(a, b, (((1,), (0,)), ((), ())), preferred_element_type=F32)


def tn(a, b):
    return lax.dot_general(a, b, (((0,), (0,)), ((), ())), preferred_element_type=F32)


def hi_lo(x):
    high = x.astype(BF).astype(F32)
    return [high, x - high]


def rows(parts):
    return jnp.concatenate(parts, axis=0).astype(BF)


def project(frozen, low_t, up):
    return (frozen.astype(F32) + ADAPTER_SCALE * tn(low_t, up)).astype(BF)


def scores(items, mask):
    sts = [nt(k, q) for q, k, v, g, ups, lows in items]
    dps = [nt(v, g) for q, k, v, g, ups, lows in items]
    bs = [(nt(ups[1], q), nt(ups[2], g)) for q, k, v, g, ups, lows in items]
    pbs, dss = [], []
    for st, dp in zip(sts, dps):
        st = jnp.where(mask, st * SCALE, -jnp.inf)
        e = jnp.exp(st - jnp.max(st, axis=0, keepdims=True))
        p = e * (1.0 / jnp.sum(e, axis=0, keepdims=True))
        pb = p.astype(BF)
        row_dot = jnp.sum(pb.astype(F32) * dp, axis=0, keepdims=True)
        pbs.append(pb)
        dss.append((p * (dp - row_dot) * SCALE).astype(BF))
    by_k = [nt(rows([it[5][0]] + hi_lo(b[0])), ds) for it, b, ds in zip(items, bs, dss)]
    by_v = [nt(rows(hi_lo(b[1])), pb) for b, pb in zip(bs, pbs)]
    return [
        (pb, ds, bk[:8], bk[8:16] + bk[16:24], r[:8] + r[8:])
        for pb, ds, bk, r in zip(pbs, dss, by_k, by_v)
    ]


def rest(items, found):
    bqs = [nt(it[4][0], it[1]) for it in items]
    by_q = [nn(rows([it[5][1]] + hi_lo(b)), f[1]) for it, b, f in zip(items, bqs, found)]
    av = [nn(it[5][2].astype(BF), f[0]) for it, f in zip(items, found)]
    out = []
    for it, f, bq, a in zip(items, found, by_q, av):
        q, k, v, g = it[:4]
        us = [nn(rows(hi_lo(f[2])), k), nn(rows(hi_lo(bq[:8])), q), nn(rows(hi_lo(a)), g)]
        out.append(([u[:8] + u[8:] for u in us], bq[8:16] + bq[16:24]))
    return out


def heads(items, mask):
    found = scores(items, mask)
    return [
        (grads, [rank_q, f[3], f[4]]) for f, (grads, rank_q) in zip(found, rest(items, found))
    ]


def causal(keys, queries, offset):
    return lax.broadcasted_iota(jnp.int32, (keys, queries), 0) <= offset + lax.broadcasted_iota(
        jnp.int32, (keys, queries), 1
    )


def project_kernel(frozen, low_t, up, out):
    for j in range(3):
        for start in range(0, out.shape[2], 512):
            cols = slice(start, start + 512)
            out[j, :, cols] = project(frozen[j, 0, :, cols], low_t[j], up[j, :, cols])


def group_kernel(first, start, projected, grad, low_t, up, up_out, rank_out):
    count = grad.shape[1]
    low = [low_t[j].astype(F32)[:, first:] for j in range(3)]
    starts = range(0, up_out.shape[1], HEAD_DIM)
    items = []
    for h in starts:
        cols = slice(start + h, start + h + HEAD_DIM)
        q, k, v = [projected[j, first:, cols] for j in range(3)]
        items.append((q, k, v, grad[0, first:, cols], [up[j, :, cols] for j in range(3)], low))
    parts = heads(items, causal(count - first, count - first, 0))
    for h, (grads, _) in zip(starts, parts):
        for j in range(3):
            up_out[8 * j : 8 * j + 8, h : h + HEAD_DIM] = grads[j]
    for j in range(3):
        part = sum(ranks[j] for _, ranks in parts)
        rank_out[8 * j : 8 * j + 8, :] = right(part) if first else part


def left(x):
    return jnp.concatenate([x, jnp.zeros_like(x)], axis=1)


def right(x):
    return jnp.concatenate([jnp.zeros_like(x), x], axis=1)


def shifted_pairs(up):
    half_width = up.shape[2] // 2
    return [slice(start, start + 2 * HEAD_DIM) for start in range(half_width, 2 * half_width, 2 * HEAD_DIM)]


def block_diagonal(x):
    none = jnp.zeros_like(x[:, :HEAD_DIM])
    return jnp.concatenate(
        [
            jnp.concatenate([x[:, :HEAD_DIM], none], axis=1),
            jnp.concatenate([none, x[:, HEAD_DIM:]], axis=1),
        ],
        axis=0,
    )


def far_ready(projected, grad, up, q_out, g_out, e_out, dp_out, top_out, sum_out, bk_out, bv_out):
    half = projected.shape[1] // 2
    key = lax.broadcasted_iota(jnp.int32, (half, 2 * half), 0)
    query = lax.broadcasted_iota(jnp.int32, (half, 2 * half), 1)
    mask = key <= jnp.where(query >= half, query - half, query)
    for h, cols in enumerate(shifted_pairs(up)):
        q = block_diagonal(projected[0, :half, cols])
        g = block_diagonal(grad[0, :half, cols])
        st = jnp.where(mask, nt(projected[1, :half, cols], q) * SCALE, -jnp.inf)
        top = jnp.max(st, axis=0, keepdims=True)
        e = jnp.exp(st - top)
        q_out[h] = q
        g_out[h] = g
        e_out[h] = e
        dp_out[h] = nt(projected[2, :half, cols], g)
        top_out[h : h + 1, :] = top
        sum_out[h : h + 1, :] = jnp.sum(e, axis=0, keepdims=True)
        bk_out[h] = rows(hi_lo(nt(up[1, :, cols], q)))
        bv_out[h] = rows(hi_lo(nt(up[2, :, cols], g)))


def far_scores(
    frozen_kv, low_kv, up, q, g, e, dp, top, total, bk, bv,
    cross_out, near_out, pb_out, ds_out, factor_out, dot_out,
):
    pairs = shifted_pairs(up)
    wide = [project(frozen_kv[j], low_kv[j], up[j + 1, :, pairs[0].start :]) for j in range(2)]
    here = [slice(h * 2 * HEAD_DIM, (h + 1) * 2 * HEAD_DIM) for h in range(len(pairs))]
    sts = [nt(wide[0][:, cols], q[h]) for h, cols in enumerate(here)]
    dps = [nt(wide[1][:, cols], g[h]) for h, cols in enumerate(here)]
    found = []
    for h, (st, dpn) in enumerate(zip(sts, dps)):
        st = st * SCALE
        far_top = top[h : h + 1, :]
        highest = jnp.maximum(far_top, jnp.max(st, axis=0, keepdims=True))
        en = jnp.exp(st - highest)
        rescale = jnp.exp(far_top - highest)
        inverse = 1.0 / (total[h : h + 1, :] * rescale + jnp.sum(en, axis=0, keepdims=True))
        factor = rescale * inverse
        p = en * inverse
        pb = p.astype(BF)
        far_pb = (e[h] * factor).astype(BF).astype(F32)
        dot = jnp.sum(pb.astype(F32) * dpn, axis=0, keepdims=True)
        dot = dot + jnp.sum(far_pb * dp[h], axis=0, keepdims=True)
        ds = (p * (dpn - dot) * SCALE).astype(BF)
        factor_out[h : h + 1, :] = factor
        dot_out[h : h + 1, :] = dot
        found.append((pb, ds))
    by_k = sum(nt(bk[h], ds) for h, (_, ds) in enumerate(found))
    by_v = sum(nt(bv[h], pb) for h, (pb, _) in enumerate(found))
    cross_out[:8, :] = right(by_k[:8] + by_k[8:])
    cross_out[8:, :] = right(by_v[:8] + by_v[8:])
    near_out[...] = wide[0]
    for h, (pb, ds) in enumerate(found):
        pb_out[h] = pb
        ds_out[h] = ds


def far_rest(
    projected, low_kv, low_t, up, q, g, e, dp, bk, bv, near, near_pb, near_ds, factor, dot, up_out, rank_out
):
    half = projected.shape[1] // 2
    far_f = [low_t[j].astype(F32)[:, :half] for j in range(3)]
    low_q = rows([left(far_f[0]), right(far_f[0])])
    low_k, low_v = [jnp.concatenate([low_kv[j].astype(F32), far_f[j + 1]], axis=1) for j in range(2)]
    first_head = lax.broadcasted_iota(jnp.int32, (3 * RANK, 2 * half), 1) < half
    pairs = shifted_pairs(up)
    here = [slice(h * 2 * HEAD_DIM, (h + 1) * 2 * HEAD_DIM) for h in range(len(pairs))]
    far_ds, far_pb, whole_ds, whole_pb, keys = [], [], [], [], []
    for h, cols in enumerate(pairs):
        p = e[h] * factor[h : h + 1, :]
        far_pb.append(p.astype(BF))
        far_ds.append((p * (dp[h] - dot[h : h + 1, :]) * SCALE).astype(BF))
        whole_pb.append(jnp.concatenate([near_pb[h], far_pb[h]], axis=0))
        whole_ds.append(jnp.concatenate([near_ds[h], far_ds[h]], axis=0))
        keys.append(jnp.concatenate([near[:, here[h]], projected[1, :half, cols]], axis=0))
    by_k = sum(nt(bk[h], ds) for h, ds in enumerate(far_ds))
    by_v = sum(nt(bv[h], pb) for h, pb in enumerate(far_pb))
    aq = [nt(low_q, ds) for ds in whole_ds]
    av = [nn(low_v.astype(BF), pb) for pb in whole_pb]
    by_q = []
    for h, cols in enumerate(pairs):
        both = []
        for t in range(2):
            head = slice(t * HEAD_DIM, (t + 1) * HEAD_DIM)
            both += [low_k] + hi_lo(nt(up[0, :, cols][:, head], keys[h][:, head]))
        x = nn(rows(both), whole_ds[h])
        by_q.append(jnp.where(first_head, x[: 3 * RANK], x[3 * RANK :]))
    rank_q = 0.0
    for h in range(len(pairs)):
        uk = nn(rows(hi_lo(by_q[h][:8])), q[h])
        uv = nn(rows(hi_lo(av[h])), g[h])
        up_out[8:16, here[h]] = uk[:8] + uk[8:]
        up_out[16:, here[h]] = uv[:8] + uv[8:]
        for t in range(2):
            uq = nn(rows(hi_lo(aq[h][8 * t : 8 * t + 8])), keys[h][:, t * HEAD_DIM : (t + 1) * HEAD_DIM])
            start = here[h].start + t * HEAD_DIM
            up_out[:8, start : start + HEAD_DIM] = uq[:8] + uq[8:]
        rank_q = rank_q + by_q[h][8:16] + by_q[h][16:24]
    rank_out[:8, :] = left(rank_q[:, :half] + rank_q[:, half:])
    rank_out[8:16, :] = left(by_k[:8] + by_k[8:])
    rank_out[16:, :] = left(by_v[:8] + by_v[8:])


def position():
    seq, dp = lax.axis_index("seq"), lax.axis_index("dp")
    return (seq ^ dp) & 1, (dp & 2) | (seq & 1)


def down_kernel(tokens, rank_plain, rank_near, rank_far, cross, up_plain, up_near, up_far, keep, send):
    half, quarter = position()
    first = half == 0
    ranks = rank_plain[...] + rank_near[...] + rank_far[...]
    ranks = ranks + jnp.concatenate([jnp.zeros((RANK, ranks.shape[1]), F32), cross[...]], axis=0)
    both = rows(hi_lo(ranks))
    n = ranks.shape[0]
    up_step, down_step = up_plain.shape[1] // 4, tokens.shape[2] // 8
    for c in range(4):
        d = nn(both, tokens[0, :, 2 * c * down_step : 2 * (c + 1) * down_step])
        d = ADAPTER_SCALE * (d[:n] + d[n:])
        cols = slice((c % 2) * 2 * up_step, (c % 2 + 1) * 2 * up_step)
        if c < 2:
            u = up_plain[:, cols]
        else:
            u = up_near[:, cols] + up_far[:, cols]
        u = ADAPTER_SCALE * u
        slot = quarter ^ c
        keep[slot, :, :up_step] = jnp.where(first, u[:, :up_step], u[:, up_step:])
        send[slot, :, :up_step] = jnp.where(first, u[:, up_step:], u[:, :up_step])
        keep[slot, :, up_step:] = jnp.where(first, d[:, :down_step], d[:, down_step:])
        send[slot, :, up_step:] = jnp.where(first, d[:, down_step:], d[:, :down_step])


def spread(pieces, own, down_out, up_out):
    half, quarter = position()
    half = half if own else 1 - half
    up_step, down_step = up_out.shape[2] // 8, down_out.shape[2] // 8
    for away in range(4):
        x = pieces[away][...].astype(F32)
        at = 2 * (quarter ^ away) + half
        ups = pl.ds(pl.multiple_of(at * up_step, up_step), up_step)
        downs = pl.ds(pl.multiple_of(at * down_step, down_step), down_step)
        for j in range(3):
            part = x[8 * j : 8 * j + 8]
            up_out[j, :, ups] = part[:, :up_step]
            down_out[j, :, downs] = part[:, up_step:]


def first_spread(a, b, c, d, down_out, up_out):
    spread((a, b, c, d), True, down_out, up_out)


def last_spread(a, b, c, d, down_in, up_in, down_out, up_out):
    down_out[...] = down_in[...]
    up_out[...] = up_in[...]
    spread((a, b, c, d), False, down_out, up_out)


def call(kernel, outs, *args):
    return pl.pallas_call(
        kernel,
        out_shape=outs,
        in_specs=[VMEM] * len(args),
        out_specs=jax.tree.map(lambda _: VMEM, outs),
        compiler_params=pltpu.CompilerParams(vmem_limit_bytes=LIMIT),
        cost_estimate=COST,
    )(*args)


def swap(x, bits, total):
    return lax.ppermute(x, AXES, [(i, i ^ bits) for i in range(total)])


def total_sum(keep, send, seqs, dps):
    total = seqs * dps
    partner = {1: dps | 1, 2: 2, 3: dps | 3}
    keep = keep + swap(send.astype(BF), 1, total).astype(F32)
    got = [swap(keep[s].astype(BF), partner[s], total).astype(F32) for s in (1, 2, 3)]
    own = keep[0] + got[2] + got[0] + got[1]
    bit = 2
    while bit < seqs:
        steps = [bit, 2 * bit, 3 * bit] if 2 * bit < seqs else [bit]
        bit *= len(steps) + 1
        if bit >= seqs:
            own = own.astype(BF)
        parts = [swap(own, step * dps, total) for step in steps]
        own = own.astype(F32)
        if len(parts) == 3:
            own = (own + parts[0].astype(F32)) + (parts[2].astype(F32) + parts[1].astype(F32))
        else:
            own = own + parts[0].astype(F32)
    piece = own.astype(BF)
    mine = [piece] + [swap(piece, partner[s], total) for s in (1, 2, 3)]
    return mine, [swap(x, 1, total) for x in mine]


def on_device(tokens, frozen, grad, down_weight, up_weight):
    seqs, dps = lax.axis_size("seq"), lax.axis_size("dp")
    count, width = grad.shape[1:]
    half, half_width = count // 2, width // 2
    forward = [(i, (i + 1) % seqs) for i in range(seqs)]
    backward = [(i, (i - 1) % seqs) for i in range(seqs)]
    frozen_kv = lax.ppermute(frozen[1:, 0, half:, half_width:], "seq", forward)
    low_t = jnp.einsum("psw,gw->psg", down_weight, tokens[0], preferred_element_type=F32).astype(BF)
    low_kv = lax.ppermute(low_t[1:, :, half:], "seq", forward)
    sds = jax.ShapeDtypeStruct
    up_half, rank_side = sds((24, half_width), F32), sds((24, count), F32)
    projected = call(project_kernel, sds((3, count, width), BF), frozen, low_t, up_weight)
    up_plain, rank_plain = call(
        functools.partial(group_kernel, 0, 0), [up_half, rank_side], projected, grad, low_t, up_weight
    )
    n = half_width // HEAD_DIM // 2
    diagonal, line, pairs = sds((n, 2 * half, 2 * HEAD_DIM), BF), sds((n, 2 * half), F32), sds((n, 2 * RANK, 2 * half), BF)
    square = sds((n, half, 2 * half), F32)
    q, g, e, dp, top, total, bk, bv = call(
        far_ready, [diagonal, diagonal, square, square, line, line, pairs, pairs], projected, grad, up_weight
    )
    up_near, rank_near = call(
        functools.partial(group_kernel, half, half_width), [up_half, rank_side], projected, grad, low_t, up_weight
    )
    bk, rank_plain, rank_near = lax.optimization_barrier((bk, rank_plain, rank_near))
    squares = sds((n, half, 2 * half), BF)
    cross, near, pb, ds, factor, dot = call(
        far_scores,
        [sds((2 * RANK, count), F32), sds((half, half_width), BF), squares, squares, line, line],
        frozen_kv, low_kv, up_weight, q, g, e, dp, top, total, bk, bv,
    )
    cross = lax.ppermute(cross, "seq", backward)
    up_far, rank_far = call(
        far_rest, [up_half, rank_side],
        projected, low_kv, low_t, up_weight, q, g, e, dp, bk, bv, near, pb, ds, factor, dot,
    )
    columns = (width + tokens.shape[2]) // 8
    piece = sds((4, 24, columns), F32)
    keep, send = call(down_kernel, [piece, piece], tokens, rank_plain, rank_near, rank_far, cross, up_plain, up_near, up_far)
    mine, other = total_sum(keep, send, seqs, dps)
    outs = [sds((3, RANK, tokens.shape[2]), F32), sds((3, RANK, width), F32)]
    return tuple(call(last_spread, outs, *other, *call(first_spread, outs, *mine)))


def solution(mesh):
    return jax.shard_map(
        on_device,
        mesh=mesh,
        in_specs=(P("dp", "seq", None), P(None, "dp", "seq", None), P("dp", "seq", None), P(), P()),
        out_specs=(P(), P()),
        check_vma=False,
    )
```

```python
import functools

import jax
import jax.numpy as jnp
from jax import lax
from jax.experimental import pallas as pl
from jax.experimental.pallas import tpu as pltpu
from jax.sharding import PartitionSpec as P

HEAD_DIM = 128
RANK = 8
SCALE = HEAD_DIM ** -0.5
ADAPTER_SCALE = 2.0
BF = jnp.bfloat16
F32 = jnp.float32
AXES = ("seq", "dp")
COST = pl.CostEstimate(flops=10**6, bytes_accessed=10**4, transcendentals=0)
VMEM = pl.BlockSpec(memory_space=pltpu.VMEM)
LIMIT = 48 * 1024 * 1024


def nt(a, b):
    return lax.dot_general(a, b, (((1,), (1,)), ((), ())), preferred_element_type=F32)


def nn(a, b):
    return lax.dot_general(a, b, (((1,), (0,)), ((), ())), preferred_element_type=F32)


def tn(a, b):
    return lax.dot_general(a, b, (((0,), (0,)), ((), ())), preferred_element_type=F32)


def hi_lo(x):
    high = x.astype(BF).astype(F32)
    return [high, x - high]


def rows(parts):
    return jnp.concatenate(parts, axis=0).astype(BF)


def project(frozen, low_t, up):
    return (frozen.astype(F32) + ADAPTER_SCALE * tn(low_t, up)).astype(BF)


def scores(items, mask):
    sts = [nt(k, q) for q, k, v, g, ups, lows in items]
    dps = [nt(v, g) for q, k, v, g, ups, lows in items]
    bs = [(nt(ups[1], q), nt(ups[2], g)) for q, k, v, g, ups, lows in items]
    pbs, dss = [], []
    for st, dp in zip(sts, dps):
        st = jnp.where(mask, st * SCALE, -jnp.inf)
        e = jnp.exp(st - jnp.max(st, axis=0, keepdims=True))
        p = e * (1.0 / jnp.sum(e, axis=0, keepdims=True))
        pb = p.astype(BF)
        row_dot = jnp.sum(pb.astype(F32) * dp, axis=0, keepdims=True)
        pbs.append(pb)
        dss.append((p * (dp - row_dot) * SCALE).astype(BF))
    by_k = [nt(rows([it[5][0]] + hi_lo(b[0])), ds) for it, b, ds in zip(items, bs, dss)]
    by_v = [nt(rows(hi_lo(b[1])), pb) for b, pb in zip(bs, pbs)]
    return [
        (pb, ds, bk[:8], bk[8:16] + bk[16:24], r[:8] + r[8:])
        for pb, ds, bk, r in zip(pbs, dss, by_k, by_v)
    ]


def rest(items, found):
    bqs = [nt(it[4][0], it[1]) for it in items]
    by_q = [nn(rows([it[5][1]] + hi_lo(b)), f[1]) for it, b, f in zip(items, bqs, found)]
    av = [nn(it[5][2].astype(BF), f[0]) for it, f in zip(items, found)]
    out = []
    for it, f, bq, a in zip(items, found, by_q, av):
        q, k, v, g = it[:4]
        us = [nn(rows(hi_lo(f[2])), k), nn(rows(hi_lo(bq[:8])), q), nn(rows(hi_lo(a)), g)]
        out.append(([u[:8] + u[8:] for u in us], bq[8:16] + bq[16:24]))
    return out


def heads(items, mask):
    found = scores(items, mask)
    return [
        (grads, [rank_q, f[3], f[4]]) for f, (grads, rank_q) in zip(found, rest(items, found))
    ]


def causal(keys, queries, offset):
    return lax.broadcasted_iota(jnp.int32, (keys, queries), 0) <= offset + lax.broadcasted_iota(
        jnp.int32, (keys, queries), 1
    )


def project_kernel(frozen, low_t, up, out):
    for j in range(3):
        for start in range(0, out.shape[2], 512):
            cols = slice(start, start + 512)
            out[j, :, cols] = project(frozen[j, 0, :, cols], low_t[j], up[j, :, cols])


def group_kernel(first, start, projected, grad, low_t, up, up_out, rank_out):
    count = grad.shape[1]
    low = [low_t[j].astype(F32)[:, first:] for j in range(3)]
    starts = range(0, up_out.shape[1], HEAD_DIM)
    items = []
    for h in starts:
        cols = slice(start + h, start + h + HEAD_DIM)
        q, k, v = [projected[j, first:, cols] for j in range(3)]
        items.append((q, k, v, grad[0, first:, cols], [up[j, :, cols] for j in range(3)], low))
    parts = heads(items, causal(count - first, count - first, 0))
    for h, (grads, _) in zip(starts, parts):
        for j in range(3):
            up_out[8 * j : 8 * j + 8, h : h + HEAD_DIM] = grads[j]
    for j in range(3):
        part = sum(ranks[j] for _, ranks in parts)
        rank_out[8 * j : 8 * j + 8, :] = right(part) if first else part


def left(x):
    return jnp.concatenate([x, jnp.zeros_like(x)], axis=1)


def right(x):
    return jnp.concatenate([jnp.zeros_like(x), x], axis=1)


def shifted_pairs(up):
    half_width = up.shape[2] // 2
    return [slice(start, start + 2 * HEAD_DIM) for start in range(half_width, 2 * half_width, 2 * HEAD_DIM)]


def block_diagonal(x):
    none = jnp.zeros_like(x[:, :HEAD_DIM])
    return jnp.concatenate(
        [
            jnp.concatenate([x[:, :HEAD_DIM], none], axis=1),
            jnp.concatenate([none, x[:, HEAD_DIM:]], axis=1),
        ],
        axis=0,
    )


def far_ready(projected, grad, up, q_out, g_out, e_out, dp_out, top_out, sum_out, bk_out, bv_out):
    half = projected.shape[1] // 2
    key = lax.broadcasted_iota(jnp.int32, (half, 2 * half), 0)
    query = lax.broadcasted_iota(jnp.int32, (half, 2 * half), 1)
    mask = key <= jnp.where(query >= half, query - half, query)
    for h, cols in enumerate(shifted_pairs(up)):
        q = block_diagonal(projected[0, :half, cols])
        g = block_diagonal(grad[0, :half, cols])
        st = jnp.where(mask, nt(projected[1, :half, cols], q) * SCALE, -jnp.inf)
        top = jnp.max(st, axis=0, keepdims=True)
        e = jnp.exp(st - top)
        q_out[h] = q
        g_out[h] = g
        e_out[h] = e
        dp_out[h] = nt(projected[2, :half, cols], g)
        top_out[h : h + 1, :] = top
        sum_out[h : h + 1, :] = jnp.sum(e, axis=0, keepdims=True)
        bk_out[h] = rows(hi_lo(nt(up[1, :, cols], q)))
        bv_out[h] = rows(hi_lo(nt(up[2, :, cols], g)))


def far_scores(
    frozen_kv, low_kv, up, q, g, e, dp, top, total, bk, bv,
    cross_out, near_out, pb_out, ds_out, factor_out, dot_out,
):
    pairs = shifted_pairs(up)
    wide = [project(frozen_kv[j], low_kv[j], up[j + 1, :, pairs[0].start :]) for j in range(2)]
    here = [slice(h * 2 * HEAD_DIM, (h + 1) * 2 * HEAD_DIM) for h in range(len(pairs))]
    sts = [nt(wide[0][:, cols], q[h]) for h, cols in enumerate(here)]
    dps = [nt(wide[1][:, cols], g[h]) for h, cols in enumerate(here)]
    found = []
    for h, (st, dpn) in enumerate(zip(sts, dps)):
        st = st * SCALE
        far_top = top[h : h + 1, :]
        highest = jnp.maximum(far_top, jnp.max(st, axis=0, keepdims=True))
        en = jnp.exp(st - highest)
        rescale = jnp.exp(far_top - highest)
        inverse = 1.0 / (total[h : h + 1, :] * rescale + jnp.sum(en, axis=0, keepdims=True))
        factor = rescale * inverse
        p = en * inverse
        pb = p.astype(BF)
        far_pb = (e[h] * factor).astype(BF).astype(F32)
        dot = jnp.sum(pb.astype(F32) * dpn, axis=0, keepdims=True)
        dot = dot + jnp.sum(far_pb * dp[h], axis=0, keepdims=True)
        ds = (p * (dpn - dot) * SCALE).astype(BF)
        factor_out[h : h + 1, :] = factor
        dot_out[h : h + 1, :] = dot
        found.append((pb, ds))
    by_k = sum(nt(bk[h], ds) for h, (_, ds) in enumerate(found))
    by_v = sum(nt(bv[h], pb) for h, (pb, _) in enumerate(found))
    cross_out[:8, :] = right(by_k[:8] + by_k[8:])
    cross_out[8:, :] = right(by_v[:8] + by_v[8:])
    near_out[...] = wide[0]
    for h, (pb, ds) in enumerate(found):
        pb_out[h] = pb
        ds_out[h] = ds


def far_rest(
    projected, low_kv, low_t, up, q, g, e, dp, bk, bv, near, near_pb, near_ds, factor, dot, up_out, rank_out
):
    half = projected.shape[1] // 2
    far_f = [low_t[j].astype(F32)[:, :half] for j in range(3)]
    low_q = rows([left(far_f[0]), right(far_f[0])])
    low_k, low_v = [jnp.concatenate([low_kv[j].astype(F32), far_f[j + 1]], axis=1) for j in range(2)]
    first_head = lax.broadcasted_iota(jnp.int32, (3 * RANK, 2 * half), 1) < half
    pairs = shifted_pairs(up)
    here = [slice(h * 2 * HEAD_DIM, (h + 1) * 2 * HEAD_DIM) for h in range(len(pairs))]
    far_ds, far_pb, whole_ds, whole_pb, keys = [], [], [], [], []
    for h, cols in enumerate(pairs):
        p = e[h] * factor[h : h + 1, :]
        far_pb.append(p.astype(BF))
        far_ds.append((p * (dp[h] - dot[h : h + 1, :]) * SCALE).astype(BF))
        whole_pb.append(jnp.concatenate([near_pb[h], far_pb[h]], axis=0))
        whole_ds.append(jnp.concatenate([near_ds[h], far_ds[h]], axis=0))
        keys.append(jnp.concatenate([near[:, here[h]], projected[1, :half, cols]], axis=0))
    by_k = sum(nt(bk[h], ds) for h, ds in enumerate(far_ds))
    by_v = sum(nt(bv[h], pb) for h, pb in enumerate(far_pb))
    aq = [nt(low_q, ds) for ds in whole_ds]
    av = [nn(low_v.astype(BF), pb) for pb in whole_pb]
    by_q = []
    for h, cols in enumerate(pairs):
        both = []
        for t in range(2):
            head = slice(t * HEAD_DIM, (t + 1) * HEAD_DIM)
            both += [low_k] + hi_lo(nt(up[0, :, cols][:, head], keys[h][:, head]))
        x = nn(rows(both), whole_ds[h])
        by_q.append(jnp.where(first_head, x[: 3 * RANK], x[3 * RANK :]))
    rank_q = 0.0
    for h in range(len(pairs)):
        uk = nn(rows(hi_lo(by_q[h][:8])), q[h])
        uv = nn(rows(hi_lo(av[h])), g[h])
        up_out[8:16, here[h]] = uk[:8] + uk[8:]
        up_out[16:, here[h]] = uv[:8] + uv[8:]
        for t in range(2):
            uq = nn(rows(hi_lo(aq[h][8 * t : 8 * t + 8])), keys[h][:, t * HEAD_DIM : (t + 1) * HEAD_DIM])
            start = here[h].start + t * HEAD_DIM
            up_out[:8, start : start + HEAD_DIM] = uq[:8] + uq[8:]
        rank_q = rank_q + by_q[h][8:16] + by_q[h][16:24]
    rank_out[:8, :] = left(rank_q[:, :half] + rank_q[:, half:])
    rank_out[8:16, :] = left(by_k[:8] + by_k[8:])
    rank_out[16:, :] = left(by_v[:8] + by_v[8:])


def position():
    seq, dp = lax.axis_index("seq"), lax.axis_index("dp")
    return (seq ^ dp) & 1, (dp & 2) | (seq & 1)


def down_kernel(tokens, rank_plain, rank_near, rank_far, cross, up_plain, up_near, up_far, keep, send):
    half, quarter = position()
    first = half == 0
    ranks = rank_plain[...] + rank_near[...] + rank_far[...]
    ranks = ranks + jnp.concatenate([jnp.zeros((RANK, ranks.shape[1]), F32), cross[...]], axis=0)
    both = rows(hi_lo(ranks))
    n = ranks.shape[0]
    up_step, down_step = up_plain.shape[1] // 4, tokens.shape[2] // 8
    for c in range(4):
        d = nn(both, tokens[0, :, 2 * c * down_step : 2 * (c + 1) * down_step])
        d = ADAPTER_SCALE * (d[:n] + d[n:])
        cols = slice((c % 2) * 2 * up_step, (c % 2 + 1) * 2 * up_step)
        if c < 2:
            u = up_plain[:, cols]
        else:
            u = up_near[:, cols] + up_far[:, cols]
        u = ADAPTER_SCALE * u
        slot = quarter ^ c
        keep[slot, :, :up_step] = jnp.where(first, u[:, :up_step], u[:, up_step:])
        send[slot, :, :up_step] = jnp.where(first, u[:, up_step:], u[:, :up_step]).astype(BF)
        keep[slot, :, up_step:] = jnp.where(first, d[:, :down_step], d[:, down_step:])
        send[slot, :, up_step:] = jnp.where(first, d[:, down_step:], d[:, :down_step]).astype(BF)


def spread(pieces, own, down_out, up_out):
    half, quarter = position()
    half = half if own else 1 - half
    up_step, down_step = up_out.shape[2] // 8, down_out.shape[2] // 8
    for away in range(4):
        x = pieces[away][...].astype(F32)
        at = 2 * (quarter ^ away) + half
        ups = pl.ds(pl.multiple_of(at * up_step, up_step), up_step)
        downs = pl.ds(pl.multiple_of(at * down_step, down_step), down_step)
        for j in range(3):
            part = x[8 * j : 8 * j + 8]
            up_out[j, :, ups] = part[:, :up_step]
            down_out[j, :, downs] = part[:, up_step:]


def first_spread(a, b, c, d, down_out, up_out):
    spread((a, b, c, d), True, down_out, up_out)


def last_spread(a, b, c, d, down_in, up_in, down_out, up_out):
    down_out[...] = down_in[...]
    up_out[...] = up_in[...]
    spread((a, b, c, d), False, down_out, up_out)


def call(kernel, outs, *args):
    return pl.pallas_call(
        kernel,
        out_shape=outs,
        in_specs=[VMEM] * len(args),
        out_specs=jax.tree.map(lambda _: VMEM, outs),
        compiler_params=pltpu.CompilerParams(vmem_limit_bytes=LIMIT),
        cost_estimate=COST,
    )(*args)


def swap(x, bits, total):
    return lax.ppermute(x, AXES, [(i, i ^ bits) for i in range(total)])


def total_sum(keep, send, seqs, dps):
    total = seqs * dps
    partner = {1: dps | 1, 2: 2, 3: dps | 3}
    keep = keep + swap(send, 1, total).astype(F32)
    got = [swap(keep[s].astype(BF), partner[s], total).astype(F32) for s in (1, 2, 3)]
    own = keep[0] + got[2] + got[0] + got[1]
    bit = 2
    while bit < seqs:
        steps = [bit, 2 * bit, 3 * bit] if 2 * bit < seqs else [bit]
        bit *= len(steps) + 1
        if bit >= seqs:
            own = own.astype(BF)
        parts = [swap(own, step * dps, total) for step in steps]
        own = own.astype(F32)
        if len(parts) == 3:
            own = (own + parts[0].astype(F32)) + (parts[2].astype(F32) + parts[1].astype(F32))
        else:
            own = own + parts[0].astype(F32)
    piece = own.astype(BF)
    mine = [piece] + [swap(piece, partner[s], total) for s in (1, 2, 3)]
    return mine, [swap(x, 1, total) for x in mine]


def on_device(tokens, frozen, grad, down_weight, up_weight):
    seqs, dps = lax.axis_size("seq"), lax.axis_size("dp")
    count, width = grad.shape[1:]
    half, half_width = count // 2, width // 2
    forward = [(i, (i + 1) % seqs) for i in range(seqs)]
    backward = [(i, (i - 1) % seqs) for i in range(seqs)]
    frozen_kv = lax.ppermute(frozen[1:, 0, half:, half_width:], "seq", forward)
    low_t = jnp.einsum("psw,gw->psg", down_weight, tokens[0], preferred_element_type=F32).astype(BF)
    low_kv = lax.ppermute(low_t[1:, :, half:], "seq", forward)
    sds = jax.ShapeDtypeStruct
    up_half, rank_side = sds((24, half_width), F32), sds((24, count), F32)
    projected = call(project_kernel, sds((3, count, width), BF), frozen, low_t, up_weight)
    up_plain, rank_plain = call(
        functools.partial(group_kernel, 0, 0), [up_half, rank_side], projected, grad, low_t, up_weight
    )
    n = half_width // HEAD_DIM // 2
    diagonal, line, pairs = sds((n, 2 * half, 2 * HEAD_DIM), BF), sds((n, 2 * half), F32), sds((n, 2 * RANK, 2 * half), BF)
    square = sds((n, half, 2 * half), F32)
    q, g, e, dp, top, total, bk, bv = call(
        far_ready, [diagonal, diagonal, square, square, line, line, pairs, pairs], projected, grad, up_weight
    )
    up_near, rank_near = call(
        functools.partial(group_kernel, half, half_width), [up_half, rank_side], projected, grad, low_t, up_weight
    )
    bk, rank_plain, rank_near = lax.optimization_barrier((bk, rank_plain, rank_near))
    squares = sds((n, half, 2 * half), BF)
    cross, near, pb, ds, factor, dot = call(
        far_scores,
        [sds((2 * RANK, count), F32), sds((half, half_width), BF), squares, squares, line, line],
        frozen_kv, low_kv, up_weight, q, g, e, dp, top, total, bk, bv,
    )
    cross = lax.ppermute(cross, "seq", backward)
    up_far, rank_far = call(
        far_rest, [up_half, rank_side],
        projected, low_kv, low_t, up_weight, q, g, e, dp, bk, bv, near, pb, ds, factor, dot,
    )
    columns = (width + tokens.shape[2]) // 8
    piece = sds((4, 24, columns), F32)
    keep, send = call(down_kernel, [piece, sds(piece.shape, BF)], tokens, rank_plain, rank_near, rank_far, cross, up_plain, up_near, up_far)
    mine, other = total_sum(keep, send, seqs, dps)
    outs = [sds((3, RANK, tokens.shape[2]), F32), sds((3, RANK, width), F32)]
    return tuple(call(last_spread, outs, *other, *call(first_spread, outs, *mine)))


def solution(mesh):
    return jax.shard_map(
        on_device,
        mesh=mesh,
        in_specs=(P("dp", "seq", None), P(None, "dp", "seq", None), P("dp", "seq", None), P(), P()),
        out_specs=(P(), P()),
        check_vma=False,
    )
```
